32 devices in a mesh: fsdp: 8 (over z, y), seq: 4 (over x, core).
Axes of the slice: x: 2, y: 2, z: 4, core: 2. Of those that a mesh axis runs over, the one named last changes fastest.
Arguments:
- inputs: bfloat16 [2, 16, 320, 1024], P(None, 'fsdp', 'seq'), may hold values from -6 to 6
- keep_mask: int32 [2, 16, 320], P(None, 'fsdp'), may hold values from 0 to 1, as said below
- cotangent: bfloat16 [2, 16, 320, 1024], P(None, 'fsdp', 'seq'), may hold values from -6 to 6
- first_gain: bfloat16 [1024], P(('fsdp', 'seq')), may hold values from 0.099609375 to 1.8984375
- first_shift: bfloat16 [1024], P(('fsdp', 'seq')), may hold values from -3 to 3
- qkv_weight: bfloat16 [1024, 3072], P(('fsdp', 'seq')), may hold values from -0.1875 to 0.1875
- query_bias: bfloat16 [1024], P(('fsdp', 'seq')), may hold values from -3 to 3
- value_bias: bfloat16 [1024], P(('fsdp', 'seq')), may hold values from -3 to 3
- out_weight: bfloat16 [1024, 1024], P(('fsdp', 'seq')), may hold values from -0.75 to 0.75
- out_bias: bfloat16 [1024], P(('fsdp', 'seq')), may hold values from -3 to 3
- second_gain: bfloat16 [1024], P(('fsdp', 'seq')), may hold values from 0.099609375 to 1.8984375
- second_shift: bfloat16 [1024], P(('fsdp', 'seq')), may hold values from -3 to 3
- up_weight: bfloat16 [1024, 4096], P(('fsdp', 'seq')), may hold values from -0.1875 to 0.1875
- up_bias: bfloat16 [4096], P(('fsdp', 'seq')), may hold values from -3 to 3
- down_weight: bfloat16 [4096, 1024], P(('fsdp', 'seq')), may hold values from -0.09375 to 0.09375
- down_bias: bfloat16 [1024], P(('fsdp', 'seq')), may hold values from -3 to 3
Outputs:
- layer_out: bfloat16 [2, 16, 320, 1024], P(None, 'fsdp', 'seq')
- input_grad: bfloat16 [2, 16, 320, 1024], P(None, 'fsdp', 'seq')
- first_gain_grad: float32 [1024], P(('fsdp', 'seq'))
- first_shift_grad: float32 [1024], P(('fsdp', 'seq'))
- qkv_weight_grad: float32 [1024, 3072], P(('fsdp', 'seq'))
- query_bias_grad: float32 [1024], P(('fsdp', 'seq'))
- value_bias_grad: float32 [1024], P(('fsdp', 'seq'))
- out_weight_grad: float32 [1024, 1024], P(('fsdp', 'seq'))
- out_bias_grad: float32 [1024], P(('fsdp', 'seq'))
- second_gain_grad: float32 [1024], P(('fsdp', 'seq'))
- second_shift_grad: float32 [1024], P(('fsdp', 'seq'))
- up_weight_grad: float32 [1024, 4096], P(('fsdp', 'seq'))
- up_bias_grad: float32 [4096], P(('fsdp', 'seq'))
- down_weight_grad: float32 [4096, 1024], P(('fsdp', 'seq'))
- down_bias_grad: float32 [1024], P(('fsdp', 'seq'))
The draws below stay inside these ranges and needn't reach their ends.
Inputs may be any that keep to these rules, and one draw needn't show every extreme that they name: `keep_mask`: in each image, k of its 320 keys are 0, k between 32 and 128, at random places.
All inputs are finite; a program needn't handle non-finite values.
Results may differ from the reference program's by a relative error of at most 0.015.
Values may be sent and summed in bfloat16 or wider, within the bound.
No kernel may reach another device: no remote copies, remote signals or barrier semaphores. Data moves between devices by JAX's collectives and lax.ppermute only.
A program may use at most 256 MiB of HBM per device.

```python
import math
import jax
import jax.numpy as jnp
from jax import lax

D = 1024
FF = 4096
HEADS = 16
HEAD_DIM = 64
MICRO = 2
SEQ_LEN = 320
IMAGES = 16


def draw_keep_mask(key, part):
    key = jax.random.fold_in(key, 7)
    count_key, place_key = jax.random.split(key)
    masked_count = jax.random.randint(count_key, (MICRO, IMAGES, 1), SEQ_LEN // 10, 2 * SEQ_LEN // 5 + 1)
    places = jnp.broadcast_to(jnp.arange(SEQ_LEN, dtype=jnp.int32), (MICRO, IMAGES, SEQ_LEN))
    ranking = jax.random.permutation(place_key, places, axis=2, independent=True)
    return (ranking >= masked_count).astype(jnp.int32)


def steps_of(rng, dims, cuts, smallest, largest):
    def one(axis_at, blocks):
        heights = jax.random.uniform(jax.random.fold_in(jax.random.fold_in(rng, 6), axis_at), (blocks,), jnp.float32, smallest / len(cuts), largest / len(cuts))
        return jnp.repeat(jnp.exp(heights), dims[axis_at] // blocks).reshape((-1,) + (1,) * (len(dims) - axis_at - 1))

    gain = one(*cuts[0])
    for cut in cuts[1:]:
        gain = gain * one(*cut)
    return gain


def normal_values(rng, extent, deviation, most, pieces=(), kind=jnp.bfloat16):
    values = jax.random.normal(rng, extent, jnp.float32) * deviation
    if len(pieces) > 0:
        values = steps_of(rng, extent, pieces, -0.22, 0.18) * values
    return jnp.clip(values, min=-most, max=most).astype(kind)


def setup_inputs(seed: int = 0) -> dict:
    seeds = jax.random.split(jax.random.key(seed), 17)
    inputs = normal_values(seeds[0], (MICRO, IMAGES, SEQ_LEN, D), 1.0, 6.0, ((1, 8), (2, 4)))
    keep_mask = draw_keep_mask(jax.random.fold_in(seeds[16], 71), 0)
    cotangent = normal_values(seeds[2], (MICRO, IMAGES, SEQ_LEN, D), 1.0, 6.0, ((1, 8), (2, 4)))
    first_gain = jnp.clip(1.0 + 0.18 * jax.random.normal(seeds[3], (D,), jnp.float32), 0.099609375, 1.8984375).astype(jnp.bfloat16)
    first_shift = normal_values(seeds[4], (D,), 0.5, 3.0, ((0, 32),))
    qkv_weight = normal_values(seeds[5], (D, 3 * D), D ** -0.5, 0.1875, ((0, 32),))
    query_bias = normal_values(seeds[6], (D,), 0.5, 3.0, ((0, 32),))
    value_bias = normal_values(seeds[7], (D,), 0.5, 3.0, ((0, 32),))
    out_weight = normal_values(seeds[8], (D, D), HEAD_DIM ** -0.5, 0.75, ((0, 32),))
    out_bias = normal_values(seeds[9], (D,), 0.5, 3.0, ((0, 32),))
    second_gain = jnp.clip(1.0 + 0.18 * jax.random.normal(seeds[10], (D,), jnp.float32), 0.099609375, 1.8984375).astype(jnp.bfloat16)
    second_shift = normal_values(seeds[11], (D,), 0.5, 3.0, ((0, 32),))
    up_weight = normal_values(seeds[12], (D, FF), D ** -0.5, 0.1875, ((0, 32),))
    up_bias = normal_values(seeds[13], (FF,), 0.5, 3.0, ((0, 32),))
    down_weight = normal_values(seeds[14], (FF, D), FF ** -0.5, 0.09375, ((0, 32),))
    down_bias = normal_values(seeds[15], (D,), 0.5, 3.0, ((0, 32),))
    return {"inputs": inputs, "keep_mask": keep_mask, "cotangent": cotangent, "first_gain": first_gain, "first_shift": first_shift, "qkv_weight": qkv_weight, "query_bias": query_bias, "value_bias": value_bias, "out_weight": out_weight, "out_bias": out_bias, "second_gain": second_gain, "second_shift": second_shift, "up_weight": up_weight, "up_bias": up_bias, "down_weight": down_weight, "down_bias": down_bias}


@jax.custom_vjp
def low(v):
    return lax.optimization_barrier(v.astype(jnp.bfloat16)).astype(jnp.float32)

@jax.custom_vjp
def low_back(v):
    return v

def low_keep(v):
    return (low(v), None)

def low_pass(kept, grad):
    return (grad,)

def back_keep(v):
    return (v, None)

def back_low(kept, grad):
    return (low(grad),)
low.defvjp(low_keep, low_pass)
low_back.defvjp(back_keep, back_low)
negative_fill = -1e+30
highest = lax.Precision.HIGHEST

def layer_norm(values, gain_row, shift_row):
    average = lax.optimization_barrier(jnp.mean(values, axis=-1, keepdims=True))
    centred = values - average
    spread = lax.optimization_barrier(jnp.mean(centred * centred, axis=-1, keepdims=True))
    return centred * lax.rsqrt(spread + 1e-06) * gain_row + shift_row

def exact_gelu(values):
    return jax.nn.gelu(values, approximate=False)

def encoder(block_rows, block_keep, params):
    first_gain, first_shift, qkv_weight, query_bias, value_bias, out_weight, out_bias, second_gain, second_shift, up_weight, up_bias, down_weight, down_bias = params
    batch_size = block_rows.shape[0]
    head_shape = (batch_size, SEQ_LEN, HEADS, HEAD_DIM)
    normed_one = low(layer_norm(block_rows, first_gain, first_shift))
    joined = jnp.dot(normed_one, qkv_weight, precision=highest)
    queries = low(low_back(joined[..., :D] + query_bias)).reshape(head_shape)
    key_rows = low(low_back(joined[..., D:2 * D])).reshape(head_shape)
    value_rows = low(low_back(joined[..., 2 * D:] + value_bias)).reshape(head_shape)
    scores = low_back(jnp.einsum('bqhe,bkhe->bhqk', queries, key_rows, precision=highest) * HEAD_DIM ** (-0.5))
    scores = jnp.where(block_keep[:, None, None, :] > 0, scores, negative_fill)
    ceiling = lax.optimization_barrier(jnp.max(scores, axis=-1, keepdims=True))
    exponent = jnp.exp(scores - ceiling)
    attention_weights = exponent / lax.optimization_barrier(jnp.sum(exponent, axis=-1, keepdims=True))
    attended = jnp.einsum('bhqk,bkhe->bqhe', low(attention_weights), value_rows, precision=highest)
    attended = low(low_back(attended)).reshape(batch_size, SEQ_LEN, D)
    middle = block_rows + low_back(jnp.dot(attended, out_weight, precision=highest) + out_bias)
    normed_two = low(layer_norm(middle, second_gain, second_shift))
    hidden = low_back(jnp.dot(normed_two, up_weight, precision=highest) + up_bias)
    active = low(exact_gelu(hidden))
    return middle + low_back(jnp.dot(active, down_weight, precision=highest) + down_bias)

def reference(inputs, keep_mask, cotangent, first_gain, first_shift, qkv_weight, query_bias, value_bias, out_weight, out_bias, second_gain, second_shift, up_weight, up_bias, down_weight, down_bias):
    params = tuple((weight.astype(jnp.float32) for weight in (first_gain, first_shift, qkv_weight, query_bias, value_bias, out_weight, out_bias, second_gain, second_shift, up_weight, up_bias, down_weight, down_bias)))
    total_images = MICRO * IMAGES
    group_size = math.gcd(total_images, 8)
    block_count = total_images // group_size
    block_shape = (block_count, group_size, SEQ_LEN, D)
    flat_inputs = inputs.astype(jnp.float32).reshape(block_shape)
    flat_cot = cotangent.astype(jnp.float32).reshape(block_shape)
    keep_blocks = keep_mask.reshape(block_count, group_size, SEQ_LEN)

    def whole(source, weights):

        def one_step(carried, block_pair):
            return (carried, jax.checkpoint(encoder)(block_pair[0], block_pair[1], weights))
        _, results = lax.scan(one_step, jnp.zeros((), jnp.float32), (source, keep_blocks))
        return results
    results, pull_back = jax.vjp(whole, flat_inputs, params)
    input_grad, grads = pull_back(flat_cot)
    full_shape = (MICRO, IMAGES, SEQ_LEN, D)
    return (results.reshape(full_shape).astype(jnp.bfloat16), input_grad.reshape(full_shape).astype(jnp.bfloat16), grads[0], grads[1], grads[2], grads[3], grads[4], grads[5], grads[6], grads[7], grads[8], grads[9], grads[10], grads[11], grads[12])
```

```python
import functools

import jax
import jax.numpy as jnp
from jax import lax
from jax.experimental import pallas as pl
from jax.experimental.pallas import tpu as pltpu
from jax.sharding import PartitionSpec as P

HEADS = 16
HEAD_DIM = 64
SEQ = 4
BF = jnp.bfloat16
F32 = jnp.float32
FILL = -1e30
BOTH = ("fsdp", "seq")


def hop(array, mask):
    return lax.ppermute(array, "seq", [(i, i ^ mask) for i in range(SEQ)])


def by_xor(pieces, place):
    low, high = (place & 1) == 1, (place & 2) == 2
    a, b, c, d = pieces
    a, b, c, d = (
        jnp.where(low, b, a),
        jnp.where(low, a, b),
        jnp.where(low, d, c),
        jnp.where(low, c, d),
    )
    return [
        jnp.where(high, c, a),
        jnp.where(high, d, b),
        jnp.where(high, a, c),
        jnp.where(high, b, d),
    ]


def seq_gather(array):
    far = hop(array, 2)
    return [array, hop(array, 1), far, hop(far, 1)]


def seq_exchange(pieces):
    return [pieces[0]] + [hop(pieces[d], d) for d in (1, 2, 3)]


def seq_scatter(pieces):
    far = pieces[2].astype(F32) + hop(pieces[3], 1).astype(F32)
    arrived = hop(far.astype(pieces[0].dtype), 2)
    near = pieces[0].astype(F32) + hop(pieces[1], 1).astype(F32)
    return near + arrived.astype(F32)


def digits_of(size):
    digits, stride = [], 1
    while stride < size:
        radix = 2 if stride == 1 or size // stride < 4 else 4
        digits.append((stride, radix))
        stride *= radix
    return digits


def shift(array, size, stride, radix, step):
    pairs = []
    for i in range(size):
        digit = i // stride % radix
        pairs.append((i, i + ((digit + step) % radix - digit) * stride))
    return lax.ppermute(array, "fsdp", pairs)


def fsdp_gather(array, size, place):
    pieces = [(array, place)]
    for stride, radix in reversed(digits_of(size)):
        digit = place // stride % radix
        more = []
        for step in range(1, radix):
            change = ((digit + radix - step) % radix - digit) * stride
            for piece, owner in pieces:
                more.append((shift(piece, size, stride, radix, step), owner + change))
        pieces = pieces + more
    out = jnp.zeros((size,) + array.shape, array.dtype)
    for piece, owner in pieces:
        out = lax.dynamic_update_index_in_dim(out, piece, owner, 0)
    return out


def fsdp_scatter(array, size, place):
    kind = array.dtype
    rest = array.shape[1:]
    acc = array
    for stride, radix in digits_of(size):
        digit = place // stride % radix
        outer = acc.shape[0] // radix
        blocks = acc.reshape((outer, radix) + rest)
        mine = lax.dynamic_index_in_dim(blocks, digit, 1, keepdims=False).astype(F32)
        for step in range(1, radix):
            away = lax.dynamic_index_in_dim(
                blocks, (digit + step) % radix, 1, keepdims=False
            ).astype(kind)
            mine = mine + shift(away, size, stride, radix, step).astype(F32)
        acc = mine.astype(kind) if outer > 1 else mine
    return acc.reshape(rest)


def rows_dot(left, right):
    return lax.dot_general(left, right, (((0,), (0,)), ((), ())), preferred_element_type=F32)


def cols_dot(left, right):
    return lax.dot_general(left, right, (((1,), (1,)), ((), ())), preferred_element_type=F32)


def plain_dot(left, right):
    return jnp.dot(left, right, preferred_element_type=F32)


def norm_parts(values):
    average = jnp.mean(values, axis=-1, keepdims=True)
    centred = values - average
    scale = lax.rsqrt(jnp.mean(centred * centred, axis=-1, keepdims=True) + 1e-06)
    return centred * scale, scale


def norm_back(grad, hat, scale, gain):
    spread = grad * gain
    return scale * (
        spread
        - jnp.mean(spread, axis=-1, keepdims=True)
        - hat * jnp.mean(spread * hat, axis=-1, keepdims=True)
    )


def attention_kernel(joined_ref, keep_ref, out0, out1, out2, out3, probs_ref):
    tokens = joined_ref.shape[2]
    rows = SEQ * tokens
    width = joined_ref.shape[3] // 3
    joined = joined_ref[...].reshape(rows, 3 * width)
    keep = keep_ref[0] > 0
    outs = []
    for head in range(width // HEAD_DIM):
        low = head * HEAD_DIM
        q = joined[:, low : low + HEAD_DIM]
        k = joined[:, width + low : width + low + HEAD_DIM]
        v = joined[:, 2 * width + low : 2 * width + low + HEAD_DIM]
        scores = cols_dot(k, q) * HEAD_DIM ** (-0.5)
        scores = jnp.where(keep, scores, FILL)
        top = jnp.max(scores, axis=0, keepdims=True)
        mass = jnp.exp(scores - top)
        probs = (mass / jnp.sum(mass, axis=0, keepdims=True)).astype(BF)
        probs_ref[0, head] = probs
        outs.append(rows_dot(v, probs))
    attended = jnp.concatenate(outs, axis=0).T.astype(BF).reshape(SEQ, tokens, width)
    for at, ref in enumerate((out0, out1, out2, out3)):
        ref[0] = attended[at]


def attention(joined, keep):
    _, images, tokens, triple = joined.shape
    width = triple // 3
    rows = SEQ * tokens
    heads = width // HEAD_DIM
    return pl.pallas_call(
        attention_kernel,
        grid=(images,),
        in_specs=[
            pl.BlockSpec((SEQ, 1, tokens, triple), lambda i: (0, i, 0, 0)),
            pl.BlockSpec((1, rows, 1), lambda i: (i, 0, 0)),
        ],
        out_specs=[pl.BlockSpec((1, tokens, width), lambda i: (i, 0, 0))] * SEQ
        + [pl.BlockSpec((1, heads, rows, rows), lambda i: (i, 0, 0, 0))],
        out_shape=[jax.ShapeDtypeStruct((images, tokens, width), BF)] * SEQ
        + [jax.ShapeDtypeStruct((images, heads, rows, rows), BF)],
        compiler_params=pltpu.CompilerParams(vmem_limit_bytes=40 * 2**20),
    )(joined, keep)


def attention_back_kernel(joined_ref, probs_ref, ga0, ga1, ga2, ga3, out_ref):
    tokens = joined_ref.shape[2]
    rows = SEQ * tokens
    width = joined_ref.shape[3] // 3
    joined = joined_ref[...].reshape(rows, 3 * width)
    grad = jnp.concatenate([ga0[0], ga1[0], ga2[0], ga3[0]], axis=0)
    scale = HEAD_DIM ** (-0.5)
    queries, keys, values = [], [], []
    for head in range(width // HEAD_DIM):
        low = head * HEAD_DIM
        q = joined[:, low : low + HEAD_DIM]
        k = joined[:, width + low : width + low + HEAD_DIM]
        v = joined[:, 2 * width + low : 2 * width + low + HEAD_DIM]
        ga = grad[:, low : low + HEAD_DIM]
        probs = probs_ref[0, head]
        values.append(plain_dot(probs, ga))
        wide = probs.astype(F32)
        grad_probs = cols_dot(v, ga)
        centre = jnp.sum(wide * grad_probs, axis=0, keepdims=True)
        grad_scores = (wide * (grad_probs - centre)).astype(BF)
        keys.append(plain_dot(grad_scores, q) * scale)
        queries.append(rows_dot(k, grad_scores) * scale)
    out_ref[...] = jnp.concatenate(
        [jnp.concatenate(queries, axis=0).T.astype(BF)]
        + [x.astype(BF) for x in keys]
        + [x.astype(BF) for x in values],
        axis=1,
    ).reshape(SEQ, 1, tokens, 3 * width)


def attention_back(joined, probs, grads):
    _, images, tokens, triple = joined.shape
    width = triple // 3
    rows = SEQ * tokens
    heads = width // HEAD_DIM
    return pl.pallas_call(
        attention_back_kernel,
        grid=(images,),
        in_specs=[
            pl.BlockSpec((SEQ, 1, tokens, triple), lambda i: (0, i, 0, 0)),
            pl.BlockSpec((1, heads, rows, rows), lambda i: (i, 0, 0, 0)),
        ]
        + [pl.BlockSpec((1, tokens, width), lambda i: (i, 0, 0))] * SEQ,
        out_specs=pl.BlockSpec((SEQ, 1, tokens, triple), lambda i: (0, i, 0, 0)),
        out_shape=jax.ShapeDtypeStruct(joined.shape, BF),
        compiler_params=pltpu.CompilerParams(vmem_limit_bytes=40 * 2**20),
    )(joined, probs, *grads)


def on_device(
    fsdp,
    inputs,
    keep_mask,
    cotangent,
    first_gain,
    first_shift,
    qkv_weight,
    query_bias,
    value_bias,
    out_weight,
    out_bias,
    second_gain,
    second_shift,
    up_weight,
    up_bias,
    down_weight,
    down_bias,
):
    micros, images, tokens, model = inputs.shape
    rows = images * tokens
    at_f, at_s = lax.axis_index("fsdp"), lax.axis_index("seq")
    depth = qkv_weight.shape[0]
    block = SEQ * depth
    width = model // SEQ
    hidden_block = up_bias.shape[0]
    hidden_part = fsdp * hidden_block
    micro_range = range(micros)

    x_pieces = [seq_gather(inputs[m].reshape(rows, model)) for m in micro_range]

    vectors = jnp.stack(
        [
            first_gain,
            first_shift,
            query_bias,
            value_bias,
            out_bias,
            second_gain,
            second_shift,
            down_bias,
        ]
    )
    count = vectors.shape[0]
    seq_vectors = jnp.stack(by_xor(seq_exchange([vectors] * SEQ), at_s))
    flat = jnp.concatenate([seq_vectors.reshape(-1), up_bias])
    padded = -(-flat.shape[0] // 128) * 128
    small = jnp.pad(flat, (0, padded - flat.shape[0])).reshape(-1, 128)
    small = fsdp_gather(small, fsdp, at_f).reshape(fsdp, padded)
    up_bias_part = small[:, block * count : block * count + hidden_block].reshape(hidden_part)
    full = small[:, : block * count].reshape(fsdp, SEQ, count, depth)
    full = full.transpose(2, 0, 1, 3).reshape(count, model).astype(F32)
    g1, b1, q_bias, v_bias, o_bias, g2, b2, d_bias = [full[i] for i in range(count)]
    q_part = lax.dynamic_slice_in_dim(q_bias, at_s * width, width)
    v_part = lax.dynamic_slice_in_dim(v_bias, at_s * width, width)
    joined_bias = jnp.concatenate([q_part, jnp.zeros_like(q_part), v_part])

    def columns_gather(weight, order):
        parts = [order(weight, s) for s in range(SEQ)]
        arrived = by_xor(seq_exchange(by_xor(parts, at_s)), at_s)
        return fsdp_gather(jnp.concatenate(arrived, axis=0), fsdp, at_f)

    def qkv_order(weight, s):
        return weight.reshape(depth, 3, SEQ, width)[:, :, s].reshape(depth, 3 * width)

    def up_order(weight, s):
        return weight.reshape(depth, fsdp, SEQ, hidden_block)[:, :, s].reshape(depth, hidden_part)

    w_qkv = columns_gather(qkv_weight, qkv_order).reshape(model, 3 * width)
    half = model // 2
    halves = [out_weight[:, :half], out_weight[:, half:]]
    core = at_s & 1
    own_half = jnp.where(core == 1, halves[1], halves[0])
    other_half = jnp.where(core == 1, halves[0], halves[1])
    came = hop(other_half, 1)
    two = jnp.stack([jnp.where(core == 1, came, own_half), jnp.where(core == 1, own_half, came)])
    two_far = hop(two, 2)
    high = at_s >= 2
    four = jnp.concatenate(
        [jnp.where(high, two_far, two), jnp.where(high, two, two_far)], axis=0
    ).reshape(block, half)
    w_out_half = fsdp_gather(four, fsdp, at_f).reshape(model, half)
    w_out_other = hop(w_out_half, 1)
    w_out = jnp.concatenate(
        [
            jnp.where(core == 1, w_out_other, w_out_half),
            jnp.where(core == 1, w_out_half, w_out_other),
        ],
        axis=1,
    )
    w_up = columns_gather(up_weight, up_order).reshape(model, hidden_part)
    w_down = fsdp_gather(down_weight, fsdp, at_f).reshape(hidden_part, model)

    c_pieces = [seq_gather(cotangent[m].reshape(rows, model)) for m in micro_range]

    kept = []
    outputs = []
    for m in micro_range:
        hats = [norm_parts(p.astype(F32)) for p in x_pieces[m]]
        normed_one = jnp.concatenate([(hat * g1 + b1).astype(BF) for hat, _ in hats], axis=0)
        joined = (plain_dot(normed_one, w_qkv) + joined_bias).astype(BF)
        joined = joined.reshape(SEQ, images, tokens, 3 * width)
        keep = keep_mask[m].reshape(images, SEQ, tokens)
        keep = jnp.stack(by_xor([keep[:, s] for s in range(SEQ)], at_s), axis=1)
        *heads_out, probs = attention(joined, keep.reshape(images, SEQ * tokens, 1))
        arrived = seq_exchange([h.reshape(rows, width) for h in heads_out])
        attended = jnp.concatenate(by_xor(arrived, at_s), axis=1)
        middle = x_pieces[m][0].astype(F32) + plain_dot(attended, w_out) + o_bias
        hat_two, scale_two = norm_parts(middle)
        two_pieces = seq_gather((hat_two * g2 + b2).astype(BF))
        normed_two = jnp.concatenate(two_pieces, axis=0)
        hidden = plain_dot(normed_two, w_up) + up_bias_part.astype(F32)
        active = jax.nn.gelu(hidden, approximate=False).astype(BF)
        partial = plain_dot(active, w_down).astype(BF).reshape(SEQ, rows, model)
        result = middle + seq_scatter([partial[d] for d in range(SEQ)]) + d_bias
        outputs.append(result.astype(BF).reshape(images, tokens, model))
        kept.append(
            (hats[0], normed_one, joined, probs, attended, hat_two, scale_two, normed_two, hidden, active)
        )

    stages = []
    inputs_back = []
    small_sums = []
    for m in micro_range:
        hat_one, normed_one, joined, probs, attended, hat_two, scale_two, normed_two, hidden, active = kept[m]
        cot = jnp.concatenate(c_pieces[m], axis=0)
        cot_own = c_pieces[m][0].astype(F32)
        _, pull = jax.vjp(lambda v: jax.nn.gelu(v, approximate=False), hidden)
        grad_hidden = pull(cols_dot(cot, w_down))[0].astype(BF)
        partial = cols_dot(grad_hidden, w_up).astype(BF).reshape(SEQ, rows, model)
        grad_two = seq_scatter([partial[d] for d in range(SEQ)])
        grad_middle = cot_own + norm_back(grad_two, hat_two, scale_two, g2)
        grad_branch = grad_middle.astype(BF)
        grad_attended = cols_dot(grad_branch, w_out).astype(BF)
        parts = [grad_attended[:, s * width : (s + 1) * width] for s in range(SEQ)]
        arrived = seq_exchange(by_xor(parts, at_s))
        grad_joined = attention_back(
            joined, probs, [a.reshape(images, tokens, width) for a in arrived]
        ).reshape(SEQ * rows, 3 * width)
        partial = cols_dot(grad_joined, w_qkv).astype(BF).reshape(SEQ, rows, model)
        grad_one = seq_scatter([partial[d] for d in range(SEQ)])
        grad_input = grad_middle + norm_back(grad_one, hat_one[0], hat_one[1], g1)
        inputs_back.append(grad_input.astype(BF).reshape(images, tokens, model))
        stages.append((normed_one, grad_joined, attended, grad_branch, normed_two, grad_hidden, active, cot))
        sums = lambda v: jnp.sum(v.astype(F32), axis=0)
        small_sums.append(
            (
                sums(grad_one * hat_one[0]),
                sums(grad_one),
                sums(grad_joined[:, :width]),
                sums(grad_joined[:, 2 * width :]),
                sums(grad_branch),
                sums(grad_two * hat_two),
                sums(grad_two),
                sums(cot_own),
                sums(grad_hidden),
            )
        )

    def joint(at):
        return jnp.concatenate([stages[m][at] for m in micro_range], axis=0)

    down_grad = rows_dot(joint(6), joint(7)).astype(BF)
    down_grad = fsdp_scatter(down_grad.reshape(fsdp, hidden_block, model), fsdp, at_f)

    def columns_scatter(grad, order):
        mine = fsdp_scatter(grad.astype(BF).reshape(fsdp, block, grad.shape[1]), fsdp, at_f)
        parts = [mine[s * depth : (s + 1) * depth].astype(BF) for s in range(SEQ)]
        arrived = by_xor(seq_exchange(by_xor(parts, at_s)), at_s)
        return order(jnp.stack(arrived).astype(F32))

    def up_back(parts):
        return parts.reshape(SEQ, depth, fsdp, hidden_block).transpose(1, 2, 0, 3).reshape(depth, -1)

    def qkv_back(parts):
        return parts.reshape(SEQ, depth, 3, width).transpose(1, 2, 0, 3).reshape(depth, -1)

    up_grad = columns_scatter(rows_dot(joint(4), joint(5)), up_back)

    out_grad = rows_dot(joint(2), joint(3)).astype(BF)
    halves = [out_grad[:, :half], out_grad[:, half:]]
    own_half = jnp.where(core == 1, halves[1], halves[0])
    other_half = jnp.where(core == 1, halves[0], halves[1])
    chip_half = (own_half.astype(F32) + hop(other_half, 1).astype(F32)).astype(BF)
    mine = fsdp_scatter(chip_half.reshape(fsdp, block, half), fsdp, at_f).astype(BF)
    mine = mine.reshape(2, 2 * depth, half)
    own_rows = jnp.where(high, mine[1], mine[0])
    other_rows = jnp.where(high, mine[0], mine[1])
    pair = own_rows.astype(F32) + hop(other_rows, 2).astype(F32)
    pair = pair.astype(BF).reshape(2, depth, half)
    own_rows = jnp.where(core == 1, pair[1], pair[0])
    other_rows = hop(jnp.where(core == 1, pair[0], pair[1]), 1)
    out_weight_grad = jnp.concatenate(
        [
            jnp.where(core == 1, other_rows, own_rows),
            jnp.where(core == 1, own_rows, other_rows),
        ],
        axis=1,
    ).astype(F32)

    qkv_grad = columns_scatter(rows_dot(joint(0), joint(1)), qkv_back)

    totals = [sum(parts) for parts in zip(*small_sums)]

    def spread(part):
        return lax.dynamic_update_slice_in_dim(jnp.zeros((model,), F32), part, at_s * width, 0)

    eight = jnp.stack(
        totals[:2] + [spread(totals[2]), spread(totals[3])] + totals[4:8]
    )
    eight = eight.reshape(count, fsdp, SEQ, depth).transpose(2, 1, 0, 3)
    eight = seq_scatter(by_xor([eight[s] for s in range(SEQ)], at_s))
    both = jnp.concatenate(
        [eight.reshape(fsdp, count * depth), totals[8].reshape(fsdp, hidden_block)], axis=1
    )
    both = fsdp_scatter(both, fsdp, at_f)
    vector_grads = both[: count * depth].reshape(count, depth)
    up_bias_grad = both[count * depth :]

    return (
        jnp.stack(outputs),
        jnp.stack(inputs_back),
        vector_grads[0],
        vector_grads[1],
        qkv_grad,
        vector_grads[2],
        vector_grads[3],
        out_weight_grad,
        vector_grads[4],
        vector_grads[5],
        vector_grads[6],
        up_grad,
        up_bias_grad,
        down_grad,
        vector_grads[7],
    )


def solution(mesh):
    shard = P(BOTH)
    tokens = P(None, "fsdp", "seq", None)
    in_specs = (tokens, P(None, "fsdp", None), tokens) + (shard,) * 13
    out_specs = (tokens, tokens) + (shard,) * 13
    return jax.shard_map(
        functools.partial(on_device, mesh.shape["fsdp"]),
        mesh=mesh,
        in_specs=in_specs,
        out_specs=out_specs,
        check_vma=False,
    )
```

```python
import functools

import jax
import jax.numpy as jnp
from jax import lax
from jax.experimental import pallas as pl
from jax.experimental.pallas import tpu as pltpu
from jax.sharding import PartitionSpec as P

HEAD_DIM = 64
SEQ = 4
BF = jnp.bfloat16
F32 = jnp.float32
FILL = -1e30
LANES = 128
VECTORS = 8
SCALE = HEAD_DIM ** (-0.5)
BOTH = ("fsdp", "seq")
ORDER = (0, 2, 1, 3)
ANY = pl.BlockSpec(memory_space=pl.ANY)
SMEM = pl.BlockSpec(memory_space=pltpu.SMEM)
VMEM = pl.BlockSpec(memory_space=pltpu.VMEM)


def hop(array, mask):
    return lax.ppermute(array, "seq", [(i, i ^ mask) for i in range(SEQ)])


def seq_gather(array):
    far = hop(array, 2)
    return [array, far, hop(array, 1), hop(far, 1)]


def seq_exchange(pieces):
    return [pieces[0]] + [hop(pieces[k], ORDER[k]) for k in (1, 2, 3)]


def seq_scatter(chip, sibling):
    came = hop(sibling, 1)
    return came, (chip[1].astype(F32) + came[1].astype(F32)).astype(BF)


def digits_of(size):
    digits, stride = [], 1
    while stride < size:
        radix = 2 if stride == 1 or size // stride < 4 else 4
        digits.append((stride, radix))
        stride *= radix
    return digits


def shift(array, size, stride, radix, step):
    pairs = []
    for i in range(size):
        digit = i // stride % radix
        pairs.append((i, i + ((digit + step) % radix - digit) * stride))
    return lax.ppermute(array, "fsdp", pairs)


def steps_of(radix):
    return [step for _, step in sorted((min(s, radix - s), s) for s in range(1, radix))]


def fsdp_owners(size, place):
    owners = [place]
    for stride, radix in reversed(digits_of(size)):
        digit = place // stride % radix
        changes = [((digit + radix - step) % radix - digit) * stride for step in steps_of(radix)]
        owners = owners + [o + change for change in changes for o in owners]
    return owners


def after(array, *done):
    return lax.optimization_barrier((array,) + done)[0] if done else array


def fsdp_gather(array, size):
    pieces = [array]
    for stride, radix in reversed(digits_of(size)):
        pieces = pieces + [
            shift(piece, size, stride, radix, step) for step in steps_of(radix) for piece in pieces
        ]
    return pieces


class Gather:
    def __init__(self, array, size):
        self.array, self.size = array, size
        self.near, self.far = digits_of(size)
        self.steps = steps_of(self.far[1])
        self.came, self.passed = {}, {}

    def send(self, at, *done):
        self.came[at] = shift(after(self.array, *done), self.size, *self.far, self.steps[at])
        return self.came[at]

    def forward(self, at, *done):
        source = self.array if at is None else self.came[at]
        self.passed[at] = shift(after(source, *done), self.size, *self.near, 1)
        return self.passed[at]

    def pieces(self):
        order = range(len(self.steps))
        return (
            [self.array]
            + [self.came[at] for at in order]
            + [self.passed[None]]
            + [self.passed[at] for at in order]
        )


def split_kernel(count, radix, digit_ref, *refs):
    parts, outs = refs[:count], refs[count:]
    digit = digit_ref[0]
    for step, out in zip([0] + steps_of(radix), outs):
        at = lax.rem(digit + step, radix)
        out[0] = functools.reduce(jnp.add, [part[0, at].astype(F32) for part in parts]).astype(out.dtype)


def split_sum(parts, outer, radix, digit):
    rows, cols = parts[0].shape[1:]
    return pl.pallas_call(
        functools.partial(split_kernel, len(parts), radix),
        grid=(outer,),
        in_specs=[SMEM]
        + [pl.BlockSpec((1, radix, rows, cols), lambda i: (i, 0, 0, 0))] * len(parts),
        out_specs=[pl.BlockSpec((1, rows, cols), lambda i: (i, 0, 0))] * radix,
        out_shape=[jax.ShapeDtypeStruct((outer, rows, cols), BF)] * radix,
        compiler_params=params(),
        name="split",
    )(digit, *[part.reshape(outer, radix, rows, cols) for part in parts])


def scatter_near(keep, send, size, place):
    digits = digits_of(size)
    parts = [keep, shift(send, size, *digits[0], 1)]
    stride, radix = digits[1]
    digit = place // stride % radix
    outer = keep.shape[0] // radix
    return split_sum(parts, outer, radix, jnp.asarray(digit, jnp.int32).reshape(1))


def scatter_far(blocks, size, place):
    digits = digits_of(size)
    for at, (stride, radix) in enumerate(digits[1:]):
        parts = list(blocks[:1]) + [
            shift(block, size, stride, radix, step) for block, step in zip(blocks[1:], steps_of(radix))
        ]
        if at + 2 < len(digits):
            stride, radix = digits[at + 2]
            digit = place // stride % radix
            outer = parts[0].shape[0] // radix
            blocks = split_sum(parts, outer, radix, jnp.asarray(digit, jnp.int32).reshape(1))
    return functools.reduce(jnp.add, [part[0].astype(F32) for part in parts])


def rows_dot(left, right):
    return lax.dot_general(left, right, (((0,), (0,)), ((), ())), preferred_element_type=F32)


def cols_dot(left, right):
    return lax.dot_general(left, right, (((1,), (1,)), ((), ())), preferred_element_type=F32)


def plain_dot(left, right):
    return jnp.dot(left, right, preferred_element_type=F32)


def norm_parts(values):
    average = jnp.mean(values, axis=-1, keepdims=True)
    centred = values - average
    scale = lax.rsqrt(jnp.mean(centred * centred, axis=-1, keepdims=True) + 1e-06)
    return centred * scale, scale


def norm_back(grad, hat, scale, gain):
    spread = grad * gain
    return scale * (
        spread
        - jnp.mean(spread, axis=-1, keepdims=True)
        - hat * jnp.mean(spread * hat, axis=-1, keepdims=True)
    )


def column_sums(values):
    return jnp.sum(values, axis=0, keepdims=True)


def params():
    return pltpu.CompilerParams(vmem_limit_bytes=60 * 2**20)


def estimate(flops, moved):
    return pl.CostEstimate(flops=int(flops), bytes_accessed=int(moved), transcendentals=0)


def pack_kernel(fsdp, qkv, out, vectors, up, ref):
    width = qkv.shape[1] // 3 // SEQ
    half = out.shape[1] // 2
    block = up.shape[1] // SEQ // fsdp
    for s in range(SEQ):
        spans = [(qkv, (part * SEQ + s) * width, width) for part in range(3)]
        spans += [(vectors, 0, LANES), (out, (s % 2) * half, half)]
        spans += [(up, (f * SEQ + s) * block, block) for f in range(fsdp)]
        low = 0
        for source, start, cols in spans:
            ref[s, :, low : low + cols] = source[:, start : start + cols]
            low += cols


def pack(fsdp, qkv, out, vectors, up):
    depth = qkv.shape[0]
    cols = (qkv.shape[1] + up.shape[1]) // SEQ + LANES + out.shape[1] // 2
    return pl.pallas_call(
        functools.partial(pack_kernel, fsdp),
        in_specs=[VMEM] * 4,
        out_specs=VMEM,
        out_shape=jax.ShapeDtypeStruct((SEQ, depth, cols), BF),
        compiler_params=params(),
        name="pack",
    )(qkv, out, vectors, up)


def unpack_kernel(ref, qkv, out, up, vectors):
    width = qkv.shape[1] // 3 // SEQ
    half = out.shape[1] // 2
    units = up.shape[1] // SEQ
    low = 3 * width + LANES
    block = ref.shape[1] * SEQ
    for s in range(SEQ):
        for part in range(3):
            at = (part * SEQ + s) * width
            qkv[:, at : at + width] = ref[s, :, part * width : (part + 1) * width].astype(F32)
        for part in range(units // block):
            at = (part * SEQ + s) * block
            start = low + half + part * block
            up[:, at : at + block] = ref[s, :, start : start + block].astype(F32)
    wide = lambda s, start, cols: ref[s, :, start : start + cols].astype(F32)
    vectors[...] = functools.reduce(jnp.add, [wide(s, 3 * width, LANES) for s in range(SEQ)])
    for core in range(2):
        out[:, core * half : (core + 1) * half] = wide(core, low, half) + wide(core + 2, low, half)


def unpack(came, model, units):
    depth = came.shape[1]
    cols = (3 * model, model, SEQ * units, LANES)
    return pl.pallas_call(
        unpack_kernel,
        in_specs=[VMEM],
        out_specs=[VMEM] * 4,
        out_shape=[jax.ShapeDtypeStruct((depth, n), F32) for n in cols],
        compiler_params=params(),
        name="unpack",
    )(came)


def place_kernel(count, spans, vectors, info, *refs):
    pieces, outs = refs[:count], refs[count : count + len(spans)]
    block = pieces[0].shape[0]
    for at, piece in enumerate(pieces):
        place = pl.ds(pl.multiple_of(info[at] * block, block), block)
        for (low, cols), out in zip(spans, outs):
            out[place, :] = piece[:, low : low + cols]
    if vectors:
        rows = refs[-1]
        rows[...] = outs[-1][...].astype(F32).T[: rows.shape[0]]


def placed(info, pieces, *spans, vectors=False):
    count = len(pieces)
    rows = count * pieces[0].shape[0]
    shapes = [jax.ShapeDtypeStruct((rows, cols), BF) for _, cols in spans]
    if vectors:
        shapes.append(jax.ShapeDtypeStruct((16, rows), F32))
    return pl.pallas_call(
        functools.partial(place_kernel, count, spans, vectors),
        in_specs=[SMEM] + [VMEM] * count,
        out_specs=[VMEM] * len(shapes),
        out_shape=shapes,
        compiler_params=params(),
        name="placed",
    )(info, *pieces)


def row_copies(sources, target, sem):
    copies, low = [], 0
    for at, source in enumerate(sources):
        rows = source.shape[0]
        copies.append(pltpu.make_async_copy(source, target.at[pl.ds(low, rows), :], sem.at[at]))
        low += rows
    return copies


def weight_grad_kernel(lefts, rights, left_at, right_at, info, *refs):
    more = len(refs) - lefts - rights - 8
    left_refs, right_refs = refs[:lefts], refs[lefts : lefts + rights]
    extra = refs[lefts + rights : lefts + rights + more]
    keep, send, left, right, out, left_sem, right_sem, out_sem = refs[lefts + rights + more :]
    copies = row_copies(left_at(info, left_refs), left, left_sem) + row_copies(
        right_at(info, right_refs), right, right_sem
    )
    for copy in copies:
        copy.start()
    total, cols = left.shape[1], right.shape[1]
    if more:
        sums = functools.reduce(jnp.add, [ref[...] for ref in extra])
        sums = jnp.concatenate([sums, jnp.zeros((LANES - sums.shape[0], total), F32)], axis=0)
        out[:, cols:] = sums.T.astype(BF)
    for copy in copies:
        copy.wait()
    tile = min(256, total)
    for low in range(0, total, tile):
        out[low : low + tile, :cols] = rows_dot(left[:, low : low + tile], right[...]).astype(BF)
    groups, block = keep.shape[:2]
    low_digit = info[0] % 2
    moves = []
    for at in range(groups):
        for which, (ref, side) in enumerate(((keep, low_digit), (send, 1 - low_digit))):
            start = pl.multiple_of((2 * at + side) * block, block)
            moves.append(
                pltpu.make_async_copy(out.at[pl.ds(start, block), :], ref.at[at], out_sem.at[2 * at + which])
            )
    for move in moves:
        move.start()
    for move in moves:
        move.wait()


def feed_grads_kernel(micros, tokens_at, info, *refs):
    n2 = refs[: micros * SEQ]
    actives, hiddens = refs[micros * SEQ : micros * (SEQ + 1)], refs[micros * (SEQ + 1) : micros * (SEQ + 2)]
    cot, out = refs[micros * (SEQ + 2) : micros * (SEQ + 2) + 2]
    c_in, act_in, n2_in, gh_in, c_sem, act_sem, n2_sem, gh_sem = refs[micros * (SEQ + 2) + 2 :]
    cots = [cot.at[info[tokens_at + k], m] for m in range(micros) for k in range(SEQ)]
    first = row_copies(cots, c_in, c_sem) + row_copies(actives, act_in, act_sem)
    second = row_copies(n2, n2_in, n2_sem) + row_copies(hiddens, gh_in, gh_sem)
    for copy in first + second:
        copy.start()
    block = out.shape[2]
    step = max(256 // block, 1)
    for which, (left, right, copies) in enumerate(((act_in, c_in, first), (n2_in, gh_in, second))):
        for copy in copies:
            copy.wait()
        for low in range(0, out.shape[0], step):
            part = rows_dot(left[:, low * block : (low + step) * block], right[...]).astype(BF)
            out[low : low + step, which] = part.reshape(step, block, part.shape[1])


def feed_grads(info, fsdp, n2, actives, hiddens, c_all):
    micros = len(actives)
    rows, units = actives[0].shape
    model = c_all.shape[3]
    block = model // fsdp
    wide = pltpu.VMEM((micros * rows, model), BF)
    return pl.pallas_call(
        functools.partial(feed_grads_kernel, micros, fsdp + 2),
        in_specs=[SMEM] + [ANY] * (micros * (SEQ + 2) + 1),
        out_specs=VMEM,
        out_shape=jax.ShapeDtypeStruct((fsdp, 2, block, model), BF),
        scratch_shapes=[wide] * 4
        + [pltpu.SemaphoreType.DMA((16,))] * 4,
        compiler_params=params(),
        cost_estimate=estimate(4 * micros * rows * units * model, 16 * 2**20),
        name="feed_grads",
    )(info, *n2, *actives, *hiddens, c_all)


def plain_rows(info, refs):
    return refs


def weight_grad(info, fsdp, lefts, rights, left_at=plain_rows, right_at=plain_rows, sums=(), shape=None):
    rows, total, cols = shape
    wide = cols + (LANES if sums else 0)
    out = jax.ShapeDtypeStruct((fsdp // 2, total // fsdp, wide), BF)
    return pl.pallas_call(
        functools.partial(weight_grad_kernel, len(lefts), len(rights), left_at, right_at),
        in_specs=[SMEM] + [ANY] * (len(lefts) + len(rights)) + [VMEM] * len(sums),
        out_specs=[ANY] * 2,
        out_shape=[out] * 2,
        scratch_shapes=[
            pltpu.VMEM((rows, total), BF),
            pltpu.VMEM((rows, cols), BF),
            pltpu.VMEM((total, wide), BF),
            pltpu.SemaphoreType.DMA((16,)),
            pltpu.SemaphoreType.DMA((16,)),
            pltpu.SemaphoreType.DMA((fsdp,)),
        ],
        compiler_params=params(),
        cost_estimate=estimate(2 * rows * total * cols, 2 * rows * (total + cols) + 2 * total * cols),
        name="weight_grad",
    )(info, *lefts, *rights, *sums)


def core_grad_kernel(count, core_at, info, *refs):
    lefts, rights = refs[:count], refs[count : 2 * count]
    here, there = refs[2 * count :]
    total, half = here.shape
    core = info[core_at]
    for ref, side in ((here, core), (there, 1 - core)):
        cols = pl.ds(pl.multiple_of(side * half, half), half)
        ref[...] = functools.reduce(
            jnp.add, [rows_dot(left[...], right[:, cols]) for left, right in zip(lefts, rights)]
        ).astype(BF)


def core_grad(info, fsdp, lefts, rights):
    model = lefts[0].shape[1]
    half = jax.ShapeDtypeStruct((model, model // 2), BF)
    rows = lefts[0].shape[0] * len(lefts)
    return pl.pallas_call(
        functools.partial(core_grad_kernel, len(lefts), fsdp + 1),
        in_specs=[SMEM] + [VMEM] * (2 * len(lefts)),
        out_specs=[VMEM] * 2,
        out_shape=[half] * 2,
        compiler_params=params(),
        cost_estimate=estimate(2 * rows * model * model, 4 * 2**20),
        name="core_grad",
    )(info, *lefts, *rights)


def core_split_kernel(info, here, came, keep, send):
    groups, block = keep.shape[:2]
    low_digit = info[0] % 2
    for at in range(groups):
        for ref, side in ((keep, low_digit), (send, 1 - low_digit)):
            place = pl.ds(pl.multiple_of((2 * at + side) * block, block), block)
            ref[at] = (here[place].astype(F32) + came[place].astype(F32)).astype(BF)


def core_split(info, fsdp, here, came):
    total, half = here.shape
    out = jax.ShapeDtypeStruct((fsdp // 2, total // fsdp, half), BF)
    return pl.pallas_call(
        core_split_kernel,
        in_specs=[SMEM] + [VMEM] * 2,
        out_specs=[VMEM] * 2,
        out_shape=[out] * 2,
        compiler_params=params(),
        name="core_split",
    )(info, here, came)


def attention_kernel(count, info, x_ref, keep_ref, vec, source, *refs):
    n1_ref, hat_ref, joined_ref, e0, e1, e2, e3, probs_ref, weight, sem = refs
    tokens, model = x_ref.shape[3:]
    rows = SEQ * tokens
    triple = weight.shape[1]
    width = triple // 3
    fetch = pltpu.make_async_copy(source, weight, sem)

    @pl.when(pl.program_id(0) == 0)
    def _():
        fetch.start()

    values = jnp.concatenate(
        [x_ref[info[count + 2 + k], 0, 0].astype(F32) for k in range(SEQ)], axis=0
    )
    hat, _ = norm_parts(values)
    hat_ref[...] = hat.astype(BF).reshape(hat_ref.shape)
    normed = (hat * vec[0:1, :] + vec[1:2, :]).astype(BF)
    n1_ref[...] = normed.reshape(n1_ref.shape)

    @pl.when(pl.program_id(0) == 0)
    def _():
        fetch.wait()

    place = pl.multiple_of(info[count] * width, width)
    bias = jnp.concatenate(
        [
            vec[2:3, pl.ds(place, width)],
            jnp.zeros((1, width), F32),
            vec[3:4, pl.ds(place, width)],
        ],
        axis=1,
    )
    joined = (plain_dot(normed, weight[...]) + bias).astype(BF)
    joined_ref[...] = joined.reshape(joined_ref.shape)
    keep = keep_ref[0] > 0
    outs = []
    for head in range(width // HEAD_DIM):
        low = head * HEAD_DIM
        q = joined[:, low : low + HEAD_DIM] * jnp.asarray(SCALE, BF)
        k = joined[:, width + low : width + low + HEAD_DIM]
        v = joined[:, 2 * width + low : 2 * width + low + HEAD_DIM]
        scores = jnp.where(keep, cols_dot(k, q), FILL)
        mass = jnp.exp(scores - jnp.max(scores, axis=0, keepdims=True))
        probs = (mass * (1.0 / jnp.sum(mass, axis=0, keepdims=True))).astype(BF)
        probs_ref[0, head] = probs
        outs.append(rows_dot(v, probs))
    attended = jnp.concatenate(outs, axis=0).T.astype(BF)
    for at, ref in enumerate((e0, e1, e2, e3)):
        ref[0] = attended[at * tokens : (at + 1) * tokens]


def attention(info, count, micro, x_all, keep, vec, weight):
    images, tokens, model = x_all.shape[2:]
    triple = weight.shape[1]
    width = triple // 3
    rows = SEQ * tokens
    heads = width // HEAD_DIM
    token_block = lambda cols: pl.BlockSpec((1, tokens, cols), lambda i: (i, 0, 0))
    group_block = lambda cols: pl.BlockSpec((SEQ, 1, tokens, cols), lambda i: (0, i, 0, 0))
    group_shape = lambda cols: jax.ShapeDtypeStruct((SEQ, images, tokens, cols), BF)
    return pl.pallas_call(
        functools.partial(attention_kernel, count),
        grid=(images,),
        in_specs=[SMEM]
        + [
            pl.BlockSpec((SEQ, 1, 1, tokens, model), lambda i: (0, micro, i, 0, 0)),
            pl.BlockSpec((1, rows, 1), lambda i: (i, 0, 0)),
            pl.BlockSpec(vec.shape, lambda i: (0, 0)),
            ANY,
        ],
        out_specs=[group_block(model), group_block(model), group_block(triple)]
        + [token_block(width)] * SEQ
        + [pl.BlockSpec((1, heads, rows, rows), lambda i: (i, 0, 0, 0))],
        out_shape=[group_shape(model), group_shape(model), group_shape(triple)]
        + [jax.ShapeDtypeStruct((images, tokens, width), BF)] * SEQ
        + [jax.ShapeDtypeStruct((images, heads, rows, rows), BF)],
        scratch_shapes=[pltpu.VMEM((model, triple), BF), pltpu.SemaphoreType.DMA],
        compiler_params=params(),
        cost_estimate=estimate(
            2 * images * rows * (model * triple + 4 * width * rows), 8 * 2**20
        ),
        name="attention",
    )(info, x_all, keep, vec, weight)


def out_weight_copies(info, count, mine, other, target, sem):
    half = mine.shape[1]
    core = info[count + 1]
    return [
        pltpu.make_async_copy(
            source, target.at[:, pl.ds(pl.multiple_of(side * half, half), half)], sem.at[which]
        )
        for which, (source, side) in enumerate(((mine, core), (other, 1 - core)))
    ]


def middle_kernel(count, info, e0, e1, e2, e3, x_ref, vec, mine, other, att_ref, mid_ref, n2_ref, weight, sem):
    copies = out_weight_copies(info, count, mine, other, weight, sem)
    for copy in copies:
        copy.start()
    width = e0.shape[1]
    for at, ref in enumerate((e0, e1, e2, e3)):
        place = info[count + 2 + at]
        att_ref[:, pl.ds(pl.multiple_of(place * width, width), width)] = ref[...]
    for copy in copies:
        copy.wait()
    middle = x_ref[...].astype(F32) + plain_dot(att_ref[...], weight[...]) + vec[4:5, :]
    mid_ref[...] = middle
    hat, _ = norm_parts(middle)
    n2_ref[...] = (hat * vec[5:6, :] + vec[6:7, :]).astype(BF)


def middle_part(info, count, heads, x_own, vec, mine, other):
    rows, model = x_own.shape
    return pl.pallas_call(
        functools.partial(middle_kernel, count),
        in_specs=[SMEM] + [VMEM] * 6 + [ANY] * 2,
        out_specs=[VMEM] * 3,
        out_shape=[
            jax.ShapeDtypeStruct((rows, model), BF),
            jax.ShapeDtypeStruct((rows, model), F32),
            jax.ShapeDtypeStruct((rows, model), BF),
        ],
        scratch_shapes=[
            pltpu.VMEM((model, model), BF),
            pltpu.SemaphoreType.DMA((2,)),
        ],
        compiler_params=params(),
        cost_estimate=estimate(2 * rows * model * model, 4 * 2**20),
        name="middle",
    )(info, *heads, x_own, vec, mine, other)


def feed_kernel(count, micro, info, *refs):
    n2 = refs[:SEQ]
    cot, vec = refs[SEQ : SEQ + 2]
    up_ref, down_ref = refs[SEQ + 2 : SEQ + 4]
    act_out, gh_out, down_chip, down_sib, up_chip, up_sib, sums = refs[SEQ + 4 : SEQ + 11]
    w_up, w_down, n2_in, c_in, up_sem, down_sem, n2_sem, c_sem = refs[SEQ + 11 :]
    rows = n2[0].shape[0]
    hidden = w_up.shape[1]
    ups = [pltpu.make_async_copy(up_ref, w_up, up_sem)]
    downs = [pltpu.make_async_copy(down_ref, w_down, down_sem)]
    n2_copies = row_copies(n2, n2_in, n2_sem)
    c_copies = row_copies([cot.at[info[count + 2 + k], micro] for k in range(SEQ)], c_in, c_sem)
    for copy in n2_copies + ups + c_copies + downs:
        copy.start()
    for copy in n2_copies + ups:
        copy.wait()
    total = jnp.zeros((1, hidden), F32)
    for half in range(2):
        span = slice(half * 2 * rows, (half + 1) * 2 * rows)
        values = plain_dot(n2_in[span], w_up[...]) + vec[8:9, :]
        normal = 0.5 * (1.0 + lax.erf(values * (2.0**-0.5)))
        slope = normal + values * (jnp.exp(values * values * -0.5) * 0.3989422804014327)
        active = (values * normal).astype(BF)
        act_out[span] = active
        if half == 0:
            for copy in c_copies + downs:
                copy.wait()
        grad_hidden = (slope * cols_dot(c_in[span], w_down[...])).astype(BF)
        gh_out[span] = grad_hidden
        total = total + column_sums(grad_hidden.astype(F32))
        shape = up_chip.shape
        (down_chip, down_sib)[half][...] = plain_dot(active, w_down[...]).astype(BF).reshape(shape)
        (up_chip, up_sib)[half][...] = cols_dot(grad_hidden, w_up[...]).astype(BF).reshape(shape)
    sums[...] = jnp.zeros(sums.shape, F32)
    sums[8:9, :] = total


def feed(info, count, micro, n2_pieces, c_all, vec, w_up, w_down):
    rows, model = n2_pieces[0].shape
    hidden = w_down.shape[0]
    hiddens = jax.ShapeDtypeStruct((SEQ * rows, hidden), BF)
    pair = jax.ShapeDtypeStruct((2, rows, model), BF)
    return pl.pallas_call(
        functools.partial(feed_kernel, count, micro),
        in_specs=[SMEM] + [ANY] * (SEQ + 1) + [VMEM] + [ANY] * 2,
        out_specs=[VMEM] * 7,
        out_shape=[hiddens, hiddens] + [pair] * 4 + [jax.ShapeDtypeStruct((16, model), F32)],
        scratch_shapes=[
            pltpu.VMEM((model, hidden), BF),
            pltpu.VMEM((hidden, model), BF),
            pltpu.VMEM((SEQ * rows, model), BF),
            pltpu.VMEM((SEQ * rows, model), BF),
            pltpu.SemaphoreType.DMA,
            pltpu.SemaphoreType.DMA,
            pltpu.SemaphoreType.DMA((SEQ,)),
            pltpu.SemaphoreType.DMA((SEQ,)),
        ],
        compiler_params=params(),
        cost_estimate=estimate(8 * SEQ * rows * model * hidden, 16 * 2**20),
        name="feed",
    )(info, *n2_pieces, c_all, vec, w_up, w_down)


def middle_back_kernel(count, info, p0, p1, p2, mid_ref, c_ref, vec, mine, other, gm_ref, gb_ref, g0, g1, g2, g3, sums, weight, scratch, sem):
    copies = out_weight_copies(info, count, mine, other, weight, sem)
    for copy in copies:
        copy.start()
    grad_two = p0[0].astype(F32) + p1[0].astype(F32) + p2[...].astype(F32)
    hat, scale = norm_parts(mid_ref[...])
    cot = c_ref[...].astype(F32)
    grad_middle = cot + norm_back(grad_two, hat, scale, vec[5:6, :])
    gm_ref[...] = grad_middle
    branch = grad_middle.astype(BF)
    gb_ref[...] = branch
    sums[...] = jnp.zeros(sums.shape, F32)
    sums[4:5, :] = column_sums(branch.astype(F32))
    sums[5:6, :] = column_sums(grad_two * hat)
    sums[6:7, :] = column_sums(grad_two)
    sums[7:8, :] = column_sums(cot)
    for copy in copies:
        copy.wait()
    scratch[...] = cols_dot(branch, weight[...]).astype(BF)
    width = g0.shape[1]
    for at, ref in enumerate((g0, g1, g2, g3)):
        place = info[count + 2 + at]
        ref[...] = scratch[:, pl.ds(pl.multiple_of(place * width, width), width)]


def middle_back(info, count, parts, middle, c_own, vec, mine, other):
    rows, model = middle.shape
    piece = jax.ShapeDtypeStruct((rows, model // SEQ), BF)
    return pl.pallas_call(
        functools.partial(middle_back_kernel, count),
        in_specs=[SMEM] + [VMEM] * 6 + [ANY] * 2,
        out_specs=[VMEM] * 7,
        out_shape=[
            jax.ShapeDtypeStruct((rows, model), F32),
            jax.ShapeDtypeStruct((rows, model), BF),
        ]
        + [piece] * 4
        + [jax.ShapeDtypeStruct((16, model), F32)],
        scratch_shapes=[
            pltpu.VMEM((model, model), BF),
            pltpu.VMEM((rows, model), BF),
            pltpu.SemaphoreType.DMA((2,)),
        ],
        compiler_params=params(),
        cost_estimate=estimate(2 * rows * model * model, 4 * 2**20),
        name="middle_back",
    )(info, *parts, middle, c_own, vec, mine, other)


def attention_back_kernel(count, info, joined_ref, probs_ref, g0, g1, g2, g3, hat_ref, source, *refs):
    out_ref, chip_ref, sib_ref, sums, weight, sem = refs
    tokens = joined_ref.shape[2]
    rows = SEQ * tokens
    triple = joined_ref.shape[3]
    width = triple // 3
    model = weight.shape[0]
    fetch = pltpu.make_async_copy(source, weight, sem)

    @pl.when(pl.program_id(0) == 0)
    def _():
        fetch.start()
        sums[...] = jnp.zeros(sums.shape, F32)

    joined = joined_ref[...].reshape(rows, triple)
    grad = jnp.concatenate([g0[0], g1[0], g2[0], g3[0]], axis=0)
    queries, keys, values = [], [], []
    for head in range(width // HEAD_DIM):
        low = head * HEAD_DIM
        q = joined[:, low : low + HEAD_DIM] * jnp.asarray(SCALE, BF)
        k = joined[:, width + low : width + low + HEAD_DIM] * jnp.asarray(SCALE, BF)
        v = joined[:, 2 * width + low : 2 * width + low + HEAD_DIM]
        ga = grad[:, low : low + HEAD_DIM]
        probs = probs_ref[0, head]
        values.append(plain_dot(probs, ga).astype(BF))
        wide = probs.astype(F32)
        weighted = wide * cols_dot(v, ga)
        centre = jnp.sum(weighted, axis=0, keepdims=True)
        grad_scores = (weighted - wide * centre).astype(BF)
        keys.append(plain_dot(grad_scores, q).astype(BF))
        queries.append(rows_dot(k, grad_scores))
    grad_joined = jnp.concatenate(
        [jnp.concatenate(queries, axis=0).T.astype(BF)] + keys + values, axis=1
    )
    out_ref[...] = grad_joined.reshape(out_ref.shape)
    wide = grad_joined.astype(F32)
    place = pl.multiple_of(info[count] * width, width)
    sums[2:3, pl.ds(place, width)] += column_sums(wide[:, :width])
    sums[3:4, pl.ds(place, width)] += column_sums(wide[:, 2 * width :])

    @pl.when(pl.program_id(0) == 0)
    def _():
        fetch.wait()

    partial = cols_dot(grad_joined, weight[...])
    hat = hat_ref[...].reshape(rows, model).astype(F32)
    sums[0:1, :] += column_sums(partial * hat)
    sums[1:2, :] += column_sums(partial)
    low = partial.astype(BF)
    half = rows // 2
    chip_ref[...] = low[:half].reshape(chip_ref.shape)
    sib_ref[...] = low[half:].reshape(sib_ref.shape)


def attention_back(info, count, joined, probs, grads, hat, weight):
    _, images, tokens, triple = joined.shape
    model = hat.shape[3]
    width = triple // 3
    rows = SEQ * tokens
    heads = width // HEAD_DIM
    pair = jax.ShapeDtypeStruct((2, images, tokens, model), BF)
    group_block = lambda n, cols: pl.BlockSpec((n, 1, tokens, cols), lambda i: (0, i, 0, 0))
    return pl.pallas_call(
        functools.partial(attention_back_kernel, count),
        grid=(images,),
        in_specs=[
            SMEM,
            group_block(SEQ, triple),
            pl.BlockSpec((1, heads, rows, rows), lambda i: (i, 0, 0, 0)),
        ]
        + [pl.BlockSpec((1, tokens, width), lambda i: (i, 0, 0))] * SEQ
        + [group_block(SEQ, model), ANY],
        out_specs=[
            group_block(SEQ, triple),
            group_block(2, model),
            group_block(2, model),
            pl.BlockSpec((16, model), lambda i: (0, 0)),
        ],
        out_shape=[
            jax.ShapeDtypeStruct(joined.shape, BF),
            pair,
            pair,
            jax.ShapeDtypeStruct((16, model), F32),
        ],
        scratch_shapes=[pltpu.VMEM((model, triple), BF), pltpu.SemaphoreType.DMA],
        compiler_params=params(),
        cost_estimate=estimate(
            2 * images * rows * (model * triple + 8 * width * rows), 8 * 2**20
        ),
        name="attention_back",
    )(info, joined, probs, *grads, hat, weight)


def on_device(
    fsdp,
    inputs,
    keep_mask,
    cotangent,
    first_gain,
    first_shift,
    qkv_weight,
    query_bias,
    value_bias,
    out_weight,
    out_bias,
    second_gain,
    second_shift,
    up_weight,
    up_bias,
    down_weight,
    down_bias,
):
    micros, images, tokens, model = inputs.shape
    rows = images * tokens
    at_f, at_s = lax.axis_index("fsdp"), lax.axis_index("seq")
    depth = qkv_weight.shape[0]
    block = SEQ * depth
    width = model // SEQ
    triple = 3 * width
    half = model // 2
    unit_block = up_bias.shape[0]
    units = fsdp * unit_block
    core = at_s & 1
    micro_range = range(micros)
    info = jnp.stack(
        [jnp.asarray(v, jnp.int32) for v in fsdp_owners(fsdp, at_f)]
        + [at_s, core]
        + [at_s ^ mask for mask in ORDER]
    )

    vectors = jnp.stack(
        [
            first_gain,
            first_shift,
            query_bias,
            value_bias,
            out_bias,
            second_gain,
            second_shift,
            down_bias,
        ],
        axis=1,
    )
    vectors = jnp.pad(vectors, ((0, 0), (0, LANES - VECTORS)))
    to_send = pack(fsdp, qkv_weight, out_weight, vectors, up_weight)
    arrived = lax.all_to_all(to_send, "seq", 0, 0, tiled=True).reshape(block, -1)
    early = triple + LANES
    bias_column = jnp.pad(up_bias[:, None], ((0, 0), (VECTORS, LANES - VECTORS - 1)))
    first_group = jnp.concatenate(
        [arrived[:, :triple], arrived[:, triple:early] + bias_column], axis=1
    )
    second_group = arrived[:, early:]
    x_all = lax.all_gather(inputs, "seq")
    c_all = lax.all_gather(cotangent.reshape(micros, rows, model), "seq")
    ordered = len(digits_of(fsdp)) == 2 and digits_of(fsdp)[1][1] == 4
    if ordered:
        down = Gather(down_weight, fsdp)
        down.send(0), down.send(1), down.forward(None)
        first = Gather(first_group, fsdp)
        first.send(0, down.came[0])
        first.send(1, down.came[1])
        first.send(2, down.passed[None])
        first.forward(None, down.passed[None])
        for at in range(3):
            first.forward(at)
        second = Gather(second_group, fsdp)
        second.send(0, first.came[0], first.came[1])
        second.send(1, first.came[2])
        second.forward(None, first.passed[0])
        down.forward(0, first.passed[1])
        down.forward(1, first.passed[1])
        first_pieces = first.pieces()
    else:
        first_pieces = fsdp_gather(first_group, fsdp)
        second_pieces = fsdp_gather(second_group, fsdp)
        down_pieces = fsdp_gather(down_weight, fsdp)
    x_own = [inputs[m].reshape(rows, model) for m in micro_range]
    c_own = [cotangent[m].reshape(rows, model) for m in micro_range]

    w_qkv, _, vec = placed(info, first_pieces, (0, triple), (triple, LANES), vectors=True)
    n1s, hats, joineds, probs, heads_in = [], [], [], [], []
    for m in micro_range:
        keep = keep_mask[m].reshape(images, SEQ, tokens)
        keep = jnp.stack(
            [lax.dynamic_index_in_dim(keep, at_s ^ mask, 1, keepdims=False) for mask in ORDER], axis=1
        )
        keep = after(keep, *joineds[-1:])
        n1, hat, joined, *heads_out, prob = attention(
            info,
            fsdp,
            m,
            x_all,
            keep.reshape(images, SEQ * tokens, 1),
            vec,
            w_qkv,
        )
        n1s.append(n1)
        hats.append(hat)
        joineds.append(joined)
        probs.append(prob)
        heads_in.append(seq_exchange([h.reshape(rows, width) for h in heads_out]))
        if ordered and m == 0:
            second.send(2, joined)
            second.forward(0, joined)
            second.forward(1, joined)
            down.send(2, joined, second.came[0])
        if ordered and m == micros - 1:
            second.forward(2, joined)
            down.forward(2, joined)
            second_pieces, down_pieces = second.pieces(), down.pieces()

    out_mine, w_up = placed(info, second_pieces, (0, half), (half, units))
    (w_down,) = placed(info, down_pieces, (0, model))
    out_other = hop(out_mine, 1)

    attendeds, middles, n2_pieces = [], [], []
    heads_in[0][0] = after(heads_in[0][0], joineds[-1])
    for m in micro_range:
        attended, middle, normed = middle_part(
            info, fsdp, heads_in[m], x_own[m], vec, out_mine, out_other
        )
        attendeds.append(attended)
        middles.append(middle)
        if m + 1 < micros:
            heads_in[m + 1][0] = after(heads_in[m + 1][0], middle)
        n2_pieces.append(seq_gather(normed))

    actives, grad_hiddens, two_parts, down_parts, sums = [], [], [], [], []
    n2_pieces[0][0] = after(n2_pieces[0][0], middles[-1])
    for m in micro_range:
        active, grad_hidden, down_chip, down_sib, up_chip, up_sib, part = feed(
            info, fsdp, m, n2_pieces[m], c_all, vec, w_up, w_down
        )
        actives.append(active)
        grad_hiddens.append(grad_hidden)
        sums.append(part)
        down_parts.append((down_chip, down_sib))
        came, far = seq_scatter(up_chip, up_sib)
        two_parts.append((up_chip, came, hop(far, 2)))
        if m + 1 < micros:
            n2_pieces[m + 1][0] = after(n2_pieces[m + 1][0], far)
        else:
            actives[0] = after(actives[0], far)

    group_rows = micros * SEQ * rows

    feed_grad = feed_grads(info, fsdp, n2_pieces[0] + n2_pieces[1], actives, grad_hiddens, c_all)
    down_grad, up_grad = lax.psum_scatter(feed_grad, "fsdp", scatter_dimension=0, tiled=False)
    down_grad = down_grad.astype(F32)

    grad_middles, branches, grads_in = [], [], []
    for m in micro_range:
        grad_middle, branch, *grads_out, part = middle_back(
            info, fsdp, two_parts[m], after(middles[m], feed_grad), c_own[m], vec, out_mine, out_other
        )
        grad_middles.append(grad_middle)
        branches.append(branch)
        sums.append(part)
        if m + 1 < micros:
            middles[m + 1] = after(middles[m + 1], branch)
        grads_in.append(seq_exchange(grads_out))

    out_here, out_there = core_grad(info, fsdp, attendeds, branches)
    out_blocks = core_split(info, fsdp, out_here, hop(out_there, 1))
    out_grad = scatter_far(scatter_near(*out_blocks, fsdp, at_f), fsdp, at_f)

    grads_in[0][0] = after(grads_in[0][0], branches[-1])
    joined_grads, inputs_back = [], []
    one_parts = []
    for m in micro_range:
        grad_joined, chip, sib, part = attention_back(
            info,
            fsdp,
            joineds[m],
            probs[m],
            [g.reshape(images, tokens, width) for g in grads_in[m]],
            hats[m],
            w_qkv,
        )
        joined_grads.append(grad_joined.reshape(SEQ * rows, triple))
        sums.append(part)
        if m + 1 < micros:
            joineds[m + 1] = after(joineds[m + 1], grad_joined)
        chip = chip.reshape(2, rows, model)
        came, far = seq_scatter(chip, sib.reshape(2, rows, model))
        one_parts.append((chip[0], came[0], hop(far, 2)))
    outputs = []
    for m in micro_range:
        chip, sib = down_parts[m]
        came, far = seq_scatter(chip, after(sib, branches[-1]))
        total = chip[0].astype(F32) + came[0].astype(F32) + hop(far, 2).astype(F32)
        result = middles[m] + total + vec[7:8]
        outputs.append(result.astype(BF).reshape(images, tokens, model))
    for m in micro_range:
        a, b, c = one_parts[m]
        grad_one = a.astype(F32) + b.astype(F32) + c.astype(F32)
        hat, scale = norm_parts(x_own[m].astype(F32))
        back = grad_middles[m] + norm_back(grad_one, hat, scale, vec[0:1])
        inputs_back.append(back.astype(BF).reshape(images, tokens, model))

    qkv_grad = weight_grad(
        info,
        fsdp,
        [n.reshape(SEQ * rows, model) for n in n1s],
        joined_grads,
        sums=sums,
        shape=(group_rows, model, triple),
    )
    qkv_grad = scatter_far(scatter_near(*qkv_grad, fsdp, at_f), fsdp, at_f)
    up_bias_grad = qkv_grad[:, triple + VECTORS]

    last = jnp.concatenate([qkv_grad.astype(BF), out_grad.astype(BF), up_grad], axis=1)
    last = lax.all_to_all(last.reshape(SEQ, depth, -1), "seq", 0, 0, tiled=True)
    qkv_weight_grad, out_weight_grad, up_weight_grad, vector_grads = unpack(last, model, units)
    vector_grads = vector_grads[:, :VECTORS].T

    return (
        jnp.stack(outputs),
        jnp.stack(inputs_back),
        vector_grads[0],
        vector_grads[1],
        qkv_weight_grad,
        vector_grads[2],
        vector_grads[3],
        out_weight_grad,
        vector_grads[4],
        vector_grads[5],
        vector_grads[6],
        up_weight_grad,
        up_bias_grad,
        down_grad,
        vector_grads[7],
    )


def solution(mesh):
    shard = P(BOTH)
    tokens = P(None, "fsdp", "seq", None)
    in_specs = (tokens, P(None, "fsdp", None), tokens) + (shard,) * 13
    out_specs = (tokens, tokens) + (shard,) * 13
    return jax.shard_map(
        functools.partial(on_device, mesh.shape["fsdp"]),
        mesh=mesh,
        in_specs=in_specs,
        out_specs=out_specs,
        check_vma=False,
    )
```

```python
import functools

import jax
import jax.numpy as jnp
from jax import lax
from jax.experimental import pallas as pl
from jax.experimental.pallas import tpu as pltpu
from jax.sharding import PartitionSpec as P

HEAD_DIM = 64
SEQ = 4
BF = jnp.bfloat16
F32 = jnp.float32
FILL = -1e30
LANES = 128
VECTORS = 8
SCALE = HEAD_DIM ** (-0.5)
BOTH = ("fsdp", "seq")
ORDER = (0, 2, 1, 3)
ANY = pl.BlockSpec(memory_space=pl.ANY)
SMEM = pl.BlockSpec(memory_space=pltpu.SMEM)
VMEM = pl.BlockSpec(memory_space=pltpu.VMEM)


def after(array, *done):
    return lax.optimization_barrier((array,) + done)[0] if done else array


def hop(array, mask):
    return lax.ppermute(array, "seq", [(i, i ^ mask) for i in range(SEQ)])


def seq_gather(array):
    far = hop(array, 2)
    return [array, far, hop(array, 1), hop(far, 1)]


def seq_gather(array, *done):
    far = hop(array, 2)
    return [array, far, hop(array, 1), hop(after(far, *done), 1)]


def seq_exchange(pieces):
    return [pieces[0]] + [hop(pieces[k], ORDER[k]) for k in (1, 2, 3)]


def seq_scatter(chip, sibling):
    came = hop(sibling, 1)
    return came, (chip[1].astype(F32) + came[1].astype(F32)).astype(BF)


def digits_of(size):
    digits, stride = [], 1
    while stride < size:
        radix = 2 if stride == 1 or size // stride < 4 else 4
        digits.append((stride, radix))
        stride *= radix
    return digits


def shift(array, size, stride, radix, step):
    pairs = []
    for i in range(size):
        digit = i // stride % radix
        pairs.append((i, i + ((digit + step) % radix - digit) * stride))
    return lax.ppermute(array, "fsdp", pairs)


def steps_of(radix):
    return [step for _, step in sorted((min(s, radix - s), s) for s in range(1, radix))]


def fsdp_owners(size, place):
    owners = [place]
    for stride, radix in reversed(digits_of(size)):
        digit = place // stride % radix
        changes = [((digit + radix - step) % radix - digit) * stride for step in steps_of(radix)]
        owners = owners + [o + change for change in changes for o in owners]
    return owners


def fsdp_gather(array, size):
    pieces = [array]
    for stride, radix in reversed(digits_of(size)):
        pieces = pieces + [
            shift(piece, size, stride, radix, step) for step in steps_of(radix) for piece in pieces
        ]
    return pieces


def split_kernel(count, radix, digit_ref, *refs):
    parts, outs = refs[:count], refs[count:]
    digit = digit_ref[0]
    for step, out in zip([0] + steps_of(radix), outs):
        at = lax.rem(digit + step, radix)
        out[0] = functools.reduce(jnp.add, [part[0, at].astype(F32) for part in parts]).astype(out.dtype)


def split_sum(parts, outer, radix, digit):
    rows, cols = parts[0].shape[1:]
    return pl.pallas_call(
        functools.partial(split_kernel, len(parts), radix),
        grid=(outer,),
        in_specs=[SMEM]
        + [pl.BlockSpec((1, radix, rows, cols), lambda i: (i, 0, 0, 0))] * len(parts),
        out_specs=[pl.BlockSpec((1, rows, cols), lambda i: (i, 0, 0))] * radix,
        out_shape=[jax.ShapeDtypeStruct((outer, rows, cols), BF)] * radix,
        compiler_params=params(),
        name="split",
    )(digit, *[part.reshape(outer, radix, rows, cols) for part in parts])


def scatter_near(keep, send, size, place):
    digits = digits_of(size)
    parts = [keep, shift(send, size, *digits[0], 1)]
    stride, radix = digits[1]
    digit = place // stride % radix
    outer = keep.shape[0] // radix
    return split_sum(parts, outer, radix, jnp.asarray(digit, jnp.int32).reshape(1))


def scatter_far(blocks, size, place):
    digits = digits_of(size)
    for at, (stride, radix) in enumerate(digits[1:]):
        parts = list(blocks[:1]) + [
            shift(block, size, stride, radix, step) for block, step in zip(blocks[1:], steps_of(radix))
        ]
        if at + 2 < len(digits):
            stride, radix = digits[at + 2]
            digit = place // stride % radix
            outer = parts[0].shape[0] // radix
            blocks = split_sum(parts, outer, radix, jnp.asarray(digit, jnp.int32).reshape(1))
    return parts


def rows_dot(left, right):
    return lax.dot_general(left, right, (((0,), (0,)), ((), ())), preferred_element_type=F32)


def cols_dot(left, right):
    return lax.dot_general(left, right, (((1,), (1,)), ((), ())), preferred_element_type=F32)


def plain_dot(left, right):
    return jnp.dot(left, right, preferred_element_type=F32)


def norm_parts(values):
    average = jnp.mean(values, axis=-1, keepdims=True)
    centred = values - average
    scale = lax.rsqrt(jnp.mean(centred * centred, axis=-1, keepdims=True) + 1e-06)
    return centred * scale, scale


def norm_back(grad, hat, scale, gain):
    spread = grad * gain
    return scale * (
        spread
        - jnp.mean(spread, axis=-1, keepdims=True)
        - hat * jnp.mean(spread * hat, axis=-1, keepdims=True)
    )


def column_sums(values):
    return jnp.sum(values, axis=0, keepdims=True)


def piece_copies(info, pieces, low, target, sem):
    block = pieces[0].shape[0]
    cols = target.shape[1]
    return [
        pltpu.make_async_copy(
            piece.at[:, pl.ds(low, cols)],
            target.at[pl.ds(pl.multiple_of(info[at] * block, block), block), :],
            sem.at[at],
        )
        for at, piece in enumerate(pieces)
    ]


def params():
    return pltpu.CompilerParams(vmem_limit_bytes=60 * 2**20)


def estimate(flops, moved):
    return pl.CostEstimate(flops=int(flops), bytes_accessed=int(moved), transcendentals=0)


def pack_kernel(fsdp, qkv, out, vectors, up, ref):
    width = qkv.shape[1] // 3 // SEQ
    half = out.shape[1] // 2
    block = up.shape[1] // SEQ // fsdp
    for s in range(SEQ):
        spans = [(qkv, (part * SEQ + s) * width, width) for part in range(3)]
        spans += [(vectors, 0, LANES), (out, (s % 2) * half, half)]
        spans += [(up, (f * SEQ + s) * block, block) for f in range(fsdp)]
        low = 0
        for source, start, cols in spans:
            ref[s, :, low : low + cols] = source[:, start : start + cols]
            low += cols


def pack(fsdp, qkv, out, vectors, up):
    depth = qkv.shape[0]
    cols = (qkv.shape[1] + up.shape[1]) // SEQ + LANES + out.shape[1] // 2
    return pl.pallas_call(
        functools.partial(pack_kernel, fsdp),
        in_specs=[VMEM] * 4,
        out_specs=VMEM,
        out_shape=jax.ShapeDtypeStruct((SEQ, depth, cols), BF),
        compiler_params=params(),
        name="pack",
    )(qkv, out, vectors, up)


def collect_kernel(counts, *refs):
    *parts, out, wide = refs
    low = at = 0
    for group, count in enumerate(counts):
        blocks = [part[...].reshape(part.shape[-2:]).astype(F32) for part in parts[at : at + count]]
        total = functools.reduce(jnp.add, blocks)
        out[:, low : low + total.shape[1]] = total.astype(BF)
        if group == 0:
            wide[...] = total[:, total.shape[1] - LANES :]
        low += total.shape[1]
        at += count


def collect(*groups):
    rows = groups[0][0].shape[-2]
    cols = sum(group[0].shape[-1] for group in groups)
    parts = [part for group in groups for part in group]
    return pl.pallas_call(
        functools.partial(collect_kernel, [len(group) for group in groups]),
        in_specs=[VMEM] * len(parts),
        out_specs=[VMEM] * 2,
        out_shape=[jax.ShapeDtypeStruct((rows, cols), BF), jax.ShapeDtypeStruct((rows, LANES), F32)],
        compiler_params=params(),
        name="collect",
    )(*parts)


def unpack_kernel(ref, qkv, out, up, vectors):
    width = qkv.shape[1] // 3 // SEQ
    half = out.shape[1] // 2
    units = up.shape[1] // SEQ
    low = 3 * width + LANES
    block = ref.shape[1] * SEQ
    for s in range(SEQ):
        for part in range(3):
            at = (part * SEQ + s) * width
            qkv[:, at : at + width] = ref[s, :, part * width : (part + 1) * width].astype(F32)
        for part in range(units // block):
            at = (part * SEQ + s) * block
            start = low + half + part * block
            up[:, at : at + block] = ref[s, :, start : start + block].astype(F32)
    wide = lambda s, start, cols: ref[s, :, start : start + cols].astype(F32)
    vectors[...] = functools.reduce(jnp.add, [wide(s, 3 * width, LANES) for s in range(SEQ)])
    for core in range(2):
        out[:, core * half : (core + 1) * half] = wide(core, low, half) + wide(core + 2, low, half)


def unpack(came, model, units):
    depth = came.shape[1]
    cols = (3 * model, model, SEQ * units, LANES)
    return pl.pallas_call(
        unpack_kernel,
        in_specs=[VMEM],
        out_specs=[VMEM] * 4,
        out_shape=[jax.ShapeDtypeStruct((depth, n), F32) for n in cols],
        compiler_params=params(),
        name="unpack",
    )(came)


def place_kernel(count, low, info, *refs):
    pieces, out, scratch, sem = refs[:count], refs[count], refs[count + 1], refs[count + 2]
    copies = piece_copies(info, pieces, low, scratch, sem)
    for copy in copies:
        copy.start()
    for copy in copies:
        copy.wait()
    out[...] = scratch[...]


def placed(info, pieces, low, cols):
    count = len(pieces)
    rows = count * pieces[0].shape[0]
    return pl.pallas_call(
        functools.partial(place_kernel, count, low),
        in_specs=[SMEM] + [ANY] * count,
        out_specs=VMEM,
        out_shape=jax.ShapeDtypeStruct((rows, cols), BF),
        scratch_shapes=[pltpu.VMEM((rows, cols), BF), pltpu.SemaphoreType.DMA((count,))],
        compiler_params=params(),
        name="placed",
    )(info, *pieces)


def row_copies(sources, target, sem):
    copies, low = [], 0
    for at, source in enumerate(sources):
        rows = source.shape[0]
        copies.append(pltpu.make_async_copy(source, target.at[pl.ds(low, rows), :], sem.at[at]))
        low += rows
    return copies


def weight_grad_kernel(lefts, rights, left_at, right_at, info, *refs):
    more = len(refs) - lefts - rights - 8
    left_refs, right_refs = refs[:lefts], refs[lefts : lefts + rights]
    extra = refs[lefts + rights : lefts + rights + more]
    keep, send, left, right, out, left_sem, right_sem, out_sem = refs[lefts + rights + more :]
    copies = row_copies(left_at(info, left_refs), left, left_sem) + row_copies(
        right_at(info, right_refs), right, right_sem
    )
    for copy in copies:
        copy.start()
    total, cols = left.shape[1], right.shape[1]
    if more:
        sums = functools.reduce(jnp.add, [ref[...] for ref in extra])
        sums = jnp.concatenate([sums, jnp.zeros((LANES - sums.shape[0], total), F32)], axis=0)
        out[:, cols:] = sums.T.astype(BF)
    for copy in copies:
        copy.wait()
    tile = min(256, total)
    for low in range(0, total, tile):
        out[low : low + tile, :cols] = rows_dot(left[:, low : low + tile], right[...]).astype(BF)
    groups, block = keep.shape[:2]
    low_digit = info[0] % 2
    moves = []
    for at in range(groups):
        for which, (ref, side) in enumerate(((keep, low_digit), (send, 1 - low_digit))):
            start = pl.multiple_of((2 * at + side) * block, block)
            moves.append(
                pltpu.make_async_copy(out.at[pl.ds(start, block), :], ref.at[at], out_sem.at[2 * at + which])
            )
    for move in moves:
        move.start()
    for move in moves:
        move.wait()


def plain_rows(info, refs):
    return refs


def weight_grad(info, fsdp, lefts, rights, left_at=plain_rows, right_at=plain_rows, sums=(), shape=None):
    rows, total, cols = shape
    wide = cols + (LANES if sums else 0)
    out = jax.ShapeDtypeStruct((fsdp // 2, total // fsdp, wide), BF)
    return pl.pallas_call(
        functools.partial(weight_grad_kernel, len(lefts), len(rights), left_at, right_at),
        in_specs=[SMEM] + [ANY] * (len(lefts) + len(rights)) + [VMEM] * len(sums),
        out_specs=[ANY] * 2,
        out_shape=[out] * 2,
        scratch_shapes=[
            pltpu.VMEM((rows, total), BF),
            pltpu.VMEM((rows, cols), BF),
            pltpu.VMEM((total, wide), BF),
            pltpu.SemaphoreType.DMA((16,)),
            pltpu.SemaphoreType.DMA((16,)),
            pltpu.SemaphoreType.DMA((fsdp,)),
        ],
        compiler_params=params(),
        cost_estimate=estimate(2 * rows * total * cols, 2 * rows * (total + cols) + 2 * total * cols),
        name="weight_grad",
    )(info, *lefts, *rights, *sums)


def core_grad_kernel(count, core_at, info, *refs):
    lefts, rights = refs[:count], refs[count : 2 * count]
    here, there = refs[2 * count :]
    total, half = here.shape
    core = info[core_at]
    for ref, side in ((here, core), (there, 1 - core)):
        cols = pl.ds(pl.multiple_of(side * half, half), half)
        ref[...] = functools.reduce(
            jnp.add, [rows_dot(left[...], right[:, cols]) for left, right in zip(lefts, rights)]
        ).astype(BF)


def core_grad(info, fsdp, lefts, rights):
    model = lefts[0].shape[1]
    half = jax.ShapeDtypeStruct((model, model // 2), BF)
    rows = lefts[0].shape[0] * len(lefts)
    return pl.pallas_call(
        functools.partial(core_grad_kernel, len(lefts), fsdp + 1),
        in_specs=[SMEM] + [VMEM] * (2 * len(lefts)),
        out_specs=[VMEM] * 2,
        out_shape=[half] * 2,
        compiler_params=params(),
        cost_estimate=estimate(2 * rows * model * model, 4 * 2**20),
        name="core_grad",
    )(info, *lefts, *rights)


def core_split_kernel(info, here, came, keep, send):
    groups, block = keep.shape[:2]
    low_digit = info[0] % 2
    for at in range(groups):
        for ref, side in ((keep, low_digit), (send, 1 - low_digit)):
            place = pl.ds(pl.multiple_of((2 * at + side) * block, block), block)
            ref[at] = (here[place].astype(F32) + came[place].astype(F32)).astype(BF)


def core_split(info, fsdp, here, came):
    total, half = here.shape
    out = jax.ShapeDtypeStruct((fsdp // 2, total // fsdp, half), BF)
    return pl.pallas_call(
        core_split_kernel,
        in_specs=[SMEM] + [VMEM] * 2,
        out_specs=[VMEM] * 2,
        out_shape=[out] * 2,
        compiler_params=params(),
        name="core_split",
    )(info, here, came)


def attention_kernel(count, info, x0, x1, x2, x3, keep_ref, *refs):
    pieces = refs[:count]
    n1_ref, hat_ref, joined_ref, e0, e1, e2, e3, probs_ref, vec, weight, sem = refs[count:]
    tokens, model = x0.shape[1:]
    rows = SEQ * tokens
    triple = weight.shape[1] - LANES
    width = triple // 3
    copies = piece_copies(info, pieces, 0, weight, sem)

    @pl.when(pl.program_id(0) == 0)
    def _():
        for copy in copies:
            copy.start()
        for copy in copies:
            copy.wait()
        vec[...] = weight[:, triple:].astype(F32).T[: vec.shape[0]]

    values = jnp.concatenate([x[0].astype(F32) for x in (x0, x1, x2, x3)], axis=0)
    hat, _ = norm_parts(values)
    hat_ref[...] = hat.astype(BF).reshape(hat_ref.shape)
    normed = (hat * vec[0:1, :] + vec[1:2, :]).astype(BF)
    n1_ref[...] = normed.reshape(n1_ref.shape)
    place = pl.multiple_of(info[count] * width, width)
    bias = jnp.concatenate(
        [
            vec[2:3, pl.ds(place, width)],
            jnp.zeros((1, width), F32),
            vec[3:4, pl.ds(place, width)],
        ],
        axis=1,
    )
    joined = (plain_dot(normed, weight[:, :triple]) + bias).astype(BF)
    joined_ref[...] = joined.reshape(joined_ref.shape)
    keep = keep_ref[0] > 0
    outs = []
    for head in range(width // HEAD_DIM):
        low = head * HEAD_DIM
        q = joined[:, low : low + HEAD_DIM] * jnp.asarray(SCALE, BF)
        k = joined[:, width + low : width + low + HEAD_DIM]
        v = joined[:, 2 * width + low : 2 * width + low + HEAD_DIM]
        scores = jnp.where(keep, cols_dot(k, q), FILL)
        mass = jnp.exp(scores - jnp.max(scores, axis=0, keepdims=True))
        probs = (mass * (1.0 / jnp.sum(mass, axis=0, keepdims=True))).astype(BF)
        probs_ref[0, head] = probs
        outs.append(rows_dot(v, probs))
    attended = jnp.concatenate(outs, axis=0).T.astype(BF)
    for at, ref in enumerate((e0, e1, e2, e3)):
        ref[...] = attended[at * tokens : (at + 1) * tokens]


def attention(info, x_pieces, keep, pieces, triple):
    images, tokens, model = x_pieces[0].shape
    count = len(pieces)
    width = triple // 3
    rows = SEQ * tokens
    heads = width // HEAD_DIM
    group_block = lambda cols: pl.BlockSpec((SEQ, 1, tokens, cols), lambda i: (0, i, 0, 0))
    group_shape = lambda cols: jax.ShapeDtypeStruct((SEQ, images, tokens, cols), BF)
    return pl.pallas_call(
        functools.partial(attention_kernel, count),
        grid=(images,),
        in_specs=[SMEM]
        + [pl.BlockSpec((1, tokens, model), lambda i: (i, 0, 0))] * SEQ
        + [pl.BlockSpec((1, rows, 1), lambda i: (i, 0, 0))]
        + [ANY] * count,
        out_specs=[group_block(model), group_block(model), group_block(triple)]
        + [pl.BlockSpec((tokens, width), lambda i: (i, 0))] * SEQ
        + [
            pl.BlockSpec((1, heads, rows, rows), lambda i: (i, 0, 0, 0)),
            pl.BlockSpec((16, model), lambda i: (0, 0)),
        ],
        out_shape=[group_shape(model), group_shape(model), group_shape(triple)]
        + [jax.ShapeDtypeStruct((images * tokens, width), BF)] * SEQ
        + [
            jax.ShapeDtypeStruct((images, heads, rows, rows), BF),
            jax.ShapeDtypeStruct((16, model), F32),
        ],
        scratch_shapes=[
            pltpu.VMEM((model, triple + LANES), BF),
            pltpu.SemaphoreType.DMA((count,)),
        ],
        compiler_params=params(),
        cost_estimate=estimate(
            2 * images * rows * (model * triple + 4 * width * rows), 16 * 2**20
        ),
        name="attention",
    )(info, *x_pieces, keep, *pieces)


def out_weight_copies(info, count, mine, other, target, sem):
    half = mine.shape[1]
    core = info[count + 1]
    return [
        pltpu.make_async_copy(
            source, target.at[:, pl.ds(pl.multiple_of(side * half, half), half)], sem.at[which]
        )
        for which, (source, side) in enumerate(((mine, core), (other, 1 - core)))
    ]


def middle_kernel(count, info, e0, e1, e2, e3, x_ref, vec, mine, other, att_ref, mid_ref, n2_ref, weight, sem):
    copies = out_weight_copies(info, count, mine, other, weight, sem)
    for copy in copies:
        copy.start()
    width = e0.shape[1]
    for at, ref in enumerate((e0, e1, e2, e3)):
        place = info[count + 2 + at]
        att_ref[:, pl.ds(pl.multiple_of(place * width, width), width)] = ref[...]
    for copy in copies:
        copy.wait()
    middle = x_ref[...].astype(F32) + plain_dot(att_ref[...], weight[...]) + vec[4:5, :]
    mid_ref[...] = middle
    hat, _ = norm_parts(middle)
    n2_ref[...] = (hat * vec[5:6, :] + vec[6:7, :]).astype(BF)


def middle_part(info, count, heads, x_own, vec, mine, other):
    rows, model = x_own.shape
    return pl.pallas_call(
        functools.partial(middle_kernel, count),
        in_specs=[SMEM] + [VMEM] * 6 + [ANY] * 2,
        out_specs=[VMEM] * 3,
        out_shape=[
            jax.ShapeDtypeStruct((rows, model), BF),
            jax.ShapeDtypeStruct((rows, model), F32),
            jax.ShapeDtypeStruct((rows, model), BF),
        ],
        scratch_shapes=[
            pltpu.VMEM((model, model), BF),
            pltpu.SemaphoreType.DMA((2,)),
        ],
        compiler_params=params(),
        cost_estimate=estimate(2 * rows * model * model, 4 * 2**20),
        name="middle",
    )(info, *heads, x_own, vec, mine, other)


def feed_kernel(micros, *refs):
    n2, cot = refs[:SEQ], refs[SEQ : 2 * SEQ]
    vec, down_ref, up_ref = refs[2 * SEQ : 2 * SEQ + 3]
    down_chip, down_sib, up_chip, up_sib, grads, sums = refs[2 * SEQ + 3 : 2 * SEQ + 9]
    w_up, w_down, n2_in, c_in, act, gh, weight_sem, n2_sem, c_sem = refs[2 * SEQ + 9 :]
    rows = n2[0].shape[0] // micros
    hidden = w_up.shape[1]
    up_copy = pltpu.make_async_copy(up_ref, w_up, weight_sem.at[0])
    down_copies = [pltpu.make_async_copy(down_ref, w_down, weight_sem.at[1])]
    by_micro = lambda pieces: [p.at[pl.ds(m * rows, rows), :] for m in range(micros) for p in pieces]
    n2_copies = row_copies(by_micro(n2), n2_in, n2_sem)
    c_copies = row_copies(by_micro(cot), c_in, c_sem)
    for copy in n2_copies + [up_copy] + c_copies + down_copies:
        copy.start()
    for copy in n2_copies + [up_copy]:
        copy.wait()
    total = jnp.zeros((1, hidden), F32)
    for part in range(2 * micros):
        micro, half = part // 2, part % 2
        span = slice(part * 2 * rows, (part + 1) * 2 * rows)
        values = plain_dot(n2_in[span], w_up[...]) + vec[8:9, :]
        normal = 0.5 * (1.0 + lax.erf(values * (2.0**-0.5)))
        slope = normal + values * (jnp.exp(values * values * -0.5) * 0.3989422804014327)
        active = (values * normal).astype(BF)
        act[span] = active
        if part == 0:
            for copy in c_copies + down_copies:
                copy.wait()
        grad_hidden = (slope * cols_dot(c_in[span], w_down[...])).astype(BF)
        gh[span] = grad_hidden
        total = total + column_sums(grad_hidden.astype(F32))
        place = slice(micro * rows, (micro + 1) * rows)
        down_part = plain_dot(active, w_down[...]).astype(BF)
        up_part = cols_dot(grad_hidden, w_up[...]).astype(BF)
        for k in range(2):
            (down_chip, down_sib)[half][k, place] = down_part[k * rows : (k + 1) * rows]
            (up_chip, up_sib)[half][k, place] = up_part[k * rows : (k + 1) * rows]
    sums[...] = jnp.zeros(sums.shape, F32)
    sums[8:9, :] = total
    block = grads.shape[2]
    step = max(256 // block, 1)
    for which, (left, right) in enumerate(((act, c_in), (n2_in, gh))):
        for at in range(0, grads.shape[0], step):
            part = rows_dot(left[:, at * block : (at + step) * block], right[...]).astype(BF)
            grads[at : at + step, which] = part.reshape(step, block, part.shape[1])


def feed(fsdp, micros, n2_pieces, c_pieces, vec, w_down, w_up):
    rows, model = c_pieces[0].shape
    hidden = w_down.shape[0]
    pair = jax.ShapeDtypeStruct((2, rows, model), BF)
    group = SEQ * rows
    return pl.pallas_call(
        functools.partial(feed_kernel, micros),
        in_specs=[ANY] * (2 * SEQ) + [VMEM] + [ANY] * 2,
        out_specs=[VMEM] * 6,
        out_shape=[pair] * 4
        + [
            jax.ShapeDtypeStruct((fsdp, 2, model // fsdp, model), BF),
            jax.ShapeDtypeStruct((16, model), F32),
        ],
        scratch_shapes=[
            pltpu.VMEM((model, hidden), BF),
            pltpu.VMEM((hidden, model), BF),
            pltpu.VMEM((group, model), BF),
            pltpu.VMEM((group, model), BF),
            pltpu.VMEM((group, hidden), BF),
            pltpu.VMEM((group, hidden), BF),
            pltpu.SemaphoreType.DMA((2,)),
            pltpu.SemaphoreType.DMA((SEQ * micros,)),
            pltpu.SemaphoreType.DMA((SEQ * micros,)),
        ],
        compiler_params=params(),
        cost_estimate=estimate(12 * group * model * hidden, 24 * 2**20),
        name="feed",
    )(*n2_pieces, *c_pieces, vec, w_down, w_up)


def middle_back_kernel(count, micros, info, *refs):
    chips, cames, fars = refs[:micros], refs[micros : 2 * micros], refs[2 * micros : 3 * micros]
    mid_ref, c_ref, vec, mine, other = refs[3 * micros : 3 * micros + 5]
    gm_ref, gb_ref, g0, g1, g2, g3, sums, weight, scratch, sem = refs[3 * micros + 5 :]
    copies = out_weight_copies(info, count, mine, other, weight, sem)
    for copy in copies:
        copy.start()
    grad_two = jnp.concatenate(
        [a[0].astype(F32) + b[0].astype(F32) + c[...].astype(F32) for a, b, c in zip(chips, cames, fars)],
        axis=0,
    )
    hat, scale = norm_parts(mid_ref[...])
    cot = c_ref[...].astype(F32)
    grad_middle = cot + norm_back(grad_two, hat, scale, vec[5:6, :])
    gm_ref[...] = grad_middle
    branch = grad_middle.astype(BF)
    gb_ref[...] = branch
    sums[...] = jnp.zeros(sums.shape, F32)
    sums[4:5, :] = column_sums(branch.astype(F32))
    sums[5:6, :] = column_sums(grad_two * hat)
    sums[6:7, :] = column_sums(grad_two)
    sums[7:8, :] = column_sums(cot)
    for copy in copies:
        copy.wait()
    scratch[...] = cols_dot(branch, weight[...]).astype(BF)
    width = g0.shape[1]
    for at, ref in enumerate((g0, g1, g2, g3)):
        place = info[count + 2 + at]
        ref[...] = scratch[:, pl.ds(pl.multiple_of(place * width, width), width)]


def middle_back(info, count, parts, middle, c_own, vec, mine, other):
    rows, model = middle.shape
    micros = len(parts)
    piece = jax.ShapeDtypeStruct((rows, model // SEQ), BF)
    return pl.pallas_call(
        functools.partial(middle_back_kernel, count, micros),
        in_specs=[SMEM] + [VMEM] * (3 * micros + 3) + [ANY] * 2,
        out_specs=[VMEM] * 7,
        out_shape=[
            jax.ShapeDtypeStruct((rows, model), F32),
            jax.ShapeDtypeStruct((rows, model), BF),
        ]
        + [piece] * 4
        + [jax.ShapeDtypeStruct((16, model), F32)],
        scratch_shapes=[
            pltpu.VMEM((model, model), BF),
            pltpu.VMEM((rows, model), BF),
            pltpu.SemaphoreType.DMA((2,)),
        ],
        compiler_params=params(),
        cost_estimate=estimate(2 * rows * model * model, 4 * 2**20),
        name="middle_back",
    )(info, *[p for at in range(3) for p in [part[at] for part in parts]], middle, c_own, vec, mine, other)


def attention_back_kernel(count, info, joined_ref, probs_ref, g0, g1, g2, g3, hat_ref, *refs):
    pieces = refs[:count]
    out_ref, chip_ref, sib_ref, sums, weight, sem = refs[count:]
    tokens = joined_ref.shape[2]
    rows = SEQ * tokens
    triple = joined_ref.shape[3]
    width = triple // 3
    model = weight.shape[0]
    copies = piece_copies(info, pieces, 0, weight, sem)

    @pl.when(pl.program_id(0) == 0)
    def _():
        for copy in copies:
            copy.start()
        sums[...] = jnp.zeros(sums.shape, F32)

    joined = joined_ref[...].reshape(rows, triple)
    grad = jnp.concatenate([g0[...], g1[...], g2[...], g3[...]], axis=0)
    queries, keys, values = [], [], []
    for head in range(width // HEAD_DIM):
        low = head * HEAD_DIM
        q = joined[:, low : low + HEAD_DIM] * jnp.asarray(SCALE, BF)
        k = joined[:, width + low : width + low + HEAD_DIM] * jnp.asarray(SCALE, BF)
        v = joined[:, 2 * width + low : 2 * width + low + HEAD_DIM]
        ga = grad[:, low : low + HEAD_DIM]
        probs = probs_ref[0, head]
        values.append(plain_dot(probs, ga).astype(BF))
        wide = probs.astype(F32)
        weighted = wide * cols_dot(v, ga)
        centre = jnp.sum(weighted, axis=0, keepdims=True)
        grad_scores = (weighted - wide * centre).astype(BF)
        keys.append(plain_dot(grad_scores, q).astype(BF))
        queries.append(rows_dot(k, grad_scores))
    grad_joined = jnp.concatenate(
        [jnp.concatenate(queries, axis=0).T.astype(BF)] + keys + values, axis=1
    )
    out_ref[...] = grad_joined.reshape(out_ref.shape)
    wide = grad_joined.astype(F32)
    place = pl.multiple_of(info[count] * width, width)
    sums[2:3, pl.ds(place, width)] += column_sums(wide[:, :width])
    sums[3:4, pl.ds(place, width)] += column_sums(wide[:, 2 * width :])

    @pl.when(pl.program_id(0) == 0)
    def _():
        for copy in copies:
            copy.wait()

    partial = cols_dot(grad_joined, weight[...])
    hat = hat_ref[...].reshape(rows, model).astype(F32)
    sums[0:1, :] += column_sums(partial * hat)
    sums[1:2, :] += column_sums(partial)
    low = partial.astype(BF)
    half = rows // 2
    chip_ref[...] = low[:half].reshape(chip_ref.shape)
    sib_ref[...] = low[half:].reshape(sib_ref.shape)


def attention_back(info, joined, probs, grads, hat, pieces):
    count = len(pieces)
    _, images, tokens, triple = joined.shape
    model = hat.shape[3]
    width = triple // 3
    rows = SEQ * tokens
    heads = width // HEAD_DIM
    pair = jax.ShapeDtypeStruct((2, images, tokens, model), BF)
    group_block = lambda n, cols: pl.BlockSpec((n, 1, tokens, cols), lambda i: (0, i, 0, 0))
    return pl.pallas_call(
        functools.partial(attention_back_kernel, count),
        grid=(images,),
        in_specs=[
            SMEM,
            group_block(SEQ, triple),
            pl.BlockSpec((1, heads, rows, rows), lambda i: (i, 0, 0, 0)),
        ]
        + [pl.BlockSpec((tokens, width), lambda i: (i, 0))] * SEQ
        + [group_block(SEQ, model)]
        + [ANY] * count,
        out_specs=[
            group_block(SEQ, triple),
            group_block(2, model),
            group_block(2, model),
            pl.BlockSpec((16, model), lambda i: (0, 0)),
        ],
        out_shape=[
            jax.ShapeDtypeStruct(joined.shape, BF),
            pair,
            pair,
            jax.ShapeDtypeStruct((16, model), F32),
        ],
        scratch_shapes=[pltpu.VMEM((model, triple), BF), pltpu.SemaphoreType.DMA((count,))],
        compiler_params=params(),
        cost_estimate=estimate(
            2 * images * rows * (model * triple + 8 * width * rows), 8 * 2**20
        ),
        name="attention_back",
    )(info, joined, probs, *grads, hat, *pieces)


def on_device(
    fsdp,
    inputs,
    keep_mask,
    cotangent,
    first_gain,
    first_shift,
    qkv_weight,
    query_bias,
    value_bias,
    out_weight,
    out_bias,
    second_gain,
    second_shift,
    up_weight,
    up_bias,
    down_weight,
    down_bias,
):
    micros, images, tokens, model = inputs.shape
    rows = images * tokens
    at_f, at_s = lax.axis_index("fsdp"), lax.axis_index("seq")
    depth = qkv_weight.shape[0]
    block = SEQ * depth
    width = model // SEQ
    triple = 3 * width
    half = model // 2
    unit_block = up_bias.shape[0]
    units = fsdp * unit_block
    core = at_s & 1
    micro_range = range(micros)
    info = jnp.stack(
        [jnp.asarray(v, jnp.int32) for v in fsdp_owners(fsdp, at_f)]
        + [at_s, core]
        + [at_s ^ mask for mask in ORDER]
    )

    vectors = jnp.stack(
        [
            first_gain,
            first_shift,
            query_bias,
            value_bias,
            out_bias,
            second_gain,
            second_shift,
            down_bias,
        ],
        axis=1,
    )
    vectors = jnp.pad(vectors, ((0, 0), (0, LANES - VECTORS)))
    to_send = pack(fsdp, qkv_weight, out_weight, vectors, up_weight)
    arrived = lax.all_to_all(to_send, "seq", 0, 0, tiled=True).reshape(block, -1)
    early = triple + LANES
    bias_column = jnp.pad(up_bias[:, None], ((0, 0), (VECTORS, LANES - VECTORS - 1)))
    first_group = jnp.concatenate(
        [
            arrived[:, :triple],
            arrived[:, triple:early] + bias_column,
            arrived[:, early : early + half],
        ],
        axis=1,
    )
    x_pieces = seq_gather(inputs.reshape(micros * rows, model))
    first_pieces = fsdp_gather(first_group, fsdp)
    w_down = lax.all_gather(down_weight, "fsdp", tiled=True)
    w_up = lax.all_gather(arrived[:, early + half :], "fsdp", tiled=True)

    x_own = inputs.reshape(micros * rows, model)
    c_own = cotangent.reshape(micros * rows, model)
    keep = keep_mask.reshape(micros * images, SEQ, tokens)
    keep = jnp.stack(
        [lax.dynamic_index_in_dim(keep, at_s ^ mask, 1, keepdims=False) for mask in ORDER], axis=1
    )
    n1, hat_one, joined, *heads_out, probs, vec = attention(
        info,
        [x.reshape(micros * images, tokens, model) for x in x_pieces],
        keep.reshape(micros * images, SEQ * tokens, 1),
        first_pieces,
        triple,
    )
    c_pieces = seq_gather(after(c_own, x_pieces[1]))
    heads_out[1:] = [after(h, c_pieces[1]) for h in heads_out[1:]]
    heads_in = seq_exchange(heads_out)
    out_mine = placed(info, first_pieces, early, half)
    out_other = hop(out_mine, 1)
    attended, middle, normed = middle_part(
        info, fsdp, heads_in, x_own, vec, out_mine, out_other
    )
    n2_pieces = seq_gather(normed)

    group_rows = micros * SEQ * rows
    down_chip, down_sib, up_chip, up_sib, feed_grad, part = feed(
        fsdp, micros, n2_pieces, c_pieces, vec, w_down, w_up
    )
    sums = [part]
    down_grad, up_grad = lax.psum_scatter(feed_grad, "fsdp", scatter_dimension=0, tiled=False)
    down_grad = down_grad.astype(F32)
    came, far = seq_scatter(up_chip, up_sib)
    two_parts = [(up_chip, came, hop(far, 2))]
    down_parts = [(down_chip, down_sib)]

    grad_middle, branch, *grads_out, part = middle_back(
        info, fsdp, two_parts, middle, c_own, vec, out_mine, out_other
    )
    sums.append(part)
    grads_in = seq_exchange(grads_out)
    out_here, out_there = core_grad(info, fsdp, [attended], [branch])
    down_sums = []
    for chip, sib in down_parts:
        came, far = seq_scatter(chip, after(sib, branch))
        down_sums.append((chip[0], came[0], far))
    out_blocks = core_split(info, fsdp, out_here, hop(out_there, 1))
    grads_in[0] = after(grads_in[0], *[far for _, _, far in down_sums], out_blocks[1])

    grad_joined, chip, sib, part = attention_back(info, joined, probs, grads_in, hat_one, first_pieces)
    sums.append(part)
    qkv_blocks = weight_grad(
        info,
        fsdp,
        [n1.reshape(group_rows, model)],
        [grad_joined.reshape(group_rows, triple)],
        sums=sums,
        shape=(group_rows, model, triple),
    )
    chip = chip.reshape(2, micros * rows, model)
    came, far = seq_scatter(chip, sib.reshape(2, micros * rows, model))
    grad_one = chip[0].astype(F32) + came[0].astype(F32) + hop(far, 2).astype(F32)

    [(a, b, c)] = down_sums
    total = a.astype(F32) + b.astype(F32) + hop(c, 2).astype(F32)
    layer_out = (middle + total + vec[7:8]).astype(BF).reshape(micros, images, tokens, model)
    hat, scale = norm_parts(x_own.astype(F32))
    input_grad = grad_middle + norm_back(grad_one, hat, scale, vec[0:1])
    input_grad = input_grad.astype(BF).reshape(micros, images, tokens, model)

    out_parts = scatter_far(scatter_near(*out_blocks, fsdp, at_f), fsdp, at_f)
    qkv_parts = scatter_far(scatter_near(*qkv_blocks, fsdp, at_f), fsdp, at_f)

    last, own_vectors = collect(qkv_parts, out_parts, [up_grad])
    up_bias_grad = own_vectors[:, VECTORS]
    last = lax.all_to_all(last.reshape(SEQ, depth, -1), "seq", 0, 0, tiled=True)
    qkv_weight_grad, out_weight_grad, up_weight_grad, vector_grads = unpack(last, model, units)
    vector_grads = vector_grads[:, :VECTORS].T

    return (
        layer_out,
        input_grad,
        vector_grads[0],
        vector_grads[1],
        qkv_weight_grad,
        vector_grads[2],
        vector_grads[3],
        out_weight_grad,
        vector_grads[4],
        vector_grads[5],
        vector_grads[6],
        up_weight_grad,
        up_bias_grad,
        down_grad,
        vector_grads[7],
    )


def solution(mesh):
    shard = P(BOTH)
    tokens = P(None, "fsdp", "seq", None)
    in_specs = (tokens, P(None, "fsdp", None), tokens) + (shard,) * 13
    out_specs = (tokens, tokens) + (shard,) * 13
    return jax.shard_map(
        functools.partial(on_device, mesh.shape["fsdp"]),
        mesh=mesh,
        in_specs=in_specs,
        out_specs=out_specs,
        check_vma=False,
    )
```

```python
import functools

import jax
import jax.numpy as jnp
from jax import lax
from jax.experimental import pallas as pl
from jax.experimental.pallas import tpu as pltpu
from jax.sharding import PartitionSpec as P

HEAD_DIM = 64
SEQ = 4
BF = jnp.bfloat16
F32 = jnp.float32
FILL = -1e30
LANES = 128
VECTORS = 8
SCALE = HEAD_DIM ** (-0.5)
BOTH = ("fsdp", "seq")
ORDER = (0, 2, 1, 3)
ANY = pl.BlockSpec(memory_space=pl.ANY)
SMEM = pl.BlockSpec(memory_space=pltpu.SMEM)
VMEM = pl.BlockSpec(memory_space=pltpu.VMEM)


def after(array, *done):
    return lax.optimization_barrier((array,) + done)[0] if done else array


def hop(array, mask):
    return lax.ppermute(array, "seq", [(i, i ^ mask) for i in range(SEQ)])


def seq_gather(array):
    far = hop(array, 2)
    return [array, far, hop(array, 1), hop(far, 1)]


def seq_gather(array, *done):
    far = hop(array, 2)
    return [array, far, hop(array, 1), hop(after(far, *done), 1)]


def seq_exchange(pieces):
    return [pieces[0]] + [hop(pieces[k], ORDER[k]) for k in (1, 2, 3)]


def seq_scatter(chip, sibling):
    came = hop(sibling, 1)
    return came, (chip[1].astype(F32) + came[1].astype(F32)).astype(BF)


def digits_of(size):
    digits, stride = [], 1
    while stride < size:
        radix = 2 if stride == 1 or size // stride < 4 else 4
        digits.append((stride, radix))
        stride *= radix
    return digits


def shift(array, size, stride, radix, step):
    pairs = []
    for i in range(size):
        digit = i // stride % radix
        pairs.append((i, i + ((digit + step) % radix - digit) * stride))
    return lax.ppermute(array, "fsdp", pairs)


def steps_of(radix):
    return [step for _, step in sorted((min(s, radix - s), s) for s in range(1, radix))]


def fsdp_owners(size, place):
    owners = [place]
    for stride, radix in reversed(digits_of(size)):
        digit = place // stride % radix
        changes = [((digit + radix - step) % radix - digit) * stride for step in steps_of(radix)]
        owners = owners + [o + change for change in changes for o in owners]
    return owners


def fsdp_gather(array, size):
    pieces = [array]
    for stride, radix in reversed(digits_of(size)):
        pieces = pieces + [
            shift(piece, size, stride, radix, step) for step in steps_of(radix) for piece in pieces
        ]
    return pieces


def split_kernel(count, radix, digit_ref, *refs):
    parts, outs = refs[:count], refs[count:]
    digit = digit_ref[0]
    for step, out in zip([0] + steps_of(radix), outs):
        at = lax.rem(digit + step, radix)
        out[0] = functools.reduce(jnp.add, [part[0, at].astype(F32) for part in parts]).astype(out.dtype)


def split_sum(parts, outer, radix, digit):
    rows, cols = parts[0].shape[1:]
    return pl.pallas_call(
        functools.partial(split_kernel, len(parts), radix),
        grid=(outer,),
        in_specs=[SMEM]
        + [pl.BlockSpec((1, radix, rows, cols), lambda i: (i, 0, 0, 0))] * len(parts),
        out_specs=[pl.BlockSpec((1, rows, cols), lambda i: (i, 0, 0))] * radix,
        out_shape=[jax.ShapeDtypeStruct((outer, rows, cols), BF)] * radix,
        compiler_params=params(),
        name="split",
    )(digit, *[part.reshape(outer, radix, rows, cols) for part in parts])


def scatter_near(parts, size, place):
    digits = digits_of(size)
    stride, radix = digits[1]
    digit = place // stride % radix
    outer = parts[0].shape[0] // radix
    return split_sum(parts, outer, radix, jnp.asarray(digit, jnp.int32).reshape(1))


def scatter_far(blocks, size, place):
    digits = digits_of(size)
    for at, (stride, radix) in enumerate(digits[1:]):
        parts = list(blocks[:1]) + [
            shift(block, size, stride, radix, step) for block, step in zip(blocks[1:], steps_of(radix))
        ]
        if at + 2 < len(digits):
            stride, radix = digits[at + 2]
            digit = place // stride % radix
            outer = parts[0].shape[0] // radix
            blocks = split_sum(parts, outer, radix, jnp.asarray(digit, jnp.int32).reshape(1))
    return parts


def rows_dot(left, right):
    return lax.dot_general(left, right, (((0,), (0,)), ((), ())), preferred_element_type=F32)


def cols_dot(left, right):
    return lax.dot_general(left, right, (((1,), (1,)), ((), ())), preferred_element_type=F32)


def plain_dot(left, right):
    return jnp.dot(left, right, preferred_element_type=F32)


def norm_parts(values):
    average = jnp.mean(values, axis=-1, keepdims=True)
    centred = values - average
    scale = lax.rsqrt(jnp.mean(centred * centred, axis=-1, keepdims=True) + 1e-06)
    return centred * scale, scale


def norm_back(grad, hat, scale, gain):
    spread = grad * gain
    return scale * (
        spread
        - jnp.mean(spread, axis=-1, keepdims=True)
        - hat * jnp.mean(spread * hat, axis=-1, keepdims=True)
    )


def column_sums(values):
    return jnp.sum(values, axis=0, keepdims=True)


def piece_copies(info, pieces, low, target, sem):
    block = pieces[0].shape[0]
    cols = target.shape[1]
    return [
        pltpu.make_async_copy(
            piece.at[:, pl.ds(low, cols)],
            target.at[pl.ds(pl.multiple_of(info[at] * block, block), block), :],
            sem.at[at],
        )
        for at, piece in enumerate(pieces)
    ]


def params():
    return pltpu.CompilerParams(vmem_limit_bytes=60 * 2**20)


def estimate(flops, moved):
    return pl.CostEstimate(flops=int(flops), bytes_accessed=int(moved), transcendentals=0)


def pack_kernel(fsdp, qkv, out, vectors, up, ref):
    width = qkv.shape[1] // 3 // SEQ
    half = out.shape[1] // 2
    block = up.shape[1] // SEQ // fsdp
    for s in range(SEQ):
        spans = [(qkv, (part * SEQ + s) * width, width) for part in range(3)]
        spans += [(vectors, 0, LANES), (out, (s % 2) * half, half)]
        spans += [(up, (f * SEQ + s) * block, block) for f in range(fsdp)]
        low = 0
        for source, start, cols in spans:
            ref[s, :, low : low + cols] = source[:, start : start + cols]
            low += cols


def pack(fsdp, qkv, out, vectors, up):
    depth = qkv.shape[0]
    cols = (qkv.shape[1] + up.shape[1]) // SEQ + LANES + out.shape[1] // 2
    return pl.pallas_call(
        functools.partial(pack_kernel, fsdp),
        in_specs=[VMEM] * 4,
        out_specs=VMEM,
        out_shape=jax.ShapeDtypeStruct((SEQ, depth, cols), BF),
        compiler_params=params(),
        name="pack",
    )(qkv, out, vectors, up)


def collect_kernel(counts, *refs):
    *parts, out, wide = refs
    low = at = 0
    for group, count in enumerate(counts):
        blocks = [part[...].reshape(part.shape[-2:]).astype(F32) for part in parts[at : at + count]]
        total = functools.reduce(jnp.add, blocks)
        out[:, low : low + total.shape[1]] = total.astype(BF)
        if group == 0:
            wide[...] = total[:, total.shape[1] - LANES :]
        low += total.shape[1]
        at += count


def collect(*groups):
    rows = groups[0][0].shape[-2]
    cols = sum(group[0].shape[-1] for group in groups)
    parts = [part for group in groups for part in group]
    return pl.pallas_call(
        functools.partial(collect_kernel, [len(group) for group in groups]),
        in_specs=[VMEM] * len(parts),
        out_specs=[VMEM] * 2,
        out_shape=[jax.ShapeDtypeStruct((rows, cols), BF), jax.ShapeDtypeStruct((rows, LANES), F32)],
        compiler_params=params(),
        name="collect",
    )(*parts)


def unpack_up_kernel(ref, up):
    block = ref.shape[1] * SEQ
    for s in range(SEQ):
        for part in range(ref.shape[2] // block):
            at = (part * SEQ + s) * block
            up[:, at : at + block] = ref[s, :, part * block : (part + 1) * block].astype(F32)


def unpack_up(came):
    return pl.pallas_call(
        unpack_up_kernel,
        in_specs=[VMEM],
        out_specs=VMEM,
        out_shape=jax.ShapeDtypeStruct((came.shape[1], SEQ * came.shape[2]), F32),
        compiler_params=params(),
        name="unpack_up",
    )(came)


def unpack_kernel(ref, qkv, out, vectors):
    width = qkv.shape[1] // 3 // SEQ
    half = out.shape[1] // 2
    low = 3 * width + LANES
    for s in range(SEQ):
        for part in range(3):
            at = (part * SEQ + s) * width
            qkv[:, at : at + width] = ref[s, :, part * width : (part + 1) * width].astype(F32)
    wide = lambda s, start, cols: ref[s, :, start : start + cols].astype(F32)
    vectors[...] = functools.reduce(jnp.add, [wide(s, 3 * width, LANES) for s in range(SEQ)])
    for core in range(2):
        out[:, core * half : (core + 1) * half] = wide(core, low, half) + wide(core + 2, low, half)


def unpack(came, model):
    depth = came.shape[1]
    return pl.pallas_call(
        unpack_kernel,
        in_specs=[VMEM],
        out_specs=[VMEM] * 3,
        out_shape=[jax.ShapeDtypeStruct((depth, n), F32) for n in (3 * model, model, LANES)],
        compiler_params=params(),
        name="unpack",
    )(came)


def place_kernel(count, low, info, *refs):
    pieces, out, scratch, sem = refs[:count], refs[count], refs[count + 1], refs[count + 2]
    copies = piece_copies(info, pieces, low, scratch, sem)
    for copy in copies:
        copy.start()
    for copy in copies:
        copy.wait()
    out[...] = scratch[...]


def placed(info, pieces, low, cols):
    count = len(pieces)
    rows = count * pieces[0].shape[0]
    return pl.pallas_call(
        functools.partial(place_kernel, count, low),
        in_specs=[SMEM] + [ANY] * count,
        out_specs=VMEM,
        out_shape=jax.ShapeDtypeStruct((rows, cols), BF),
        scratch_shapes=[pltpu.VMEM((rows, cols), BF), pltpu.SemaphoreType.DMA((count,))],
        compiler_params=params(),
        name="placed",
    )(info, *pieces)


def row_copies(sources, target, sem):
    copies, low = [], 0
    for at, source in enumerate(sources):
        rows = source.shape[0]
        copies.append(pltpu.make_async_copy(source, target.at[pl.ds(low, rows), :], sem.at[at]))
        low += rows
    return copies


def digit_moves(info, out, keep, send, sem):
    groups, block = keep.shape[:2]
    low_digit = info[0] % 2
    moves = []
    for at in range(groups):
        for which, (ref, side) in enumerate(((keep, low_digit), (send, 1 - low_digit))):
            start = pl.multiple_of((2 * at + side) * block, block)
            moves.append(
                pltpu.make_async_copy(out.at[pl.ds(start, block), :], ref.at[at], sem.at[2 * at + which])
            )
    return moves


def core_grad_kernel(core_at, info, left, right, here, there, product):
    groups, block, half = here.shape[1:]
    core, low_digit = info[core_at], info[0] % 2
    for ref, side in ((here, core), (there, 1 - core)):
        cols = pl.ds(pl.multiple_of(side * half, half), half)
        product[...] = rows_dot(left[...], right[:, cols]).astype(BF)
        for at in range(groups):
            for which, digit in enumerate((low_digit, 1 - low_digit)):
                start = pl.multiple_of((2 * at + digit) * block, block)
                ref[which, at] = product[pl.ds(start, block), :]


def core_grad(info, fsdp, left, right):
    rows, model = left.shape
    half = jax.ShapeDtypeStruct((2, fsdp // 2, model // fsdp, model // 2), BF)
    return pl.pallas_call(
        functools.partial(core_grad_kernel, fsdp + 1),
        in_specs=[SMEM] + [VMEM] * 2,
        out_specs=[VMEM] * 2,
        out_shape=[half] * 2,
        scratch_shapes=[pltpu.VMEM((model, model // 2), BF)],
        compiler_params=params(),
        cost_estimate=estimate(2 * rows * model * model, 4 * 2**20),
        name="core_grad",
    )(info, left, right)


def attention_kernel(count, info, x0, x1, x2, x3, keep_ref, *refs):
    pieces = refs[:count]
    n1_ref, hat_ref, joined_ref, e0, e1, e2, e3, probs_ref, vec, weight, sem = refs[count:]
    tokens, model = x0.shape[1:]
    rows = SEQ * tokens
    triple = weight.shape[1] - LANES
    width = triple // 3
    copies = piece_copies(info, pieces, 0, weight, sem)

    @pl.when(pl.program_id(0) == 0)
    def _():
        for copy in copies:
            copy.start()

    values = jnp.concatenate([x[0].astype(F32) for x in (x0, x1, x2, x3)], axis=0)
    hat, _ = norm_parts(values)
    hat_ref[...] = hat.astype(BF).reshape(hat_ref.shape)

    @pl.when(pl.program_id(0) == 0)
    def _():
        for copy in copies:
            copy.wait()
        vec[...] = weight[:, triple:].astype(F32).T[: vec.shape[0]]

    normed = (hat * vec[0:1, :] + vec[1:2, :]).astype(BF)
    n1_ref[...] = normed.reshape(n1_ref.shape)
    place = pl.multiple_of(info[count] * width, width)
    bias = jnp.concatenate(
        [
            vec[2:3, pl.ds(place, width)],
            jnp.zeros((1, width), F32),
            vec[3:4, pl.ds(place, width)],
        ],
        axis=1,
    )
    joined = (plain_dot(normed, weight[:, :triple]) + bias).astype(BF)
    joined_ref[...] = joined.reshape(joined_ref.shape)
    keep = keep_ref[0] > 0
    outs = []
    for head in range(width // HEAD_DIM):
        low = head * HEAD_DIM
        q = joined[:, low : low + HEAD_DIM] * jnp.asarray(SCALE, BF)
        k = joined[:, width + low : width + low + HEAD_DIM]
        v = joined[:, 2 * width + low : 2 * width + low + HEAD_DIM]
        scores = jnp.where(keep, cols_dot(k, q), FILL)
        mass = jnp.exp(scores - jnp.max(scores, axis=0, keepdims=True))
        probs = (mass * (1.0 / jnp.sum(mass, axis=0, keepdims=True))).astype(BF)
        probs_ref[0, head] = probs
        outs.append(rows_dot(v, probs))
    attended = jnp.concatenate(outs, axis=0).T.astype(BF)
    for at, ref in enumerate((e0, e1, e2, e3)):
        ref[...] = attended[at * tokens : (at + 1) * tokens]


def attention(info, x_pieces, keep, pieces, triple):
    images, tokens, model = x_pieces[0].shape
    count = len(pieces)
    width = triple // 3
    rows = SEQ * tokens
    heads = width // HEAD_DIM
    group_block = lambda cols: pl.BlockSpec((SEQ, 1, tokens, cols), lambda i: (0, i, 0, 0))
    group_shape = lambda cols: jax.ShapeDtypeStruct((SEQ, images, tokens, cols), BF)
    return pl.pallas_call(
        functools.partial(attention_kernel, count),
        grid=(images,),
        in_specs=[SMEM]
        + [pl.BlockSpec((1, tokens, model), lambda i: (i, 0, 0))] * SEQ
        + [pl.BlockSpec((1, rows, 1), lambda i: (i, 0, 0))]
        + [ANY] * count,
        out_specs=[group_block(model), group_block(model), group_block(triple)]
        + [pl.BlockSpec((tokens, width), lambda i: (i, 0))] * SEQ
        + [
            pl.BlockSpec((1, heads, rows, rows), lambda i: (i, 0, 0, 0)),
            pl.BlockSpec((16, model), lambda i: (0, 0)),
        ],
        out_shape=[group_shape(model), group_shape(model), group_shape(triple)]
        + [jax.ShapeDtypeStruct((images * tokens, width), BF)] * SEQ
        + [
            jax.ShapeDtypeStruct((images, heads, rows, rows), BF),
            jax.ShapeDtypeStruct((16, model), F32),
        ],
        scratch_shapes=[
            pltpu.VMEM((model, triple + LANES), BF),
            pltpu.SemaphoreType.DMA((count,)),
        ],
        compiler_params=params(),
        cost_estimate=estimate(
            2 * images * rows * (model * triple + 4 * width * rows), 16 * 2**20
        ),
        name="attention",
    )(info, *x_pieces, keep, *pieces)


def out_weight_copies(info, count, mine, other, target, sem):
    half = mine.shape[1]
    core = info[count + 1]
    return [
        pltpu.make_async_copy(
            source, target.at[:, pl.ds(pl.multiple_of(side * half, half), half)], sem.at[which]
        )
        for which, (source, side) in enumerate(((mine, core), (other, 1 - core)))
    ]


def middle_kernel(count, info, e0, e1, e2, e3, x_ref, vec, mine, other, att_ref, mid_ref, n2_ref, weight, sem):
    copies = out_weight_copies(info, count, mine, other, weight, sem)
    for copy in copies:
        copy.start()
    width = e0.shape[1]
    for at, ref in enumerate((e0, e1, e2, e3)):
        place = info[count + 2 + at]
        att_ref[:, pl.ds(pl.multiple_of(place * width, width), width)] = ref[...]
    for copy in copies:
        copy.wait()
    middle = x_ref[...].astype(F32) + plain_dot(att_ref[...], weight[...]) + vec[4:5, :]
    mid_ref[...] = middle
    hat, _ = norm_parts(middle)
    n2_ref[...] = (hat * vec[5:6, :] + vec[6:7, :]).astype(BF)


def middle_part(info, count, heads, x_own, vec, mine, other):
    rows, model = x_own.shape
    return pl.pallas_call(
        functools.partial(middle_kernel, count),
        in_specs=[SMEM] + [VMEM] * 6 + [ANY] * 2,
        out_specs=[VMEM] * 3,
        out_shape=[
            jax.ShapeDtypeStruct((rows, model), BF),
            jax.ShapeDtypeStruct((rows, model), F32),
            jax.ShapeDtypeStruct((rows, model), BF),
        ],
        scratch_shapes=[
            pltpu.VMEM((model, model), BF),
            pltpu.SemaphoreType.DMA((2,)),
        ],
        compiler_params=params(),
        cost_estimate=estimate(2 * rows * model * model, 4 * 2**20),
        name="middle",
    )(info, *heads, x_own, vec, mine, other)


def feed_kernel(micros, *refs):
    n2, cot = refs[:SEQ], refs[SEQ : 2 * SEQ]
    vec, down_ref, up_ref = refs[2 * SEQ : 2 * SEQ + 3]
    down_chip, down_sib, up_chip, up_sib, grads, sums = refs[2 * SEQ + 3 : 2 * SEQ + 9]
    w_up, w_down, n2_in, c_in, act, gh, weight_sem, n2_sem, c_sem = refs[2 * SEQ + 9 :]
    rows = n2[0].shape[0] // micros
    hidden = w_up.shape[1]
    up_copy = pltpu.make_async_copy(up_ref, w_up, weight_sem.at[0])
    down_copies = [pltpu.make_async_copy(down_ref, w_down, weight_sem.at[1])]
    by_micro = lambda pieces: [p.at[pl.ds(m * rows, rows), :] for m in range(micros) for p in pieces]
    n2_copies = row_copies(by_micro(n2), n2_in, n2_sem)
    c_copies = row_copies(by_micro(cot), c_in, c_sem)
    for copy in n2_copies + [up_copy] + c_copies + down_copies:
        copy.start()
    for copy in n2_copies + [up_copy]:
        copy.wait()
    total = jnp.zeros((1, hidden), F32)
    for part in range(2 * micros):
        micro, half = part // 2, part % 2
        span = slice(part * 2 * rows, (part + 1) * 2 * rows)
        values = plain_dot(n2_in[span], w_up[...]) + vec[8:9, :]
        normal = 0.5 * (1.0 + lax.erf(values * (2.0**-0.5)))
        slope = normal + values * (jnp.exp(values * values * -0.5) * 0.3989422804014327)
        active = (values * normal).astype(BF)
        act[span] = active
        if part == 0:
            for copy in c_copies + down_copies:
                copy.wait()
        grad_hidden = (slope * cols_dot(c_in[span], w_down[...])).astype(BF)
        gh[span] = grad_hidden
        total = total + column_sums(grad_hidden.astype(F32))
        place = slice(micro * rows, (micro + 1) * rows)
        down_part = plain_dot(active, w_down[...]).astype(BF)
        up_part = cols_dot(grad_hidden, w_up[...]).astype(BF)
        for k in range(2):
            (down_chip, down_sib)[half][k, place] = down_part[k * rows : (k + 1) * rows]
            (up_chip, up_sib)[half][k, place] = up_part[k * rows : (k + 1) * rows]
    sums[...] = jnp.zeros(sums.shape, F32)
    sums[8:9, :] = total
    block = grads.shape[2]
    step = max(256 // block, 1)
    for which, (left, right) in enumerate(((act, c_in), (n2_in, gh))):
        for at in range(0, grads.shape[0], step):
            part = rows_dot(left[:, at * block : (at + step) * block], right[...]).astype(BF)
            grads[at : at + step, which] = part.reshape(step, block, part.shape[1])


def feed(fsdp, micros, n2_pieces, c_pieces, vec, w_down, w_up):
    rows, model = c_pieces[0].shape
    hidden = w_down.shape[0]
    pair = jax.ShapeDtypeStruct((2, rows, model), BF)
    group = SEQ * rows
    return pl.pallas_call(
        functools.partial(feed_kernel, micros),
        in_specs=[ANY] * (2 * SEQ) + [VMEM] + [ANY] * 2,
        out_specs=[VMEM] * 6,
        out_shape=[pair] * 4
        + [
            jax.ShapeDtypeStruct((fsdp, 2, model // fsdp, model), BF),
            jax.ShapeDtypeStruct((16, model), F32),
        ],
        scratch_shapes=[
            pltpu.VMEM((model, hidden), BF),
            pltpu.VMEM((hidden, model), BF),
            pltpu.VMEM((group, model), BF),
            pltpu.VMEM((group, model), BF),
            pltpu.VMEM((group, hidden), BF),
            pltpu.VMEM((group, hidden), BF),
            pltpu.SemaphoreType.DMA((2,)),
            pltpu.SemaphoreType.DMA((SEQ * micros,)),
            pltpu.SemaphoreType.DMA((SEQ * micros,)),
        ],
        compiler_params=params(),
        cost_estimate=estimate(12 * group * model * hidden, 24 * 2**20),
        name="feed",
    )(*n2_pieces, *c_pieces, vec, w_down, w_up)


def middle_back_kernel(count, micros, info, *refs):
    chips, cames, fars = refs[:micros], refs[micros : 2 * micros], refs[2 * micros : 3 * micros]
    mid_ref, c_ref, vec, mine, other = refs[3 * micros : 3 * micros + 5]
    gm_ref, gb_ref, g0, g1, g2, g3, sums, weight, scratch, sem = refs[3 * micros + 5 :]
    copies = out_weight_copies(info, count, mine, other, weight, sem)
    for copy in copies:
        copy.start()
    grad_two = jnp.concatenate(
        [a[0].astype(F32) + b[0].astype(F32) + c[...].astype(F32) for a, b, c in zip(chips, cames, fars)],
        axis=0,
    )
    hat, scale = norm_parts(mid_ref[...])
    cot = c_ref[...].astype(F32)
    grad_middle = cot + norm_back(grad_two, hat, scale, vec[5:6, :])
    gm_ref[...] = grad_middle
    branch = grad_middle.astype(BF)
    gb_ref[...] = branch
    sums[...] = jnp.zeros(sums.shape, F32)
    sums[4:5, :] = column_sums(branch.astype(F32))
    sums[5:6, :] = column_sums(grad_two * hat)
    sums[6:7, :] = column_sums(grad_two)
    sums[7:8, :] = column_sums(cot)
    for copy in copies:
        copy.wait()
    scratch[...] = cols_dot(branch, weight[...]).astype(BF)
    width = g0.shape[1]
    for at, ref in enumerate((g0, g1, g2, g3)):
        place = info[count + 2 + at]
        ref[...] = scratch[:, pl.ds(pl.multiple_of(place * width, width), width)]


def middle_back(info, count, parts, middle, c_own, vec, mine, other):
    rows, model = middle.shape
    micros = len(parts)
    piece = jax.ShapeDtypeStruct((rows, model // SEQ), BF)
    return pl.pallas_call(
        functools.partial(middle_back_kernel, count, micros),
        in_specs=[SMEM] + [VMEM] * (3 * micros + 3) + [ANY] * 2,
        out_specs=[VMEM] * 7,
        out_shape=[
            jax.ShapeDtypeStruct((rows, model), F32),
            jax.ShapeDtypeStruct((rows, model), BF),
        ]
        + [piece] * 4
        + [jax.ShapeDtypeStruct((16, model), F32)],
        scratch_shapes=[
            pltpu.VMEM((model, model), BF),
            pltpu.VMEM((rows, model), BF),
            pltpu.SemaphoreType.DMA((2,)),
        ],
        compiler_params=params(),
        cost_estimate=estimate(2 * rows * model * model, 4 * 2**20),
        name="middle_back",
    )(info, *[p for at in range(3) for p in [part[at] for part in parts]], middle, c_own, vec, mine, other)


def attention_back_kernel(count, info, joined_ref, probs_ref, g0, g1, g2, g3, hat_ref, *refs):
    pieces, n1_ref = refs[:count], refs[count]
    more = len(refs) - count - 13
    extra = refs[count + 1 : count + 1 + more]
    keep, send, chip_ref, sib_ref = refs[count + 1 + more : count + 5 + more]
    sums, weight, sem, n1_in, n1_sem, grads, out, out_sem = refs[count + 5 + more :]
    image = pl.program_id(0)
    tokens = joined_ref.shape[2]
    rows = SEQ * tokens
    triple = joined_ref.shape[3]
    width = triple // 3
    model = weight.shape[0]
    copies = piece_copies(info, pieces, 0, weight, sem)
    n1_copy = pltpu.make_async_copy(n1_ref, n1_in, n1_sem)

    @pl.when(pl.program_id(0) == 0)
    def _():
        for copy in copies:
            copy.start()
        n1_copy.start()
        sums[...] = functools.reduce(jnp.add, [ref[...] for ref in extra])

    joined = joined_ref[...].reshape(rows, triple)
    grad = jnp.concatenate([g0[...], g1[...], g2[...], g3[...]], axis=0)
    queries, keys, values = [], [], []
    for head in range(width // HEAD_DIM):
        low = head * HEAD_DIM
        q = joined[:, low : low + HEAD_DIM] * jnp.asarray(SCALE, BF)
        k = joined[:, width + low : width + low + HEAD_DIM] * jnp.asarray(SCALE, BF)
        v = joined[:, 2 * width + low : 2 * width + low + HEAD_DIM]
        ga = grad[:, low : low + HEAD_DIM]
        probs = probs_ref[0, head]
        values.append(plain_dot(probs, ga).astype(BF))
        wide = probs.astype(F32)
        weighted = wide * cols_dot(v, ga)
        centre = jnp.sum(weighted, axis=0, keepdims=True)
        grad_scores = (weighted - wide * centre).astype(BF)
        keys.append(plain_dot(grad_scores, q).astype(BF))
        queries.append(rows_dot(k, grad_scores))
    grad_joined = jnp.concatenate(
        [jnp.concatenate(queries, axis=0).T.astype(BF)] + keys + values, axis=1
    )
    grads[:, image] = grad_joined.reshape(SEQ, tokens, triple)
    wide = grad_joined.astype(F32)
    place = pl.multiple_of(info[count] * width, width)
    sums[2:3, pl.ds(place, width)] += column_sums(wide[:, :width])
    sums[3:4, pl.ds(place, width)] += column_sums(wide[:, 2 * width :])

    @pl.when(pl.program_id(0) == 0)
    def _():
        for copy in copies:
            copy.wait()

    partial = cols_dot(grad_joined, weight[...])
    hat = hat_ref[...].reshape(rows, model).astype(F32)
    sums[0:1, :] += column_sums(partial * hat)
    sums[1:2, :] += column_sums(partial)
    low = partial.astype(BF)
    half = rows // 2
    chip_ref[...] = low[:half].reshape(chip_ref.shape)
    sib_ref[...] = low[half:].reshape(sib_ref.shape)

    @pl.when(image == pl.num_programs(0) - 1)
    def _():
        n1_copy.wait()
        right = grads[...].reshape(n1_in.shape[0], triple)
        total = jnp.concatenate([sums[...], jnp.zeros((LANES - sums.shape[0], model), F32)], axis=0)
        out[:, triple:] = total.T.astype(BF)
        tile = min(256, model)
        for at in range(0, model, tile):
            out[at : at + tile, :triple] = rows_dot(n1_in[:, at : at + tile], right).astype(BF)
        moves = digit_moves(info, out, keep, send, out_sem)
        for move in moves:
            move.start()
        for move in moves:
            move.wait()


def attention_back(info, joined, probs, grads, hat, pieces, n1, extra):
    count = len(pieces)
    _, images, tokens, triple = joined.shape
    model = hat.shape[3]
    width = triple // 3
    rows = SEQ * tokens
    heads = width // HEAD_DIM
    pair = jax.ShapeDtypeStruct((2, images, tokens, model), BF)
    group_block = lambda n, cols: pl.BlockSpec((n, 1, tokens, cols), lambda i: (0, i, 0, 0))
    part = jax.ShapeDtypeStruct((count // 2, model // count, triple + LANES), BF)
    return pl.pallas_call(
        functools.partial(attention_back_kernel, count),
        grid=(images,),
        in_specs=[
            SMEM,
            group_block(SEQ, triple),
            pl.BlockSpec((1, heads, rows, rows), lambda i: (i, 0, 0, 0)),
        ]
        + [pl.BlockSpec((tokens, width), lambda i: (i, 0))] * SEQ
        + [group_block(SEQ, model)]
        + [ANY] * (count + 1)
        + [pl.BlockSpec((16, model), lambda i: (0, 0))] * len(extra),
        out_specs=[ANY, ANY, group_block(2, model), group_block(2, model)],
        out_shape=[part, part, pair, pair],
        scratch_shapes=[
            pltpu.VMEM((16, model), F32),
            pltpu.VMEM((model, triple), BF),
            pltpu.SemaphoreType.DMA((count,)),
            pltpu.VMEM((images * rows, model), BF),
            pltpu.SemaphoreType.DMA,
            pltpu.VMEM((SEQ, images, tokens, triple), BF),
            pltpu.VMEM((model, triple + LANES), BF),
            pltpu.SemaphoreType.DMA((count,)),
        ],
        compiler_params=params(),
        cost_estimate=estimate(
            2 * images * rows * (2 * model * triple + 8 * width * rows), 12 * 2**20
        ),
        name="attention_back",
    )(info, joined, probs, *grads, hat, *pieces, n1, *extra)


def on_device(
    fsdp,
    inputs,
    keep_mask,
    cotangent,
    first_gain,
    first_shift,
    qkv_weight,
    query_bias,
    value_bias,
    out_weight,
    out_bias,
    second_gain,
    second_shift,
    up_weight,
    up_bias,
    down_weight,
    down_bias,
):
    micros, images, tokens, model = inputs.shape
    rows = images * tokens
    at_f, at_s = lax.axis_index("fsdp"), lax.axis_index("seq")
    depth = qkv_weight.shape[0]
    block = SEQ * depth
    width = model // SEQ
    triple = 3 * width
    half = model // 2
    unit_block = up_bias.shape[0]
    units = fsdp * unit_block
    core = at_s & 1
    micro_range = range(micros)
    info = jnp.stack(
        [jnp.asarray(v, jnp.int32) for v in fsdp_owners(fsdp, at_f)]
        + [at_s, core]
        + [at_s ^ mask for mask in ORDER]
    )

    vectors = jnp.stack(
        [
            first_gain,
            first_shift,
            query_bias,
            value_bias,
            out_bias,
            second_gain,
            second_shift,
            down_bias,
        ],
        axis=1,
    )
    vectors = jnp.pad(vectors, ((0, 0), (0, LANES - VECTORS)))
    to_send = pack(fsdp, qkv_weight, out_weight, vectors, up_weight)
    arrived = lax.all_to_all(to_send, "seq", 0, 0, tiled=True).reshape(block, -1)
    early = triple + LANES
    bias_column = jnp.pad(up_bias[:, None], ((0, 0), (VECTORS, LANES - VECTORS - 1)))
    first_group = jnp.concatenate(
        [
            arrived[:, :triple],
            arrived[:, triple:early] + bias_column,
            arrived[:, early : early + half],
        ],
        axis=1,
    )
    x_pieces = seq_gather(inputs.reshape(micros * rows, model))
    first_pieces = fsdp_gather(first_group, fsdp)
    w_down = lax.all_gather(down_weight, "fsdp", tiled=True)
    w_up = lax.all_gather(arrived[:, early + half :], "fsdp", tiled=True)

    x_own = inputs.reshape(micros * rows, model)
    c_own = cotangent.reshape(micros * rows, model)
    keep = keep_mask.reshape(micros * images, SEQ, tokens)
    keep = jnp.stack(
        [lax.dynamic_index_in_dim(keep, at_s ^ mask, 1, keepdims=False) for mask in ORDER], axis=1
    )
    n1, hat_one, joined, *heads_out, probs, vec = attention(
        info,
        [x.reshape(micros * images, tokens, model) for x in x_pieces],
        keep.reshape(micros * images, SEQ * tokens, 1),
        first_pieces,
        triple,
    )
    c_pieces = seq_gather(after(c_own, x_pieces[1]))
    heads_out[1:] = [after(h, c_pieces[1]) for h in heads_out[1:]]
    heads_in = seq_exchange(heads_out)
    out_mine = placed(info, first_pieces, early, half)
    out_other = hop(out_mine, 1)
    attended, middle, normed = middle_part(
        info, fsdp, heads_in, x_own, vec, out_mine, out_other
    )
    n2_pieces = seq_gather(normed)

    group_rows = micros * SEQ * rows
    down_chip, down_sib, up_chip, up_sib, feed_grad, part = feed(
        fsdp, micros, n2_pieces, c_pieces, vec, w_down, w_up
    )
    sums = [part]
    down_grad, up_grad = lax.psum_scatter(feed_grad, "fsdp", scatter_dimension=0, tiled=False)
    down_grad = down_grad.astype(F32)
    came, far = seq_scatter(up_chip, up_sib)
    two_parts = [(up_chip, came, hop(far, 2))]
    down_parts = [(down_chip, down_sib)]

    grad_middle, branch, *grads_out, part = middle_back(
        info, fsdp, two_parts, middle, c_own, vec, out_mine, out_other
    )
    sums.append(part)
    grads_in = seq_exchange(grads_out)
    out_here, out_there = core_grad(info, fsdp, attended, branch)
    down_sums = []
    for chip, sib in down_parts:
        came, far = seq_scatter(chip, after(sib, branch))
        down_sums.append((chip[0], came[0], far))
    out_sib = hop(out_there, 1)
    out_send = (out_here[1].astype(F32) + out_sib[1].astype(F32)).astype(BF)
    grads_in[0] = after(grads_in[0], *[far for _, _, far in down_sums], out_send)

    *qkv_blocks, chip, sib = attention_back(
        info,
        joined,
        probs,
        grads_in,
        hat_one,
        first_pieces,
        n1.reshape(group_rows, model),
        sums,
    )
    out_came = shift(out_send, fsdp, *digits_of(fsdp)[0], 1)
    sib, qkv_blocks[1] = after(sib, out_came), after(qkv_blocks[1], out_came)
    out_parts = scatter_far(scatter_near([out_here[0], out_sib[0], out_came], fsdp, at_f), fsdp, at_f)
    chip = chip.reshape(2, micros * rows, model)
    came, far = seq_scatter(chip, sib.reshape(2, micros * rows, model))
    grad_one = chip[0].astype(F32) + came[0].astype(F32) + hop(after(far, *out_parts[1:]), 2).astype(F32)

    [(a, b, c)] = down_sums
    total = a.astype(F32) + b.astype(F32) + hop(c, 2).astype(F32)
    layer_out = (middle + total + vec[7:8]).astype(BF).reshape(micros, images, tokens, model)
    hat, scale = norm_parts(x_own.astype(F32))
    input_grad = grad_middle + norm_back(grad_one, hat, scale, vec[0:1])
    input_grad = input_grad.astype(BF).reshape(micros, images, tokens, model)

    qkv_came = shift(qkv_blocks[1], fsdp, *digits_of(fsdp)[0], 1)
    qkv_parts = scatter_far(scatter_near([qkv_blocks[0], qkv_came], fsdp, at_f), fsdp, at_f)

    over_seq = lambda part: lax.all_to_all(part.reshape(SEQ, depth, -1), "seq", 0, 0, tiled=True)
    up_weight_grad = unpack_up(over_seq(up_grad))
    qkv_parts[0] = after(qkv_parts[0], up_weight_grad)
    last, own_vectors = collect(qkv_parts, out_parts)
    up_bias_grad = own_vectors[:, VECTORS]
    qkv_weight_grad, out_weight_grad, vector_grads = unpack(over_seq(last), model)
    vector_grads = vector_grads[:, :VECTORS].T

    return (
        layer_out,
        input_grad,
        vector_grads[0],
        vector_grads[1],
        qkv_weight_grad,
        vector_grads[2],
        vector_grads[3],
        out_weight_grad,
        vector_grads[4],
        vector_grads[5],
        vector_grads[6],
        up_weight_grad,
        up_bias_grad,
        down_grad,
        vector_grads[7],
    )


def solution(mesh):
    shard = P(BOTH)
    tokens = P(None, "fsdp", "seq", None)
    in_specs = (tokens, P(None, "fsdp", None), tokens) + (shard,) * 13
    out_specs = (tokens, tokens) + (shard,) * 13
    return jax.shard_map(
        functools.partial(on_device, mesh.shape["fsdp"]),
        mesh=mesh,
        in_specs=in_specs,
        out_specs=out_specs,
        check_vma=False,
    )
```

```python
import functools

import jax
import jax.numpy as jnp
from jax import lax
from jax.experimental import pallas as pl
from jax.experimental.pallas import tpu as pltpu
from jax.sharding import PartitionSpec as P

HEAD_DIM = 64
SEQ = 4
BF = jnp.bfloat16
F32 = jnp.float32
FILL = -1e30
LANES = 128
VECTORS = 8
SCALE = HEAD_DIM ** (-0.5)
BOTH = ("fsdp", "seq")
ORDER = (0, 2, 1, 3)
ANY = pl.BlockSpec(memory_space=pl.ANY)
SMEM = pl.BlockSpec(memory_space=pltpu.SMEM)
VMEM = pl.BlockSpec(memory_space=pltpu.VMEM)


def after(array, *done):
    return lax.optimization_barrier((array,) + done)[0] if done else array


def hop(array, mask):
    return lax.ppermute(array, "seq", [(i, i ^ mask) for i in range(SEQ)])


def seq_gather(array):
    far = hop(array, 2)
    return [array, far, hop(array, 1), hop(far, 1)]


def seq_gather(array, *done):
    far = hop(array, 2)
    return [array, far, hop(array, 1), hop(after(far, *done), 1)]


def seq_exchange(pieces):
    return [pieces[0]] + [hop(pieces[k], ORDER[k]) for k in (1, 2, 3)]


def seq_scatter(chip, sibling):
    came = hop(sibling, 1)
    return came, (chip[1].astype(F32) + came[1].astype(F32)).astype(BF)


def digits_of(size):
    digits, stride = [], 1
    while stride < size:
        radix = 2 if stride == 1 or size // stride < 4 else 4
        digits.append((stride, radix))
        stride *= radix
    return digits


def shift(array, size, stride, radix, step):
    pairs = []
    for i in range(size):
        digit = i // stride % radix
        pairs.append((i, i + ((digit + step) % radix - digit) * stride))
    return lax.ppermute(array, "fsdp", pairs)


def steps_of(radix):
    return [step for _, step in sorted((min(s, radix - s), s) for s in range(1, radix))]


def fsdp_owners(size, place):
    owners = [place]
    for stride, radix in reversed(digits_of(size)):
        digit = place // stride % radix
        changes = [((digit + radix - step) % radix - digit) * stride for step in steps_of(radix)]
        owners = owners + [o + change for change in changes for o in owners]
    return owners


def fsdp_gather(array, size):
    pieces = [array]
    for stride, radix in reversed(digits_of(size)):
        pieces = pieces + [
            shift(piece, size, stride, radix, step) for step in steps_of(radix) for piece in pieces
        ]
    return pieces


def split_kernel(count, radix, digit_ref, *refs):
    parts, outs = refs[:count], refs[count:]
    digit = digit_ref[0]
    for step, out in zip([0] + steps_of(radix), outs):
        at = lax.rem(digit + step, radix)
        out[0] = functools.reduce(jnp.add, [part[0, at].astype(F32) for part in parts]).astype(out.dtype)


def split_sum(parts, outer, radix, digit):
    rows, cols = parts[0].shape[1:]
    return pl.pallas_call(
        functools.partial(split_kernel, len(parts), radix),
        grid=(outer,),
        in_specs=[SMEM]
        + [pl.BlockSpec((1, radix, rows, cols), lambda i: (i, 0, 0, 0))] * len(parts),
        out_specs=[pl.BlockSpec((1, rows, cols), lambda i: (i, 0, 0))] * radix,
        out_shape=[jax.ShapeDtypeStruct((outer, rows, cols), BF)] * radix,
        compiler_params=params(),
        name="split",
    )(digit, *[part.reshape(outer, radix, rows, cols) for part in parts])


def scatter_near(parts, size, place):
    digits = digits_of(size)
    stride, radix = digits[1]
    digit = place // stride % radix
    outer = parts[0].shape[0] // radix
    return split_sum(parts, outer, radix, jnp.asarray(digit, jnp.int32).reshape(1))


def scatter_far(blocks, size, place):
    digits = digits_of(size)
    for at, (stride, radix) in enumerate(digits[1:]):
        parts = list(blocks[:1]) + [
            shift(block, size, stride, radix, step) for block, step in zip(blocks[1:], steps_of(radix))
        ]
        if at + 2 < len(digits):
            stride, radix = digits[at + 2]
            digit = place // stride % radix
            outer = parts[0].shape[0] // radix
            blocks = split_sum(parts, outer, radix, jnp.asarray(digit, jnp.int32).reshape(1))
    return parts


def rows_dot(left, right):
    return lax.dot_general(left, right, (((0,), (0,)), ((), ())), preferred_element_type=F32)


def cols_dot(left, right):
    return lax.dot_general(left, right, (((1,), (1,)), ((), ())), preferred_element_type=F32)


def plain_dot(left, right):
    return jnp.dot(left, right, preferred_element_type=F32)


def norm_parts(values):
    average = jnp.mean(values, axis=-1, keepdims=True)
    centred = values - average
    scale = lax.rsqrt(jnp.mean(centred * centred, axis=-1, keepdims=True) + 1e-06)
    return centred * scale, scale


def norm_back(grad, hat, scale, gain):
    spread = grad * gain
    return scale * (
        spread
        - jnp.mean(spread, axis=-1, keepdims=True)
        - hat * jnp.mean(spread * hat, axis=-1, keepdims=True)
    )


def column_sums(values):
    return jnp.sum(values, axis=0, keepdims=True)


def piece_copies(info, pieces, low, target, sem):
    block = pieces[0].shape[0]
    cols = target.shape[1]
    return [
        pltpu.make_async_copy(
            piece.at[:, pl.ds(low, cols)],
            target.at[pl.ds(pl.multiple_of(info[at] * block, block), block), :],
            sem.at[at],
        )
        for at, piece in enumerate(pieces)
    ]


def params():
    return pltpu.CompilerParams(vmem_limit_bytes=60 * 2**20)


def estimate(flops, moved):
    return pl.CostEstimate(flops=int(flops), bytes_accessed=int(moved), transcendentals=0)


def pack_kernel(fsdp, qkv, out, vectors, up, ref):
    width = qkv.shape[1] // 3 // SEQ
    half = out.shape[1] // 2
    block = up.shape[1] // SEQ // fsdp
    for s in range(SEQ):
        spans = [(qkv, (part * SEQ + s) * width, width) for part in range(3)]
        spans += [(vectors, 0, LANES), (out, (s % 2) * half, half)]
        spans += [(up, (f * SEQ + s) * block, block) for f in range(fsdp)]
        low = 0
        for source, start, cols in spans:
            ref[s, :, low : low + cols] = source[:, start : start + cols]
            low += cols


def pack(fsdp, qkv, out, vectors, up):
    depth = qkv.shape[0]
    cols = (qkv.shape[1] + up.shape[1]) // SEQ + LANES + out.shape[1] // 2
    return pl.pallas_call(
        functools.partial(pack_kernel, fsdp),
        in_specs=[VMEM] * 4,
        out_specs=VMEM,
        out_shape=jax.ShapeDtypeStruct((SEQ, depth, cols), BF),
        compiler_params=params(),
        name="pack",
    )(qkv, out, vectors, up)


def collect_kernel(counts, *refs):
    *parts, out, wide = refs
    low = at = 0
    for group, count in enumerate(counts):
        blocks = [part[...].reshape(part.shape[-2:]).astype(F32) for part in parts[at : at + count]]
        total = functools.reduce(jnp.add, blocks)
        out[:, low : low + total.shape[1]] = total.astype(BF)
        if group == 0:
            wide[...] = total[:, total.shape[1] - LANES :]
        low += total.shape[1]
        at += count


def collect(*groups):
    rows = groups[0][0].shape[-2]
    cols = sum(group[0].shape[-1] for group in groups)
    parts = [part for group in groups for part in group]
    return pl.pallas_call(
        functools.partial(collect_kernel, [len(group) for group in groups]),
        in_specs=[VMEM] * len(parts),
        out_specs=[VMEM] * 2,
        out_shape=[jax.ShapeDtypeStruct((rows, cols), BF), jax.ShapeDtypeStruct((rows, LANES), F32)],
        compiler_params=params(),
        name="collect",
    )(*parts)


def unpack_up_kernel(ref, up):
    block = ref.shape[1] * SEQ
    for s in range(SEQ):
        for part in range(ref.shape[2] // block):
            at = (part * SEQ + s) * block
            up[:, at : at + block] = ref[s, :, part * block : (part + 1) * block].astype(F32)


def unpack_up(came):
    return pl.pallas_call(
        unpack_up_kernel,
        in_specs=[VMEM],
        out_specs=VMEM,
        out_shape=jax.ShapeDtypeStruct((came.shape[1], SEQ * came.shape[2]), F32),
        compiler_params=params(),
        name="unpack_up",
    )(came)


def unpack_kernel(ref, qkv, out, vectors):
    width = qkv.shape[1] // 3 // SEQ
    half = out.shape[1] // 2
    low = 3 * width + LANES
    for s in range(SEQ):
        for part in range(3):
            at = (part * SEQ + s) * width
            qkv[:, at : at + width] = ref[s, :, part * width : (part + 1) * width].astype(F32)
    wide = lambda s, start, cols: ref[s, :, start : start + cols].astype(F32)
    vectors[...] = functools.reduce(jnp.add, [wide(s, 3 * width, LANES) for s in range(SEQ)])
    for core in range(2):
        out[:, core * half : (core + 1) * half] = wide(core, low, half) + wide(core + 2, low, half)


def unpack(came, model):
    depth = came.shape[1]
    return pl.pallas_call(
        unpack_kernel,
        in_specs=[VMEM],
        out_specs=[VMEM] * 3,
        out_shape=[jax.ShapeDtypeStruct((depth, n), F32) for n in (3 * model, model, LANES)],
        compiler_params=params(),
        name="unpack",
    )(came)


def place_kernel(count, low, info, *refs):
    pieces, out, scratch, sem = refs[:count], refs[count], refs[count + 1], refs[count + 2]
    copies = piece_copies(info, pieces, low, scratch, sem)
    for copy in copies:
        copy.start()
    for copy in copies:
        copy.wait()
    out[...] = scratch[...]


def placed(info, pieces, low, cols):
    count = len(pieces)
    rows = count * pieces[0].shape[0]
    return pl.pallas_call(
        functools.partial(place_kernel, count, low),
        in_specs=[SMEM] + [ANY] * count,
        out_specs=VMEM,
        out_shape=jax.ShapeDtypeStruct((rows, cols), BF),
        scratch_shapes=[pltpu.VMEM((rows, cols), BF), pltpu.SemaphoreType.DMA((count,))],
        compiler_params=params(),
        name="placed",
    )(info, *pieces)


def row_copies(sources, target, sem):
    copies, low = [], 0
    for at, source in enumerate(sources):
        rows = source.shape[0]
        copies.append(pltpu.make_async_copy(source, target.at[pl.ds(low, rows), :], sem.at[at]))
        low += rows
    return copies


def digit_moves(info, out, keep, send, sem):
    groups, block = keep.shape[:2]
    low_digit = info[0] % 2
    moves = []
    for at in range(groups):
        for which, (ref, side) in enumerate(((keep, low_digit), (send, 1 - low_digit))):
            start = pl.multiple_of((2 * at + side) * block, block)
            moves.append(
                pltpu.make_async_copy(out.at[pl.ds(start, block), :], ref.at[at], sem.at[2 * at + which])
            )
    return moves


def core_grad_kernel(core_at, info, left, right, here, there, product):
    groups, block, half = here.shape[1:]
    core, low_digit = info[core_at], info[0] % 2
    for ref, side in ((here, core), (there, 1 - core)):
        cols = pl.ds(pl.multiple_of(side * half, half), half)
        product[...] = rows_dot(left[...], right[:, cols]).astype(BF)
        for at in range(groups):
            for which, digit in enumerate((low_digit, 1 - low_digit)):
                start = pl.multiple_of((2 * at + digit) * block, block)
                ref[which, at] = product[pl.ds(start, block), :]


def core_grad(info, fsdp, left, right):
    rows, model = left.shape
    half = jax.ShapeDtypeStruct((2, fsdp // 2, model // fsdp, model // 2), BF)
    return pl.pallas_call(
        functools.partial(core_grad_kernel, fsdp + 1),
        in_specs=[SMEM] + [VMEM] * 2,
        out_specs=[VMEM] * 2,
        out_shape=[half] * 2,
        scratch_shapes=[pltpu.VMEM((model, model // 2), BF)],
        compiler_params=params(),
        cost_estimate=estimate(2 * rows * model * model, 4 * 2**20),
        name="core_grad",
    )(info, left, right)


def attention_kernel(count, info, x0, x1, x2, x3, keep_ref, *refs):
    pieces = refs[:count]
    n1_ref, hat_ref, joined_ref, e0, e1, e2, e3, probs_ref, vec, weight, sem = refs[count:]
    tokens, model = x0.shape[1:]
    rows = SEQ * tokens
    triple = weight.shape[1] - LANES
    width = triple // 3
    copies = piece_copies(info, pieces, 0, weight, sem)

    @pl.when(pl.program_id(0) == 0)
    def _():
        for copy in copies:
            copy.start()

    values = jnp.concatenate([x[0].astype(F32) for x in (x0, x1, x2, x3)], axis=0)
    hat, _ = norm_parts(values)
    hat_ref[...] = hat.astype(BF).reshape(hat_ref.shape)

    @pl.when(pl.program_id(0) == 0)
    def _():
        for copy in copies:
            copy.wait()
        vec[...] = weight[:, triple:].astype(F32).T[: vec.shape[0]]

    normed = (hat * vec[0:1, :] + vec[1:2, :]).astype(BF)
    n1_ref[...] = normed.reshape(n1_ref.shape)
    place = pl.multiple_of(info[count] * width, width)
    bias = jnp.concatenate(
        [
            vec[2:3, pl.ds(place, width)],
            jnp.zeros((1, width), F32),
            vec[3:4, pl.ds(place, width)],
        ],
        axis=1,
    )
    joined = (plain_dot(normed, weight[:, :triple]) + bias).astype(BF)
    joined_ref[...] = joined.reshape(joined_ref.shape)
    keep = keep_ref[0] > 0
    outs = []
    for head in range(width // HEAD_DIM):
        low = head * HEAD_DIM
        q = joined[:, low : low + HEAD_DIM] * jnp.asarray(SCALE, BF)
        k = joined[:, width + low : width + low + HEAD_DIM]
        v = joined[:, 2 * width + low : 2 * width + low + HEAD_DIM]
        scores = jnp.where(keep, cols_dot(k, q), FILL)
        mass = jnp.exp(scores - jnp.max(scores, axis=0, keepdims=True))
        probs = (mass * (1.0 / jnp.sum(mass, axis=0, keepdims=True))).astype(BF)
        probs_ref[0, head] = probs
        outs.append(rows_dot(v, probs))
    attended = jnp.concatenate(outs, axis=0).T.astype(BF)
    for at, ref in enumerate((e0, e1, e2, e3)):
        ref[...] = attended[at * tokens : (at + 1) * tokens]


def attention(info, x_pieces, keep, pieces, triple):
    images, tokens, model = x_pieces[0].shape
    count = len(pieces)
    width = triple // 3
    rows = SEQ * tokens
    heads = width // HEAD_DIM
    group_block = lambda cols: pl.BlockSpec((SEQ, 1, tokens, cols), lambda i: (0, i, 0, 0))
    group_shape = lambda cols: jax.ShapeDtypeStruct((SEQ, images, tokens, cols), BF)
    return pl.pallas_call(
        functools.partial(attention_kernel, count),
        grid=(images,),
        in_specs=[SMEM]
        + [pl.BlockSpec((1, tokens, model), lambda i: (i, 0, 0))] * SEQ
        + [pl.BlockSpec((1, rows, 1), lambda i: (i, 0, 0))]
        + [ANY] * count,
        out_specs=[group_block(model), group_block(model), group_block(triple)]
        + [pl.BlockSpec((tokens, width), lambda i: (i, 0))] * SEQ
        + [
            pl.BlockSpec((1, heads, rows, rows), lambda i: (i, 0, 0, 0)),
            pl.BlockSpec((16, model), lambda i: (0, 0)),
        ],
        out_shape=[group_shape(model), group_shape(model), group_shape(triple)]
        + [jax.ShapeDtypeStruct((images * tokens, width), BF)] * SEQ
        + [
            jax.ShapeDtypeStruct((images, heads, rows, rows), BF),
            jax.ShapeDtypeStruct((16, model), F32),
        ],
        scratch_shapes=[
            pltpu.VMEM((model, triple + LANES), BF),
            pltpu.SemaphoreType.DMA((count,)),
        ],
        compiler_params=params(),
        cost_estimate=estimate(
            2 * images * rows * (model * triple + 4 * width * rows), 16 * 2**20
        ),
        name="attention",
    )(info, *x_pieces, keep, *pieces)


def out_weight_copies(info, count, mine, other, target, sem):
    half = mine.shape[1]
    core = info[count + 1]
    return [
        pltpu.make_async_copy(
            source, target.at[:, pl.ds(pl.multiple_of(side * half, half), half)], sem.at[which]
        )
        for which, (source, side) in enumerate(((mine, core), (other, 1 - core)))
    ]


def middle_kernel(count, info, e0, e1, e2, e3, x_ref, vec, mine, other, att_ref, mid_ref, n2_ref, weight, sem):
    copies = out_weight_copies(info, count, mine, other, weight, sem)
    for copy in copies:
        copy.start()
    width = e0.shape[1]
    for at, ref in enumerate((e0, e1, e2, e3)):
        place = info[count + 2 + at]
        att_ref[:, pl.ds(pl.multiple_of(place * width, width), width)] = ref[...]
    for copy in copies:
        copy.wait()
    middle = x_ref[...].astype(F32) + plain_dot(att_ref[...], weight[...]) + vec[4:5, :]
    mid_ref[...] = middle
    hat, _ = norm_parts(middle)
    n2_ref[...] = (hat * vec[5:6, :] + vec[6:7, :]).astype(BF)


def middle_part(info, count, heads, x_own, vec, mine, other):
    rows, model = x_own.shape
    return pl.pallas_call(
        functools.partial(middle_kernel, count),
        in_specs=[SMEM] + [VMEM] * 6 + [ANY] * 2,
        out_specs=[VMEM] * 3,
        out_shape=[
            jax.ShapeDtypeStruct((rows, model), BF),
            jax.ShapeDtypeStruct((rows, model), F32),
            jax.ShapeDtypeStruct((rows, model), BF),
        ],
        scratch_shapes=[
            pltpu.VMEM((model, model), BF),
            pltpu.SemaphoreType.DMA((2,)),
        ],
        compiler_params=params(),
        cost_estimate=estimate(2 * rows * model * model, 4 * 2**20),
        name="middle",
    )(info, *heads, x_own, vec, mine, other)


def feed_kernel(micros, *refs):
    n2, cot = refs[:SEQ], refs[SEQ : 2 * SEQ]
    vec, down_ref, up_ref = refs[2 * SEQ : 2 * SEQ + 3]
    down_chip, down_sib, *ups, grads, sums = refs[2 * SEQ + 3 : 3 * SEQ + 7]
    w_up, w_down, n2_in, c_in, act, gh, weight_sem, n2_sem, c_sem = refs[3 * SEQ + 7 :]
    rows = n2[0].shape[0] // micros
    hidden = w_up.shape[1]
    up_copy = pltpu.make_async_copy(up_ref, w_up, weight_sem.at[0])
    down_copies = [pltpu.make_async_copy(down_ref, w_down, weight_sem.at[1])]
    by_micro = lambda pieces: [p.at[pl.ds(m * rows, rows), :] for m in range(micros) for p in pieces]
    n2_copies = row_copies(by_micro(n2), n2_in, n2_sem)
    c_copies = row_copies(by_micro(cot), c_in, c_sem)
    for copy in n2_copies + [up_copy] + c_copies + down_copies:
        copy.start()
    for copy in n2_copies + [up_copy]:
        copy.wait()
    total = jnp.zeros((1, hidden), F32)
    for micro in range(micros):
        span = slice(micro * SEQ * rows, (micro + 1) * SEQ * rows)
        values = plain_dot(n2_in[span], w_up[...]) + vec[8:9, :]
        normal = 0.5 * (1.0 + lax.erf(values * (2.0**-0.5)))
        slope = normal + values * (jnp.exp(values * values * -0.5) * 0.3989422804014327)
        active = (values * normal).astype(BF)
        act[span] = active
        if micro == 0:
            for copy in c_copies + down_copies:
                copy.wait()
        grad_hidden = (slope * cols_dot(c_in[span], w_down[...])).astype(BF)
        gh[span] = grad_hidden
        total = total + column_sums(grad_hidden.astype(F32))
        place = slice(micro * rows, (micro + 1) * rows)
        down_part = plain_dot(active, w_down[...]).astype(BF)
        up_part = cols_dot(grad_hidden, w_up[...]).astype(BF)
        for k in range(SEQ):
            (down_chip, down_sib)[k // 2][k % 2, place] = down_part[k * rows : (k + 1) * rows]
            ups[k][place] = up_part[k * rows : (k + 1) * rows]
    sums[...] = jnp.zeros(sums.shape, F32)
    sums[8:9, :] = total
    block = grads.shape[2]
    step = max(512 // block, 1)
    for which, (left, right) in enumerate(((act, c_in), (n2_in, gh))):
        for at in range(0, grads.shape[0], step):
            part = rows_dot(left[:, at * block : (at + step) * block], right[...]).astype(BF)
            grads[at : at + step, which] = part.reshape(step, block, part.shape[1])


def feed(fsdp, micros, n2_pieces, c_pieces, vec, w_down, w_up):
    rows, model = c_pieces[0].shape
    hidden = w_down.shape[0]
    pair = jax.ShapeDtypeStruct((2, rows, model), BF)
    group = SEQ * rows
    return pl.pallas_call(
        functools.partial(feed_kernel, micros),
        in_specs=[ANY] * (2 * SEQ) + [VMEM] + [ANY] * 2,
        out_specs=[VMEM] * (SEQ + 4),
        out_shape=[pair] * 2
        + [jax.ShapeDtypeStruct((rows, model), BF)] * SEQ
        + [
            jax.ShapeDtypeStruct((fsdp, 2, model // fsdp, model), BF),
            jax.ShapeDtypeStruct((16, model), F32),
        ],
        scratch_shapes=[
            pltpu.VMEM((model, hidden), BF),
            pltpu.VMEM((hidden, model), BF),
            pltpu.VMEM((group, model), BF),
            pltpu.VMEM((group, model), BF),
            pltpu.VMEM((group, hidden), BF),
            pltpu.VMEM((group, hidden), BF),
            pltpu.SemaphoreType.DMA((2,)),
            pltpu.SemaphoreType.DMA((SEQ * micros,)),
            pltpu.SemaphoreType.DMA((SEQ * micros,)),
        ],
        compiler_params=params(),
        cost_estimate=estimate(12 * group * model * hidden, 24 * 2**20),
        name="feed",
    )(*n2_pieces, *c_pieces, vec, w_down, w_up)


def middle_back_kernel(count, micros, info, *refs):
    chips, cames, fars = refs[:micros], refs[micros : 2 * micros], refs[2 * micros : 3 * micros]
    mid_ref, c_ref, vec, mine, other = refs[3 * micros : 3 * micros + 5]
    gm_ref, gb_ref, g0, g1, g2, g3, sums, weight, scratch, sem = refs[3 * micros + 5 :]
    copies = out_weight_copies(info, count, mine, other, weight, sem)
    for copy in copies:
        copy.start()
    grad_two = jnp.concatenate(
        [a[...].astype(F32) + b[...].astype(F32) + c[...].astype(F32) for a, b, c in zip(chips, cames, fars)],
        axis=0,
    )
    hat, scale = norm_parts(mid_ref[...])
    cot = c_ref[...].astype(F32)
    grad_middle = cot + norm_back(grad_two, hat, scale, vec[5:6, :])
    gm_ref[...] = grad_middle
    branch = grad_middle.astype(BF)
    gb_ref[...] = branch
    sums[...] = jnp.zeros(sums.shape, F32)
    sums[4:5, :] = column_sums(branch.astype(F32))
    sums[5:6, :] = column_sums(grad_two * hat)
    sums[6:7, :] = column_sums(grad_two)
    sums[7:8, :] = column_sums(cot)
    for copy in copies:
        copy.wait()
    scratch[...] = cols_dot(branch, weight[...]).astype(BF)
    width = g0.shape[1]
    for at, ref in enumerate((g0, g1, g2, g3)):
        place = info[count + 2 + at]
        ref[...] = scratch[:, pl.ds(pl.multiple_of(place * width, width), width)]


def middle_back(info, count, parts, middle, c_own, vec, mine, other):
    rows, model = middle.shape
    micros = len(parts)
    piece = jax.ShapeDtypeStruct((rows, model // SEQ), BF)
    return pl.pallas_call(
        functools.partial(middle_back_kernel, count, micros),
        in_specs=[SMEM] + [VMEM] * (3 * micros + 3) + [ANY] * 2,
        out_specs=[VMEM] * 7,
        out_shape=[
            jax.ShapeDtypeStruct((rows, model), F32),
            jax.ShapeDtypeStruct((rows, model), BF),
        ]
        + [piece] * 4
        + [jax.ShapeDtypeStruct((16, model), F32)],
        scratch_shapes=[
            pltpu.VMEM((model, model), BF),
            pltpu.VMEM((rows, model), BF),
            pltpu.SemaphoreType.DMA((2,)),
        ],
        compiler_params=params(),
        cost_estimate=estimate(2 * rows * model * model, 4 * 2**20),
        name="middle_back",
    )(info, *[p for at in range(3) for p in [part[at] for part in parts]], middle, c_own, vec, mine, other)


def attention_back_kernel(count, info, joined_ref, probs_ref, g0, g1, g2, g3, hat_ref, *refs):
    pieces, n1_ref = refs[:count], refs[count]
    more = len(refs) - count - 13
    extra = refs[count + 1 : count + 1 + more]
    keep, send, chip_ref, sib_ref = refs[count + 1 + more : count + 5 + more]
    sums, weight, sem, n1_in, n1_sem, grads, out, out_sem = refs[count + 5 + more :]
    image = pl.program_id(0)
    tokens = joined_ref.shape[2]
    rows = SEQ * tokens
    triple = joined_ref.shape[3]
    width = triple // 3
    model = weight.shape[0]
    copies = piece_copies(info, pieces, 0, weight, sem)
    n1_copy = pltpu.make_async_copy(n1_ref, n1_in, n1_sem)

    @pl.when(pl.program_id(0) == 0)
    def _():
        for copy in copies:
            copy.start()
        n1_copy.start()
        sums[...] = functools.reduce(jnp.add, [ref[...] for ref in extra])

    joined = joined_ref[...].reshape(rows, triple)
    grad = jnp.concatenate([g0[...], g1[...], g2[...], g3[...]], axis=0)
    queries, keys, values = [], [], []
    for head in range(width // HEAD_DIM):
        low = head * HEAD_DIM
        q = joined[:, low : low + HEAD_DIM] * jnp.asarray(SCALE, BF)
        k = joined[:, width + low : width + low + HEAD_DIM] * jnp.asarray(SCALE, BF)
        v = joined[:, 2 * width + low : 2 * width + low + HEAD_DIM]
        ga = grad[:, low : low + HEAD_DIM]
        probs = probs_ref[0, head]
        values.append(plain_dot(probs, ga).astype(BF))
        wide = probs.astype(F32)
        weighted = wide * cols_dot(v, ga)
        centre = jnp.sum(weighted, axis=0, keepdims=True)
        grad_scores = (weighted - wide * centre).astype(BF)
        keys.append(plain_dot(grad_scores, q).astype(BF))
        queries.append(rows_dot(k, grad_scores))
    grad_joined = jnp.concatenate(
        [jnp.concatenate(queries, axis=0).T.astype(BF)] + keys + values, axis=1
    )
    grads[:, image] = grad_joined.reshape(SEQ, tokens, triple)
    wide = grad_joined.astype(F32)
    place = pl.multiple_of(info[count] * width, width)
    sums[2:3, pl.ds(place, width)] += column_sums(wide[:, :width])
    sums[3:4, pl.ds(place, width)] += column_sums(wide[:, 2 * width :])

    @pl.when(pl.program_id(0) == 0)
    def _():
        for copy in copies:
            copy.wait()

    partial = cols_dot(grad_joined, weight[...])
    hat = hat_ref[...].reshape(rows, model).astype(F32)
    sums[0:1, :] += column_sums(partial * hat)
    sums[1:2, :] += column_sums(partial)
    low = partial.astype(BF)
    half = rows // 2
    chip_ref[...] = low[:half].reshape(chip_ref.shape)
    sib_ref[...] = low[half:].reshape(sib_ref.shape)

    @pl.when(image == pl.num_programs(0) - 1)
    def _():
        n1_copy.wait()
        right = grads[...].reshape(n1_in.shape[0], triple)
        total = jnp.concatenate([sums[...], jnp.zeros((LANES - sums.shape[0], model), F32)], axis=0)
        out[:, triple:] = total.T.astype(BF)
        tile = min(512, model)
        for at in range(0, model, tile):
            out[at : at + tile, :triple] = rows_dot(n1_in[:, at : at + tile], right).astype(BF)
        moves = digit_moves(info, out, keep, send, out_sem)
        for move in moves:
            move.start()
        for move in moves:
            move.wait()


def attention_back(info, joined, probs, grads, hat, pieces, n1, extra):
    count = len(pieces)
    _, images, tokens, triple = joined.shape
    model = hat.shape[3]
    width = triple // 3
    rows = SEQ * tokens
    heads = width // HEAD_DIM
    pair = jax.ShapeDtypeStruct((2, images, tokens, model), BF)
    group_block = lambda n, cols: pl.BlockSpec((n, 1, tokens, cols), lambda i: (0, i, 0, 0))
    part = jax.ShapeDtypeStruct((count // 2, model // count, triple + LANES), BF)
    return pl.pallas_call(
        functools.partial(attention_back_kernel, count),
        grid=(images,),
        in_specs=[
            SMEM,
            group_block(SEQ, triple),
            pl.BlockSpec((1, heads, rows, rows), lambda i: (i, 0, 0, 0)),
        ]
        + [pl.BlockSpec((tokens, width), lambda i: (i, 0))] * SEQ
        + [group_block(SEQ, model)]
        + [ANY] * (count + 1)
        + [pl.BlockSpec((16, model), lambda i: (0, 0))] * len(extra),
        out_specs=[ANY, ANY, group_block(2, model), group_block(2, model)],
        out_shape=[part, part, pair, pair],
        scratch_shapes=[
            pltpu.VMEM((16, model), F32),
            pltpu.VMEM((model, triple), BF),
            pltpu.SemaphoreType.DMA((count,)),
            pltpu.VMEM((images * rows, model), BF),
            pltpu.SemaphoreType.DMA,
            pltpu.VMEM((SEQ, images, tokens, triple), BF),
            pltpu.VMEM((model, triple + LANES), BF),
            pltpu.SemaphoreType.DMA((count,)),
        ],
        compiler_params=params(),
        cost_estimate=estimate(
            2 * images * rows * (2 * model * triple + 8 * width * rows), 12 * 2**20
        ),
        name="attention_back",
    )(info, joined, probs, *grads, hat, *pieces, n1, *extra)


def on_device(
    fsdp,
    inputs,
    keep_mask,
    cotangent,
    first_gain,
    first_shift,
    qkv_weight,
    query_bias,
    value_bias,
    out_weight,
    out_bias,
    second_gain,
    second_shift,
    up_weight,
    up_bias,
    down_weight,
    down_bias,
):
    micros, images, tokens, model = inputs.shape
    rows = images * tokens
    at_f, at_s = lax.axis_index("fsdp"), lax.axis_index("seq")
    depth = qkv_weight.shape[0]
    block = SEQ * depth
    width = model // SEQ
    triple = 3 * width
    half = model // 2
    unit_block = up_bias.shape[0]
    units = fsdp * unit_block
    core = at_s & 1
    micro_range = range(micros)
    info = jnp.stack(
        [jnp.asarray(v, jnp.int32) for v in fsdp_owners(fsdp, at_f)]
        + [at_s, core]
        + [at_s ^ mask for mask in ORDER]
    )

    vectors = jnp.stack(
        [
            first_gain,
            first_shift,
            query_bias,
            value_bias,
            out_bias,
            second_gain,
            second_shift,
            down_bias,
        ],
        axis=1,
    )
    vectors = jnp.pad(vectors, ((0, 0), (0, LANES - VECTORS)))
    to_send = pack(fsdp, qkv_weight, out_weight, vectors, up_weight)
    arrived = lax.all_to_all(to_send, "seq", 0, 0, tiled=True).reshape(block, -1)
    early = triple + LANES
    bias_column = jnp.pad(up_bias[:, None], ((0, 0), (VECTORS, LANES - VECTORS - 1)))
    first_group = jnp.concatenate(
        [
            arrived[:, :triple],
            arrived[:, triple:early] + bias_column,
            arrived[:, early : early + half],
        ],
        axis=1,
    )
    x_pieces = seq_gather(inputs.reshape(micros * rows, model))
    first_pieces = fsdp_gather(first_group, fsdp)
    w_down = lax.all_gather(down_weight, "fsdp", tiled=True)
    w_up = lax.all_gather(arrived[:, early + half :], "fsdp", tiled=True)

    x_own = inputs.reshape(micros * rows, model)
    c_own = cotangent.reshape(micros * rows, model)
    keep = keep_mask.reshape(micros * images, SEQ, tokens)
    keep = jnp.stack(
        [lax.dynamic_index_in_dim(keep, at_s ^ mask, 1, keepdims=False) for mask in ORDER], axis=1
    )
    n1, hat_one, joined, *heads_out, probs, vec = attention(
        info,
        [x.reshape(micros * images, tokens, model) for x in x_pieces],
        keep.reshape(micros * images, SEQ * tokens, 1),
        first_pieces,
        triple,
    )
    c_pieces = seq_gather(after(c_own, x_pieces[1]))
    heads_out[1:] = [after(h, c_pieces[1]) for h in heads_out[1:]]
    heads_in = seq_exchange(heads_out)
    out_mine = placed(info, first_pieces, early, half)
    out_other = hop(out_mine, 1)
    attended, middle, normed = middle_part(
        info, fsdp, heads_in, x_own, vec, out_mine, out_other
    )
    n2_pieces = seq_gather(normed)

    group_rows = micros * SEQ * rows
    down_chip, down_sib, *ups, feed_grad, part = feed(
        fsdp, micros, n2_pieces, c_pieces, vec, w_down, w_up
    )
    sums = [part]
    down_grad, up_grad = lax.psum_scatter(feed_grad, "fsdp", scatter_dimension=0, tiled=False)
    down_grad = down_grad.astype(F32)
    up_far = (ups[1].astype(F32) + hop(ups[3], 1).astype(F32)).astype(BF)
    two_parts = [(ups[0], hop(ups[2], 1), hop(up_far, 2))]
    down_parts = [(down_chip, down_sib)]

    grad_middle, branch, *grads_out, part = middle_back(
        info, fsdp, two_parts, middle, c_own, vec, out_mine, out_other
    )
    sums.append(part)
    grads_in = seq_exchange(grads_out)
    out_here, out_there = core_grad(info, fsdp, attended, branch)
    down_sums = []
    for chip, sib in down_parts:
        came, far = seq_scatter(chip, after(sib, branch))
        down_sums.append((chip[0], came[0], far))
    out_sib = hop(out_there, 1)
    out_send = (out_here[1].astype(F32) + out_sib[1].astype(F32)).astype(BF)
    grads_in[0] = after(grads_in[0], *[far for _, _, far in down_sums], out_send)

    *qkv_blocks, chip, sib = attention_back(
        info,
        joined,
        probs,
        grads_in,
        hat_one,
        first_pieces,
        n1.reshape(group_rows, model),
        sums,
    )
    out_came = shift(out_send, fsdp, *digits_of(fsdp)[0], 1)
    sib, qkv_blocks[1] = after(sib, out_came), after(qkv_blocks[1], out_came)
    out_parts = scatter_far(scatter_near([out_here[0], out_sib[0], out_came], fsdp, at_f), fsdp, at_f)
    chip = chip.reshape(2, micros * rows, model)
    came, far = seq_scatter(chip, sib.reshape(2, micros * rows, model))
    grad_one = chip[0].astype(F32) + came[0].astype(F32) + hop(after(far, *out_parts[1:]), 2).astype(F32)

    [(a, b, c)] = down_sums
    total = a.astype(F32) + b.astype(F32) + hop(c, 2).astype(F32)
    layer_out = (middle + total + vec[7:8]).astype(BF).reshape(micros, images, tokens, model)
    hat, scale = norm_parts(x_own.astype(F32))
    input_grad = grad_middle + norm_back(grad_one, hat, scale, vec[0:1])
    input_grad = input_grad.astype(BF).reshape(micros, images, tokens, model)

    qkv_came = shift(qkv_blocks[1], fsdp, *digits_of(fsdp)[0], 1)
    qkv_parts = scatter_far(scatter_near([qkv_blocks[0], qkv_came], fsdp, at_f), fsdp, at_f)

    over_seq = lambda part: lax.all_to_all(part.reshape(SEQ, depth, -1), "seq", 0, 0, tiled=True)
    up_weight_grad = unpack_up(over_seq(up_grad))
    qkv_parts[0] = after(qkv_parts[0], up_weight_grad)
    last, own_vectors = collect(qkv_parts, out_parts)
    up_bias_grad = own_vectors[:, VECTORS]
    qkv_weight_grad, out_weight_grad, vector_grads = unpack(over_seq(last), model)
    vector_grads = vector_grads[:, :VECTORS].T

    return (
        layer_out,
        input_grad,
        vector_grads[0],
        vector_grads[1],
        qkv_weight_grad,
        vector_grads[2],
        vector_grads[3],
        out_weight_grad,
        vector_grads[4],
        vector_grads[5],
        vector_grads[6],
        up_weight_grad,
        up_bias_grad,
        down_grad,
        vector_grads[7],
    )


def solution(mesh):
    shard = P(BOTH)
    tokens = P(None, "fsdp", "seq", None)
    in_specs = (tokens, P(None, "fsdp", None), tokens) + (shard,) * 13
    out_specs = (tokens, tokens) + (shard,) * 13
    return jax.shard_map(
        functools.partial(on_device, mesh.shape["fsdp"]),
        mesh=mesh,
        in_specs=in_specs,
        out_specs=out_specs,
        check_vma=False,
    )
```

```python
import functools

import jax
import jax.numpy as jnp
from jax import lax
from jax.experimental import pallas as pl
from jax.experimental.pallas import tpu as pltpu
from jax.sharding import PartitionSpec as P

HEAD_DIM = 64
SEQ = 4
BF = jnp.bfloat16
F32 = jnp.float32
FILL = -1e30
LANES = 128
VECTORS = 8
SCALE = HEAD_DIM ** (-0.5)
BOTH = ("fsdp", "seq")
ORDER = (0, 2, 1, 3)
ANY = pl.BlockSpec(memory_space=pl.ANY)
SMEM = pl.BlockSpec(memory_space=pltpu.SMEM)
VMEM = pl.BlockSpec(memory_space=pltpu.VMEM)


def after(array, *done):
    return lax.optimization_barrier((array,) + done)[0] if done else array


def hop(array, mask):
    return lax.ppermute(array, "seq", [(i, i ^ mask) for i in range(SEQ)])


def seq_gather(array):
    far = hop(array, 2)
    return [array, far, hop(array, 1), hop(far, 1)]


def seq_gather(array, *done):
    far = hop(array, 2)
    return [array, far, hop(array, 1), hop(after(far, *done), 1)]


def seq_exchange(pieces):
    return [pieces[0]] + [hop(pieces[k], ORDER[k]) for k in (1, 2, 3)]


def seq_scatter(chip, sibling):
    came = hop(sibling, 1)
    return came, (chip[1].astype(F32) + came[1].astype(F32)).astype(BF)


def digits_of(size):
    digits, stride = [], 1
    while stride < size:
        radix = 2 if stride == 1 or size // stride < 4 else 4
        digits.append((stride, radix))
        stride *= radix
    return digits


def shift(array, size, stride, radix, step):
    pairs = []
    for i in range(size):
        digit = i // stride % radix
        pairs.append((i, i + ((digit + step) % radix - digit) * stride))
    return lax.ppermute(array, "fsdp", pairs)


def steps_of(radix):
    return [step for _, step in sorted((min(s, radix - s), s) for s in range(1, radix))]


def fsdp_owners(size, place):
    owners = [place]
    for stride, radix in reversed(digits_of(size)):
        digit = place // stride % radix
        changes = [((digit + radix - step) % radix - digit) * stride for step in steps_of(radix)]
        owners = owners + [o + change for change in changes for o in owners]
    return owners


def fsdp_gather(array, size):
    pieces = [array]
    for stride, radix in reversed(digits_of(size)):
        pieces = pieces + [
            shift(piece, size, stride, radix, step) for step in steps_of(radix) for piece in pieces
        ]
    return pieces


def split_kernel(count, radix, digit_ref, *refs):
    parts, outs = refs[:count], refs[count:]
    digit = digit_ref[0]
    for step, out in zip([0] + steps_of(radix), outs):
        at = lax.rem(digit + step, radix)
        out[0] = functools.reduce(jnp.add, [part[0, at].astype(F32) for part in parts]).astype(out.dtype)


def split_sum(parts, outer, radix, digit):
    rows, cols = parts[0].shape[1:]
    return pl.pallas_call(
        functools.partial(split_kernel, len(parts), radix),
        grid=(outer,),
        in_specs=[SMEM]
        + [pl.BlockSpec((1, radix, rows, cols), lambda i: (i, 0, 0, 0))] * len(parts),
        out_specs=[pl.BlockSpec((1, rows, cols), lambda i: (i, 0, 0))] * radix,
        out_shape=[jax.ShapeDtypeStruct((outer, rows, cols), BF)] * radix,
        compiler_params=params(),
        name="split",
    )(digit, *[part.reshape(outer, radix, rows, cols) for part in parts])


def scatter_near(parts, size, place):
    digits = digits_of(size)
    stride, radix = digits[1]
    digit = place // stride % radix
    outer = parts[0].shape[0] // radix
    return split_sum(parts, outer, radix, jnp.asarray(digit, jnp.int32).reshape(1))


def scatter_far(blocks, size, place):
    digits = digits_of(size)
    for at, (stride, radix) in enumerate(digits[1:]):
        parts = list(blocks[:1]) + [
            shift(block, size, stride, radix, step) for block, step in zip(blocks[1:], steps_of(radix))
        ]
        if at + 2 < len(digits):
            stride, radix = digits[at + 2]
            digit = place // stride % radix
            outer = parts[0].shape[0] // radix
            blocks = split_sum(parts, outer, radix, jnp.asarray(digit, jnp.int32).reshape(1))
    return parts


def rows_dot(left, right):
    return lax.dot_general(left, right, (((0,), (0,)), ((), ())), preferred_element_type=F32)


def cols_dot(left, right):
    return lax.dot_general(left, right, (((1,), (1,)), ((), ())), preferred_element_type=F32)


def plain_dot(left, right):
    return jnp.dot(left, right, preferred_element_type=F32)


def norm_parts(values):
    average = jnp.mean(values, axis=-1, keepdims=True)
    centred = values - average
    scale = lax.rsqrt(jnp.mean(centred * centred, axis=-1, keepdims=True) + 1e-06)
    return centred * scale, scale


def norm_back(grad, hat, scale, gain):
    spread = grad * gain
    return scale * (
        spread
        - jnp.mean(spread, axis=-1, keepdims=True)
        - hat * jnp.mean(spread * hat, axis=-1, keepdims=True)
    )


def column_sums(values):
    return jnp.sum(values, axis=0, keepdims=True)


def piece_copies(info, pieces, low, target, sem):
    block = pieces[0].shape[0]
    cols = target.shape[1]
    return [
        pltpu.make_async_copy(
            piece.at[:, pl.ds(low, cols)],
            target.at[pl.ds(pl.multiple_of(info[at] * block, block), block), :],
            sem.at[at],
        )
        for at, piece in enumerate(pieces)
    ]


def params():
    return pltpu.CompilerParams(vmem_limit_bytes=60 * 2**20)


def estimate(flops, moved):
    return pl.CostEstimate(flops=int(flops), bytes_accessed=int(moved), transcendentals=0)


def pack_kernel(fsdp, qkv, out, vectors, up, ref):
    width = qkv.shape[1] // 3 // SEQ
    half = out.shape[1] // 2
    block = up.shape[1] // SEQ // fsdp
    for s in range(SEQ):
        spans = [(qkv, (part * SEQ + s) * width, width) for part in range(3)]
        spans += [(vectors, 0, LANES), (out, (s % 2) * half, half)]
        spans += [(up, (f * SEQ + s) * block, block) for f in range(fsdp)]
        low = 0
        for source, start, cols in spans:
            ref[s, :, low : low + cols] = source[:, start : start + cols]
            low += cols


def pack(fsdp, qkv, out, vectors, up):
    depth = qkv.shape[0]
    cols = (qkv.shape[1] + up.shape[1]) // SEQ + LANES + out.shape[1] // 2
    return pl.pallas_call(
        functools.partial(pack_kernel, fsdp),
        in_specs=[VMEM] * 4,
        out_specs=VMEM,
        out_shape=jax.ShapeDtypeStruct((SEQ, depth, cols), BF),
        compiler_params=params(),
        name="pack",
    )(qkv, out, vectors, up)


def collect_kernel(counts, *refs):
    *parts, out, wide = refs
    low = at = 0
    for group, count in enumerate(counts):
        blocks = [part[...].reshape(part.shape[-2:]).astype(F32) for part in parts[at : at + count]]
        total = functools.reduce(jnp.add, blocks)
        out[:, low : low + total.shape[1]] = total.astype(BF)
        if group == 0:
            wide[...] = total[:, total.shape[1] - LANES :]
        low += total.shape[1]
        at += count


def collect(*groups):
    rows = groups[0][0].shape[-2]
    cols = sum(group[0].shape[-1] for group in groups)
    parts = [part for group in groups for part in group]
    return pl.pallas_call(
        functools.partial(collect_kernel, [len(group) for group in groups]),
        in_specs=[VMEM] * len(parts),
        out_specs=[VMEM] * 2,
        out_shape=[jax.ShapeDtypeStruct((rows, cols), BF), jax.ShapeDtypeStruct((rows, LANES), F32)],
        compiler_params=params(),
        name="collect",
    )(*parts)


def unpack_up_kernel(ref, up):
    block = ref.shape[1] * SEQ
    for s in range(SEQ):
        for part in range(ref.shape[2] // block):
            at = (part * SEQ + s) * block
            up[:, at : at + block] = ref[s, :, part * block : (part + 1) * block].astype(F32)


def unpack_up(came):
    return pl.pallas_call(
        unpack_up_kernel,
        in_specs=[VMEM],
        out_specs=VMEM,
        out_shape=jax.ShapeDtypeStruct((came.shape[1], SEQ * came.shape[2]), F32),
        compiler_params=params(),
        name="unpack_up",
    )(came)


def unpack_kernel(ref, qkv, out, vectors):
    width = qkv.shape[1] // 3 // SEQ
    half = out.shape[1] // 2
    low = 3 * width + LANES
    for s in range(SEQ):
        for part in range(3):
            at = (part * SEQ + s) * width
            qkv[:, at : at + width] = ref[s, :, part * width : (part + 1) * width].astype(F32)
    wide = lambda s, start, cols: ref[s, :, start : start + cols].astype(F32)
    vectors[...] = functools.reduce(jnp.add, [wide(s, 3 * width, LANES) for s in range(SEQ)])
    for core in range(2):
        out[:, core * half : (core + 1) * half] = wide(core, low, half) + wide(core + 2, low, half)


def unpack(came, model):
    depth = came.shape[1]
    return pl.pallas_call(
        unpack_kernel,
        in_specs=[VMEM],
        out_specs=[VMEM] * 3,
        out_shape=[jax.ShapeDtypeStruct((depth, n), F32) for n in (3 * model, model, LANES)],
        compiler_params=params(),
        name="unpack",
    )(came)


def place_kernel(count, low, info, *refs):
    pieces, out, scratch, sem = refs[:count], refs[count], refs[count + 1], refs[count + 2]
    copies = piece_copies(info, pieces, low, scratch, sem)
    for copy in copies:
        copy.start()
    for copy in copies:
        copy.wait()
    out[...] = scratch[...]


def placed(info, pieces, low, cols):
    count = len(pieces)
    rows = count * pieces[0].shape[0]
    return pl.pallas_call(
        functools.partial(place_kernel, count, low),
        in_specs=[SMEM] + [ANY] * count,
        out_specs=VMEM,
        out_shape=jax.ShapeDtypeStruct((rows, cols), BF),
        scratch_shapes=[pltpu.VMEM((rows, cols), BF), pltpu.SemaphoreType.DMA((count,))],
        compiler_params=params(),
        name="placed",
    )(info, *pieces)


def row_copies(sources, target, sem):
    copies, low = [], 0
    for at, source in enumerate(sources):
        rows = source.shape[0]
        copies.append(pltpu.make_async_copy(source, target.at[pl.ds(low, rows), :], sem.at[at]))
        low += rows
    return copies


def digit_moves(info, out, keep, send, sem):
    groups, block = keep.shape[:2]
    low_digit = info[0] % 2
    moves = []
    for at in range(groups):
        for which, (ref, side) in enumerate(((keep, low_digit), (send, 1 - low_digit))):
            start = pl.multiple_of((2 * at + side) * block, block)
            moves.append(
                pltpu.make_async_copy(out.at[pl.ds(start, block), :], ref.at[at], sem.at[2 * at + which])
            )
    return moves


def core_grad_kernel(core_at, info, left, right, here, there, product):
    groups, block, half = here.shape[1:]
    core, low_digit = info[core_at], info[0] % 2
    for ref, side in ((here, core), (there, 1 - core)):
        cols = pl.ds(pl.multiple_of(side * half, half), half)
        product[...] = rows_dot(left[...], right[:, cols]).astype(BF)
        for at in range(groups):
            for which, digit in enumerate((low_digit, 1 - low_digit)):
                start = pl.multiple_of((2 * at + digit) * block, block)
                ref[which, at] = product[pl.ds(start, block), :]


def core_grad(info, fsdp, left, right):
    rows, model = left.shape
    half = jax.ShapeDtypeStruct((2, fsdp // 2, model // fsdp, model // 2), BF)
    return pl.pallas_call(
        functools.partial(core_grad_kernel, fsdp + 1),
        in_specs=[SMEM] + [VMEM] * 2,
        out_specs=[VMEM] * 2,
        out_shape=[half] * 2,
        scratch_shapes=[pltpu.VMEM((model, model // 2), BF)],
        compiler_params=params(),
        cost_estimate=estimate(2 * rows * model * model, 4 * 2**20),
        name="core_grad",
    )(info, left, right)


def attention_kernel(count, info, x0, x1, x2, x3, keep_ref, *refs):
    pieces = refs[:count]
    n1_ref, hat_ref, joined_ref, e0, e1, e2, e3, probs_ref, vec, weight, sem = refs[count:]
    tokens, model = x0.shape[1:]
    rows = SEQ * tokens
    triple = weight.shape[1] - LANES
    width = triple // 3
    copies = piece_copies(info, pieces, 0, weight, sem)

    @pl.when(pl.program_id(0) == 0)
    def _():
        for copy in copies:
            copy.start()

    values = jnp.concatenate([x[0].astype(F32) for x in (x0, x1, x2, x3)], axis=0)
    hat, _ = norm_parts(values)
    hat_ref[...] = hat.astype(BF).reshape(hat_ref.shape)

    @pl.when(pl.program_id(0) == 0)
    def _():
        for copy in copies:
            copy.wait()
        vec[...] = weight[:, triple:].astype(F32).T[: vec.shape[0]]

    normed = (hat * vec[0:1, :] + vec[1:2, :]).astype(BF)
    n1_ref[...] = normed.reshape(n1_ref.shape)
    place = pl.multiple_of(info[count] * width, width)
    bias = jnp.concatenate(
        [
            vec[2:3, pl.ds(place, width)],
            jnp.zeros((1, width), F32),
            vec[3:4, pl.ds(place, width)],
        ],
        axis=1,
    )
    joined = (plain_dot(normed, weight[:, :triple]) + bias).astype(BF)
    joined_ref[...] = joined.reshape(joined_ref.shape)
    keep = jnp.broadcast_to(keep_ref[0], (8, rows)).T[:, :1] > 0
    outs = []
    for head in range(width // HEAD_DIM):
        low = head * HEAD_DIM
        q = joined[:, low : low + HEAD_DIM] * jnp.asarray(SCALE, BF)
        k = joined[:, width + low : width + low + HEAD_DIM]
        v = joined[:, 2 * width + low : 2 * width + low + HEAD_DIM]
        scores = jnp.where(keep, cols_dot(k, q), FILL)
        mass = jnp.exp(scores - jnp.max(scores, axis=0, keepdims=True))
        probs = (mass * (1.0 / jnp.sum(mass, axis=0, keepdims=True))).astype(BF)
        probs_ref[0, head] = probs
        outs.append(rows_dot(v, probs))
    attended = jnp.concatenate(outs, axis=0).T.astype(BF)
    for at, ref in enumerate((e0, e1, e2, e3)):
        ref[...] = attended[at * tokens : (at + 1) * tokens]


def attention(info, x_pieces, keep, pieces, triple):
    images, tokens, model = x_pieces[0].shape
    count = len(pieces)
    width = triple // 3
    rows = SEQ * tokens
    heads = width // HEAD_DIM
    group_block = lambda cols: pl.BlockSpec((SEQ, 1, tokens, cols), lambda i: (0, i, 0, 0))
    group_shape = lambda cols: jax.ShapeDtypeStruct((SEQ, images, tokens, cols), BF)
    return pl.pallas_call(
        functools.partial(attention_kernel, count),
        grid=(images,),
        in_specs=[SMEM]
        + [pl.BlockSpec((1, tokens, model), lambda i: (i, 0, 0))] * SEQ
        + [pl.BlockSpec((1, 1, rows), lambda i: (i, 0, 0))]
        + [ANY] * count,
        out_specs=[group_block(model), group_block(model), group_block(triple)]
        + [pl.BlockSpec((tokens, width), lambda i: (i, 0))] * SEQ
        + [
            pl.BlockSpec((1, heads, rows, rows), lambda i: (i, 0, 0, 0)),
            pl.BlockSpec((16, model), lambda i: (0, 0)),
        ],
        out_shape=[group_shape(model), group_shape(model), group_shape(triple)]
        + [jax.ShapeDtypeStruct((images * tokens, width), BF)] * SEQ
        + [
            jax.ShapeDtypeStruct((images, heads, rows, rows), BF),
            jax.ShapeDtypeStruct((16, model), F32),
        ],
        scratch_shapes=[
            pltpu.VMEM((model, triple + LANES), BF),
            pltpu.SemaphoreType.DMA((count,)),
        ],
        compiler_params=params(),
        cost_estimate=estimate(
            2 * images * rows * (model * triple + 4 * width * rows), 16 * 2**20
        ),
        name="attention",
    )(info, *x_pieces, keep, *pieces)


def out_weight_copies(info, count, mine, other, target, sem):
    half = mine.shape[1]
    core = info[count + 1]
    return [
        pltpu.make_async_copy(
            source, target.at[:, pl.ds(pl.multiple_of(side * half, half), half)], sem.at[which]
        )
        for which, (source, side) in enumerate(((mine, core), (other, 1 - core)))
    ]


def middle_kernel(count, info, e0, e1, e2, e3, x_ref, vec, mine, other, att_ref, mid_ref, n2_ref, weight, sem):
    copies = out_weight_copies(info, count, mine, other, weight, sem)
    for copy in copies:
        copy.start()
    width = e0.shape[1]
    for at, ref in enumerate((e0, e1, e2, e3)):
        place = info[count + 2 + at]
        att_ref[:, pl.ds(pl.multiple_of(place * width, width), width)] = ref[...]
    for copy in copies:
        copy.wait()
    middle = x_ref[...].astype(F32) + plain_dot(att_ref[...], weight[...]) + vec[4:5, :]
    mid_ref[...] = middle
    hat, _ = norm_parts(middle)
    n2_ref[...] = (hat * vec[5:6, :] + vec[6:7, :]).astype(BF)


def middle_part(info, count, heads, x_own, vec, mine, other):
    rows, model = x_own.shape
    return pl.pallas_call(
        functools.partial(middle_kernel, count),
        in_specs=[SMEM] + [VMEM] * 6 + [ANY] * 2,
        out_specs=[VMEM] * 3,
        out_shape=[
            jax.ShapeDtypeStruct((rows, model), BF),
            jax.ShapeDtypeStruct((rows, model), F32),
            jax.ShapeDtypeStruct((rows, model), BF),
        ],
        scratch_shapes=[
            pltpu.VMEM((model, model), BF),
            pltpu.SemaphoreType.DMA((2,)),
        ],
        compiler_params=params(),
        cost_estimate=estimate(2 * rows * model * model, 4 * 2**20),
        name="middle",
    )(info, *heads, x_own, vec, mine, other)


def feed_kernel(micros, *refs):
    n2, cot = refs[:SEQ], refs[SEQ : 2 * SEQ]
    vec, down_ref, up_ref = refs[2 * SEQ : 2 * SEQ + 3]
    down_chip, down_sib, *ups, grads, sums = refs[2 * SEQ + 3 : 3 * SEQ + 7]
    w_up, w_down, n2_in, c_in, act, gh, weight_sem, n2_sem, c_sem = refs[3 * SEQ + 7 :]
    rows = n2[0].shape[0] // micros
    hidden = w_up.shape[1]
    up_copy = pltpu.make_async_copy(up_ref, w_up, weight_sem.at[0])
    down_copies = [pltpu.make_async_copy(down_ref, w_down, weight_sem.at[1])]
    by_micro = lambda pieces: [p.at[pl.ds(m * rows, rows), :] for m in range(micros) for p in pieces]
    n2_copies = row_copies(by_micro(n2), n2_in, n2_sem)
    c_copies = row_copies(by_micro(cot), c_in, c_sem)
    for copy in n2_copies + [up_copy] + c_copies + down_copies:
        copy.start()
    for copy in n2_copies + [up_copy]:
        copy.wait()
    total = jnp.zeros((1, hidden), F32)
    for micro in range(micros):
        span = slice(micro * SEQ * rows, (micro + 1) * SEQ * rows)
        values = plain_dot(n2_in[span], w_up[...]) + vec[8:9, :]
        normal = 0.5 * (1.0 + lax.erf(values * (2.0**-0.5)))
        slope = normal + values * (jnp.exp(values * values * -0.5) * 0.3989422804014327)
        active = (values * normal).astype(BF)
        act[span] = active
        if micro == 0:
            for copy in c_copies + down_copies:
                copy.wait()
        grad_hidden = (slope * cols_dot(c_in[span], w_down[...])).astype(BF)
        gh[span] = grad_hidden
        total = total + column_sums(grad_hidden.astype(F32))
        place = slice(micro * rows, (micro + 1) * rows)
        down_part = plain_dot(active, w_down[...]).astype(BF)
        up_part = cols_dot(grad_hidden, w_up[...]).astype(BF)
        for k in range(SEQ):
            (down_chip, down_sib)[k // 2][k % 2, place] = down_part[k * rows : (k + 1) * rows]
            ups[k][place] = up_part[k * rows : (k + 1) * rows]
    sums[...] = jnp.zeros(sums.shape, F32)
    sums[8:9, :] = total
    block = grads.shape[2]
    step = max(512 // block, 1)
    for which, (left, right) in enumerate(((act, c_in), (n2_in, gh))):
        for at in range(0, grads.shape[0], step):
            part = rows_dot(left[:, at * block : (at + step) * block], right[...]).astype(BF)
            grads[at : at + step, which] = part.reshape(step, block, part.shape[1])


def feed(fsdp, micros, n2_pieces, c_pieces, vec, w_down, w_up):
    rows, model = c_pieces[0].shape
    hidden = w_down.shape[0]
    pair = jax.ShapeDtypeStruct((2, rows, model), BF)
    group = SEQ * rows
    return pl.pallas_call(
        functools.partial(feed_kernel, micros),
        in_specs=[ANY] * (2 * SEQ) + [VMEM] + [ANY] * 2,
        out_specs=[VMEM] * (SEQ + 4),
        out_shape=[pair] * 2
        + [jax.ShapeDtypeStruct((rows, model), BF)] * SEQ
        + [
            jax.ShapeDtypeStruct((fsdp, 2, model // fsdp, model), BF),
            jax.ShapeDtypeStruct((16, model), F32),
        ],
        scratch_shapes=[
            pltpu.VMEM((model, hidden), BF),
            pltpu.VMEM((hidden, model), BF),
            pltpu.VMEM((group, model), BF),
            pltpu.VMEM((group, model), BF),
            pltpu.VMEM((group, hidden), BF),
            pltpu.VMEM((group, hidden), BF),
            pltpu.SemaphoreType.DMA((2,)),
            pltpu.SemaphoreType.DMA((SEQ * micros,)),
            pltpu.SemaphoreType.DMA((SEQ * micros,)),
        ],
        compiler_params=params(),
        cost_estimate=estimate(12 * group * model * hidden, 24 * 2**20),
        name="feed",
    )(*n2_pieces, *c_pieces, vec, w_down, w_up)


def middle_back_kernel(count, micros, info, *refs):
    chips, cames, fars = refs[:micros], refs[micros : 2 * micros], refs[2 * micros : 3 * micros]
    mid_ref, c_ref, vec, mine, other = refs[3 * micros : 3 * micros + 5]
    gm_ref, gb_ref, g0, g1, g2, g3, sums, weight, scratch, sem = refs[3 * micros + 5 :]
    copies = out_weight_copies(info, count, mine, other, weight, sem)
    for copy in copies:
        copy.start()
    grad_two = jnp.concatenate(
        [a[...].astype(F32) + b[...].astype(F32) + c[...].astype(F32) for a, b, c in zip(chips, cames, fars)],
        axis=0,
    )
    hat, scale = norm_parts(mid_ref[...])
    cot = c_ref[...].astype(F32)
    grad_middle = cot + norm_back(grad_two, hat, scale, vec[5:6, :])
    gm_ref[...] = grad_middle
    branch = grad_middle.astype(BF)
    gb_ref[...] = branch
    sums[...] = jnp.zeros(sums.shape, F32)
    sums[4:5, :] = column_sums(branch.astype(F32))
    sums[5:6, :] = column_sums(grad_two * hat)
    sums[6:7, :] = column_sums(grad_two)
    sums[7:8, :] = column_sums(cot)
    for copy in copies:
        copy.wait()
    scratch[...] = cols_dot(branch, weight[...]).astype(BF)
    width = g0.shape[1]
    for at, ref in enumerate((g0, g1, g2, g3)):
        place = info[count + 2 + at]
        ref[...] = scratch[:, pl.ds(pl.multiple_of(place * width, width), width)]


def middle_back(info, count, parts, middle, c_own, vec, mine, other):
    rows, model = middle.shape
    micros = len(parts)
    piece = jax.ShapeDtypeStruct((rows, model // SEQ), BF)
    return pl.pallas_call(
        functools.partial(middle_back_kernel, count, micros),
        in_specs=[SMEM] + [VMEM] * (3 * micros + 3) + [ANY] * 2,
        out_specs=[VMEM] * 7,
        out_shape=[
            jax.ShapeDtypeStruct((rows, model), F32),
            jax.ShapeDtypeStruct((rows, model), BF),
        ]
        + [piece] * 4
        + [jax.ShapeDtypeStruct((16, model), F32)],
        scratch_shapes=[
            pltpu.VMEM((model, model), BF),
            pltpu.VMEM((rows, model), BF),
            pltpu.SemaphoreType.DMA((2,)),
        ],
        compiler_params=params(),
        cost_estimate=estimate(2 * rows * model * model, 4 * 2**20),
        name="middle_back",
    )(info, *[p for at in range(3) for p in [part[at] for part in parts]], middle, c_own, vec, mine, other)


def attention_back_kernel(count, info, joined_ref, probs_ref, g0, g1, g2, g3, hat_ref, *refs):
    pieces, n1_ref = refs[:count], refs[count]
    more = len(refs) - count - 13
    extra = refs[count + 1 : count + 1 + more]
    keep, send, chip_ref, sib_ref = refs[count + 1 + more : count + 5 + more]
    sums, weight, sem, n1_in, n1_sem, grads, out, out_sem = refs[count + 5 + more :]
    image = pl.program_id(0)
    tokens = joined_ref.shape[2]
    rows = SEQ * tokens
    triple = joined_ref.shape[3]
    width = triple // 3
    model = weight.shape[0]
    copies = piece_copies(info, pieces, 0, weight, sem)
    n1_copy = pltpu.make_async_copy(n1_ref, n1_in, n1_sem)

    @pl.when(pl.program_id(0) == 0)
    def _():
        for copy in copies:
            copy.start()
        n1_copy.start()
        sums[...] = functools.reduce(jnp.add, [ref[...] for ref in extra])

    joined = joined_ref[...].reshape(rows, triple)
    grad = jnp.concatenate([g0[...], g1[...], g2[...], g3[...]], axis=0)
    queries, keys, values = [], [], []
    for head in range(width // HEAD_DIM):
        low = head * HEAD_DIM
        q = joined[:, low : low + HEAD_DIM] * jnp.asarray(SCALE, BF)
        k = joined[:, width + low : width + low + HEAD_DIM] * jnp.asarray(SCALE, BF)
        v = joined[:, 2 * width + low : 2 * width + low + HEAD_DIM]
        ga = grad[:, low : low + HEAD_DIM]
        probs = probs_ref[0, head]
        values.append(plain_dot(probs, ga).astype(BF))
        wide = probs.astype(F32)
        weighted = wide * cols_dot(v, ga)
        centre = jnp.sum(weighted, axis=0, keepdims=True)
        grad_scores = (weighted - wide * centre).astype(BF)
        keys.append(plain_dot(grad_scores, q).astype(BF))
        queries.append(rows_dot(k, grad_scores))
    grad_joined = jnp.concatenate(
        [jnp.concatenate(queries, axis=0).T.astype(BF)] + keys + values, axis=1
    )
    grads[:, image] = grad_joined.reshape(SEQ, tokens, triple)
    wide = grad_joined.astype(F32)
    place = pl.multiple_of(info[count] * width, width)
    sums[2:3, pl.ds(place, width)] += column_sums(wide[:, :width])
    sums[3:4, pl.ds(place, width)] += column_sums(wide[:, 2 * width :])

    @pl.when(pl.program_id(0) == 0)
    def _():
        for copy in copies:
            copy.wait()

    partial = cols_dot(grad_joined, weight[...])
    hat = hat_ref[...].reshape(rows, model).astype(F32)
    sums[0:1, :] += column_sums(partial * hat)
    sums[1:2, :] += column_sums(partial)
    low = partial.astype(BF)
    half = rows // 2
    chip_ref[...] = low[:half].reshape(chip_ref.shape)
    sib_ref[...] = low[half:].reshape(sib_ref.shape)

    @pl.when(image == pl.num_programs(0) - 1)
    def _():
        n1_copy.wait()
        right = grads[...].reshape(n1_in.shape[0], triple)
        total = jnp.concatenate([sums[...], jnp.zeros((LANES - sums.shape[0], model), F32)], axis=0)
        out[:, triple:] = total.T.astype(BF)
        tile = min(512, model)
        for at in range(0, model, tile):
            out[at : at + tile, :triple] = rows_dot(n1_in[:, at : at + tile], right).astype(BF)
        moves = digit_moves(info, out, keep, send, out_sem)
        for move in moves:
            move.start()
        for move in moves:
            move.wait()


def attention_back(info, joined, probs, grads, hat, pieces, n1, extra):
    count = len(pieces)
    _, images, tokens, triple = joined.shape
    model = hat.shape[3]
    width = triple // 3
    rows = SEQ * tokens
    heads = width // HEAD_DIM
    pair = jax.ShapeDtypeStruct((2, images, tokens, model), BF)
    group_block = lambda n, cols: pl.BlockSpec((n, 1, tokens, cols), lambda i: (0, i, 0, 0))
    part = jax.ShapeDtypeStruct((count // 2, model // count, triple + LANES), BF)
    return pl.pallas_call(
        functools.partial(attention_back_kernel, count),
        grid=(images,),
        in_specs=[
            SMEM,
            group_block(SEQ, triple),
            pl.BlockSpec((1, heads, rows, rows), lambda i: (i, 0, 0, 0)),
        ]
        + [pl.BlockSpec((tokens, width), lambda i: (i, 0))] * SEQ
        + [group_block(SEQ, model)]
        + [ANY] * (count + 1)
        + [pl.BlockSpec((16, model), lambda i: (0, 0))] * len(extra),
        out_specs=[ANY, ANY, group_block(2, model), group_block(2, model)],
        out_shape=[part, part, pair, pair],
        scratch_shapes=[
            pltpu.VMEM((16, model), F32),
            pltpu.VMEM((model, triple), BF),
            pltpu.SemaphoreType.DMA((count,)),
            pltpu.VMEM((images * rows, model), BF),
            pltpu.SemaphoreType.DMA,
            pltpu.VMEM((SEQ, images, tokens, triple), BF),
            pltpu.VMEM((model, triple + LANES), BF),
            pltpu.SemaphoreType.DMA((count,)),
        ],
        compiler_params=params(),
        cost_estimate=estimate(
            2 * images * rows * (2 * model * triple + 8 * width * rows), 12 * 2**20
        ),
        name="attention_back",
    )(info, joined, probs, *grads, hat, *pieces, n1, *extra)


def on_device(
    fsdp,
    inputs,
    keep_mask,
    cotangent,
    first_gain,
    first_shift,
    qkv_weight,
    query_bias,
    value_bias,
    out_weight,
    out_bias,
    second_gain,
    second_shift,
    up_weight,
    up_bias,
    down_weight,
    down_bias,
):
    micros, images, tokens, model = inputs.shape
    rows = images * tokens
    at_f, at_s = lax.axis_index("fsdp"), lax.axis_index("seq")
    depth = qkv_weight.shape[0]
    block = SEQ * depth
    width = model // SEQ
    triple = 3 * width
    half = model // 2
    unit_block = up_bias.shape[0]
    units = fsdp * unit_block
    core = at_s & 1
    micro_range = range(micros)
    info = jnp.stack(
        [jnp.asarray(v, jnp.int32) for v in fsdp_owners(fsdp, at_f)]
        + [at_s, core]
        + [at_s ^ mask for mask in ORDER]
    )

    vectors = jnp.stack(
        [
            first_gain,
            first_shift,
            query_bias,
            value_bias,
            out_bias,
            second_gain,
            second_shift,
            down_bias,
        ],
        axis=1,
    )
    vectors = jnp.pad(vectors, ((0, 0), (0, LANES - VECTORS)))
    to_send = pack(fsdp, qkv_weight, out_weight, vectors, up_weight)
    arrived = lax.all_to_all(to_send, "seq", 0, 0, tiled=True).reshape(block, -1)
    early = triple + LANES
    bias_column = jnp.pad(up_bias[:, None], ((0, 0), (VECTORS, LANES - VECTORS - 1)))
    first_group = jnp.concatenate(
        [
            arrived[:, :triple],
            arrived[:, triple:early] + bias_column,
            arrived[:, early : early + half],
        ],
        axis=1,
    )
    x_pieces = seq_gather(inputs.reshape(micros * rows, model))
    first_pieces = fsdp_gather(first_group, fsdp)
    w_down = lax.all_gather(down_weight, "fsdp", tiled=True)
    w_up = lax.all_gather(arrived[:, early + half :], "fsdp", tiled=True)

    x_own = inputs.reshape(micros * rows, model)
    c_own = cotangent.reshape(micros * rows, model)
    keep = keep_mask.reshape(micros * images, SEQ, tokens)
    keep = jnp.stack(
        [lax.dynamic_index_in_dim(keep, at_s ^ mask, 1, keepdims=False) for mask in ORDER], axis=1
    )
    n1, hat_one, joined, *heads_out, probs, vec = attention(
        info,
        [x.reshape(micros * images, tokens, model) for x in x_pieces],
        keep.reshape(micros * images, 1, SEQ * tokens).astype(F32),
        first_pieces,
        triple,
    )
    c_pieces = seq_gather(after(c_own, x_pieces[1]))
    heads_out[1:] = [after(h, c_pieces[1]) for h in heads_out[1:]]
    heads_in = seq_exchange(heads_out)
    out_mine = placed(info, first_pieces, early, half)
    out_other = hop(out_mine, 1)
    attended, middle, normed = middle_part(
        info, fsdp, heads_in, x_own, vec, out_mine, out_other
    )
    n2_pieces = seq_gather(normed)

    group_rows = micros * SEQ * rows
    down_chip, down_sib, *ups, feed_grad, part = feed(
        fsdp, micros, n2_pieces, c_pieces, vec, w_down, w_up
    )
    sums = [part]
    down_grad, up_grad = lax.psum_scatter(feed_grad, "fsdp", scatter_dimension=0, tiled=False)
    down_grad = down_grad.astype(F32)
    up_far = (ups[1].astype(F32) + hop(ups[3], 1).astype(F32)).astype(BF)
    two_parts = [(ups[0], hop(ups[2], 1), hop(up_far, 2))]
    down_parts = [(down_chip, down_sib)]

    grad_middle, branch, *grads_out, part = middle_back(
        info, fsdp, two_parts, middle, c_own, vec, out_mine, out_other
    )
    sums.append(part)
    grads_in = seq_exchange(grads_out)
    out_here, out_there = core_grad(info, fsdp, attended, branch)
    down_sums = []
    for chip, sib in down_parts:
        came, far = seq_scatter(chip, after(sib, branch))
        down_sums.append((chip[0], came[0], far))
    out_sib = hop(out_there, 1)
    out_send = (out_here[1].astype(F32) + out_sib[1].astype(F32)).astype(BF)
    grads_in[0] = after(grads_in[0], *[far for _, _, far in down_sums], out_send)

    *qkv_blocks, chip, sib = attention_back(
        info,
        joined,
        probs,
        grads_in,
        hat_one,
        first_pieces,
        n1.reshape(group_rows, model),
        sums,
    )
    out_came = shift(out_send, fsdp, *digits_of(fsdp)[0], 1)
    sib, qkv_blocks[1] = after(sib, out_came), after(qkv_blocks[1], out_came)
    out_parts = scatter_far(scatter_near([out_here[0], out_sib[0], out_came], fsdp, at_f), fsdp, at_f)
    chip = chip.reshape(2, micros * rows, model)
    came, far = seq_scatter(chip, sib.reshape(2, micros * rows, model))
    grad_one = chip[0].astype(F32) + came[0].astype(F32) + hop(after(far, *out_parts[1:]), 2).astype(F32)

    [(a, b, c)] = down_sums
    total = a.astype(F32) + b.astype(F32) + hop(c, 2).astype(F32)
    layer_out = (middle + total + vec[7:8]).astype(BF).reshape(micros, images, tokens, model)
    hat, scale = norm_parts(x_own.astype(F32))
    input_grad = grad_middle + norm_back(grad_one, hat, scale, vec[0:1])
    input_grad = input_grad.astype(BF).reshape(micros, images, tokens, model)

    qkv_came = shift(qkv_blocks[1], fsdp, *digits_of(fsdp)[0], 1)
    qkv_parts = scatter_far(scatter_near([qkv_blocks[0], qkv_came], fsdp, at_f), fsdp, at_f)

    over_seq = lambda part: lax.all_to_all(part.reshape(SEQ, depth, -1), "seq", 0, 0, tiled=True)
    up_weight_grad = unpack_up(over_seq(up_grad))
    qkv_parts[0] = after(qkv_parts[0], up_weight_grad)
    last, own_vectors = collect(qkv_parts, out_parts)
    up_bias_grad = own_vectors[:, VECTORS]
    qkv_weight_grad, out_weight_grad, vector_grads = unpack(over_seq(last), model)
    vector_grads = vector_grads[:, :VECTORS].T

    return (
        layer_out,
        input_grad,
        vector_grads[0],
        vector_grads[1],
        qkv_weight_grad,
        vector_grads[2],
        vector_grads[3],
        out_weight_grad,
        vector_grads[4],
        vector_grads[5],
        vector_grads[6],
        up_weight_grad,
        up_bias_grad,
        down_grad,
        vector_grads[7],
    )


def solution(mesh):
    shard = P(BOTH)
    tokens = P(None, "fsdp", "seq", None)
    in_specs = (tokens, P(None, "fsdp", None), tokens) + (shard,) * 13
    out_specs = (tokens, tokens) + (shard,) * 13
    return jax.shard_map(
        functools.partial(on_device, mesh.shape["fsdp"]),
        mesh=mesh,
        in_specs=in_specs,
        out_specs=out_specs,
        check_vma=False,
    )
```
